32 devices in a mesh: group: 2 (over x), det: 16 (over z, y, core).
Axes of the slice: x: 2, y: 2, z: 4, core: 2. Of those that a mesh axis runs over, the one named last changes fastest.
Arguments:
- science: float32 [2048, 4096], P(('group', 'det')), parts along dimension 0, may hold values from -6 to 6
- variance: float32 [2048, 4096], P(('group', 'det')), parts along dimension 0, may hold values from 0.5 to 18
- template_blocks: float32 [256, 2, 64, 256], P(('group', 'det')), parts along dimension 0, may hold values from -5 to 10.8, as said below
- requests: int32 [32, 16], P('group'), parts along dimension 0, may hold values from 0 to 127, as said below
- stamp_rows: int32 [32, 16], P(('group', 'det')), parts along dimension 0, may hold values from 26 to 38, as said below
- stamp_cols: int32 [32, 16], P(('group', 'det')), parts along dimension 0, may hold values from 26 to 4070, as said below
Outputs:
- decorrelated: float32 [2048, 4096], P(('group', 'det')), parts along dimension 0
- decorrelated_variance: float32 [2048, 4096], P(('group', 'det')), parts along dimension 0
The draws below stay inside these ranges and needn't reach their ends.
There are 2 independent parts, one for each index of `group`. The reference program is written for one: setup_inputs(seed, part) draws one part's arguments, and reference() takes and returns one part's arrays. A program takes and returns all parts, laid end to end along the dimension named above; each array names one. Nothing has to cross between parts.
Inputs may be any that keep to these rules, and one draw needn't show every extreme that they name: `requests`: entries name template blocks as owner * 8 + block. The entries of a row that name one owner stand next to each other, 2 of them at most; one owner, drawn afresh, is named exactly 2 times in every row. `stamp_rows`: every row holds both ends of the range. `stamp_cols`: every row holds both ends of the range. `template_blocks`: plane 1 is positive.
All inputs are finite; a program needn't handle non-finite values.
Results may differ from the reference program's by a relative error of at most 0.0003.
Values sent between devices are 32-bit elements; how exact they have to be, the bound alone decides.
No kernel may reach another device: no remote copies, remote signals or barrier semaphores. Data moves between devices by JAX's collectives and lax.ppermute only.
A program may use at most 256 MiB of HBM per device.

```python
import math
import jax
import jax.numpy as jnp
import numpy as np
from jax import lax

W = 4096
ROWS = 64
CPER = 4
STAMPS = 16
SS = 32
KS = 21
NBASIS = 27
PD = 32
BC = 256
PATCH_DEV = 8
STRIPS = 16
CCDS = 4
ROWS_ALL = 1024
TBLOCKS = 128


def draw_requests(key, part):
    key = jax.random.fold_in(key, 11)
    subkeys = jax.random.split(key, 5)
    needed = W // BC
    hottest = jax.random.randint(subkeys[0], (), 0, STRIPS)
    lengths = jax.random.randint(subkeys[1], (STRIPS, needed), 1, 3)
    lengths = lengths.at[:, 0].set(2)
    run_ends = jnp.cumsum(lengths, axis=1)
    slot_index = jnp.arange(needed)
    run_index = jnp.sum((run_ends[:, :, None] <= slot_index[None, None, :]).astype(jnp.int32), axis=1)
    favour = jax.random.randint(subkeys[2], (STRIPS,), 0, 4) * 300
    scores = jax.random.randint(subkeys[3], (STRIPS, STRIPS), 0, 1000) + favour[None, :]
    owner_grid = jnp.arange(STRIPS)
    scores = jnp.where(owner_grid[None, :] == hottest, -1, scores)
    distinct = scores * STRIPS + owner_grid[None, :]
    ranked = lax.top_k(distinct, needed)[1]
    others = jnp.take_along_axis(ranked, jnp.maximum(run_index - 1, 0), axis=1)
    owners_of = jnp.where(run_index == 0, hottest, others)
    within = jax.random.randint(subkeys[4], (STRIPS, needed), 0, PATCH_DEV)
    return (owners_of * PATCH_DEV + within).astype(jnp.int32)


def centre_draw(key, lowest, highest):
    subkeys = jax.random.split(key, 3)
    values_out = jax.random.randint(subkeys[0], (STRIPS, STAMPS), lowest, highest + 1)
    first_end = jax.random.randint(subkeys[1], (STRIPS, 1), 0, STAMPS)
    second_end = (first_end + 1 + jax.random.randint(subkeys[2], (STRIPS, 1), 0, STAMPS - 1)) % STAMPS
    column = jnp.arange(STAMPS)[None, :]
    values_out = jnp.where(column == first_end, lowest, values_out)
    values_out = jnp.where(column == second_end, highest, values_out)
    return values_out.astype(jnp.int32)


def draw_stamp_rows(key, part):
    key = jax.random.fold_in(key, 12)
    return centre_draw(key, SS // 2 + KS // 2, ROWS - SS // 2 - KS // 2)


def draw_stamp_cols(key, part):
    key = jax.random.fold_in(key, 13)
    return centre_draw(key, SS // 2 + KS // 2, W - SS // 2 - KS // 2)


def noise_levels(key, exponent):
    ccd_rows = ROWS * CPER
    row_number = jnp.arange(ROWS_ALL)
    inside = (row_number % ccd_rows).astype(jnp.float32) / (ccd_rows - 1)
    detector = (row_number // ccd_rows).astype(jnp.float32) / max(CCDS - 1, 1)
    gradient = jnp.exp(math.log(2.0) * inside + math.log(1.5) * detector)
    roughness = jnp.exp(jax.random.uniform(key, (ROWS_ALL, W), jnp.float32, math.log(0.5), math.log(2.0)))
    return gradient[:, None] ** exponent * roughness


def draw_variance(key, part):
    key = jax.random.fold_in(key, 14)
    return noise_levels(key, 1.0)


def draw_template_blocks(key, part):
    key = jax.random.fold_in(key, 15)
    subkeys = jax.random.split(key, 2)
    sky_values = jax.random.truncated_normal(subkeys[0], -5.0, 5.0, (TBLOCKS, ROWS, BC), jnp.float32)
    block_order = jnp.arange(TBLOCKS).astype(jnp.float32) / max(TBLOCKS - 1, 1)
    spreads = jnp.exp(jax.random.uniform(subkeys[1], (TBLOCKS, ROWS, BC), jnp.float32, math.log(0.3), math.log(1.2)))
    noise_level = spreads * jnp.exp(math.log(3.0) * block_order)[:, None, None]
    return jnp.stack([sky_values, noise_level], axis=1)


def shard_levels(stream_key, shape, cuts, low, largest):
    level, own = 1.0, jax.random.fold_in(stream_key, 6)
    for position, parts in cuts:
        steps = jnp.exp(jax.random.uniform(jax.random.fold_in(own, position), (parts,), jnp.float32, low / len(cuts), largest / len(cuts)))
        level = level * jnp.repeat(steps, shape[position] // parts).reshape([-1 if axis == position else 1 for axis in range(len(shape))])
    return level


def bell_draw(stream_key, shape, scale, reach, cuts=(), held_as=jnp.bfloat16):
    entries = jax.random.normal(stream_key, shape, jnp.float32) * scale
    if len(cuts) > 0:
        entries = shard_levels(stream_key, shape, cuts, -0.22, 0.18) * entries
    return jnp.clip(entries, min=-reach, max=reach).astype(held_as)


def setup_inputs(seed: int = 0, part: int = 0) -> dict:
    key_list = jax.random.split(jax.random.key(seed), 7)
    part_splits = jax.random.split(jax.random.fold_in(key_list[6], part), 7)
    return {
        "science": bell_draw(part_splits[0], (ROWS_ALL, W), 1.5, 6.0, ((0, 16),), jnp.float32),
        "variance": draw_variance(jax.random.fold_in(jax.random.fold_in(key_list[6], part), 71), part),
        "template_blocks": draw_template_blocks(jax.random.fold_in(jax.random.fold_in(key_list[6], part), 71), part),
        "requests": draw_requests(jax.random.fold_in(jax.random.fold_in(key_list[6], part), 71), part),
        "stamp_rows": draw_stamp_rows(jax.random.fold_in(jax.random.fold_in(key_list[6], part), 71), part),
        "stamp_cols": draw_stamp_cols(jax.random.fold_in(jax.random.fold_in(key_list[6], part), 71), part),
    }


HIGHEST = lax.Precision.HIGHEST
GAUSS_WIDTHS = (0.7, 1.5, 3.0)
GAUSS_DEGREES = (4, 2, 2)

def line_functions(kernel_taps):
    centre = kernel_taps // 2
    tap_grid = jnp.arange(kernel_taps).astype(jnp.float32) - centre
    raw_list = []
    for spread, degree in zip(GAUSS_WIDTHS, GAUSS_DEGREES):
        gaussian = jnp.exp(-tap_grid * tap_grid / (2.0 * spread * spread))
        for degree_power in range(degree + 1):
            raw_list.append(gaussian * tap_grid ** degree_power)
    result = []
    for vector in raw_list:
        for earlier in result:
            vector = vector - jnp.sum(vector * earlier) * earlier
        result.append(vector / jnp.sqrt(jnp.sum(vector * vector)))
    return jnp.stack(result)

def pair_tables():
    first_index = []
    second_index = []
    offset_base = 0
    for degree in GAUSS_DEGREES:
        for outer in range(degree + 1):
            for inner in range(degree + 1 - outer):
                first_index.append(offset_base + outer)
                second_index.append(offset_base + inner)
        offset_base += degree + 1
    return (np.array(first_index), np.array(second_index))

def dft_tables(length):
    positions = jnp.arange(length)
    phase_steps = positions[:, None] * positions[None, :] % length
    angles = 2.0 * math.pi / length * phase_steps.astype(jnp.float32)
    return (jnp.cos(angles), jnp.sin(angles))

def sandwich(left_matrix, values_in, right_matrix):
    return jnp.einsum('ij,...jk,kl->...il', left_matrix, values_in, right_matrix, precision=HIGHEST)

def spectrum(values_in, cosine, sine):
    real_part = sandwich(cosine, values_in, cosine) - sandwich(sine, values_in, sine)
    imag_part = -(sandwich(sine, values_in, cosine) + sandwich(cosine, values_in, sine))
    return (real_part, imag_part)

def cut_squares(source, row_starts, col_starts, extent):

    def one_square(row_start, col_start):
        return lax.dynamic_slice(source, (row_start, col_start), (extent, extent))
    return jax.vmap(one_square)(row_starts, col_starts)

def stamp_system(science_strip, weight_plane, template_strip, centre_rows, centre_cols, line_basis):
    kernel_taps = line_basis.shape[1]
    margin = kernel_taps // 2
    functions = line_basis.shape[0]
    stamp_side = SS
    half_side = stamp_side // 2
    stamps_here = centre_rows.shape[0]
    row_starts = (centre_rows - half_side).astype(jnp.int32)
    col_starts = (centre_cols - half_side).astype(jnp.int32)
    science_stamp = cut_squares(science_strip, row_starts, col_starts, stamp_side)
    weight_stamp = cut_squares(weight_plane, row_starts, col_starts, stamp_side)
    extent = stamp_side + 2 * margin
    window = cut_squares(template_strip, row_starts - margin, col_starts - margin, extent)
    template_stamp = window[:, margin:margin + stamp_side, margin:margin + stamp_side]
    cosine, sine = dft_tables(stamp_side)
    science_re, science_im = spectrum(science_stamp, cosine, sine)
    template_re, template_im = spectrum(template_stamp, cosine, sine)
    cross_re = science_re * template_re + science_im * template_im
    cross_im = science_im * template_re - science_re * template_im
    magnitude = jnp.sqrt(cross_re * cross_re + cross_im * cross_im)
    floor_level = 0.25 * (lax.optimization_barrier(jnp.mean(magnitude, axis=(1, 2), keepdims=True)) + 1e-06)
    scaling = 1.0 / jnp.maximum(magnitude, floor_level)
    unit_re = cross_re * scaling
    unit_im = cross_im * scaling
    surface = (sandwich(cosine, unit_re, cosine) - sandwich(sine, unit_re, sine) - sandwich(cosine, unit_im, sine) - sandwich(sine, unit_im, cosine)) / (stamp_side * stamp_side)
    quality = lax.optimization_barrier(jnp.max(surface, axis=(1, 2)))
    stamp_weight = jnp.maximum(quality, 0.1)
    offsets = jnp.arange(extent)[None, :] - jnp.arange(stamp_side)[:, None]
    selector = (offsets[None] == jnp.arange(kernel_taps)[:, None, None]).astype(jnp.float32)
    vertical = jnp.einsum('au,urp->arp', line_basis, selector, precision=HIGHEST).reshape(functions * stamp_side, extent)
    across = jnp.einsum('spq,mq->spm', window, vertical, precision=HIGHEST)
    both_ways = jnp.einsum('kp,spm->skm', vertical, across, precision=HIGHEST)
    stacked = both_ways.reshape(stamps_here, functions, stamp_side, functions, stamp_side).transpose(1, 3, 0, 2, 4)
    first_index, second_index = pair_tables()
    images = stacked[first_index, second_index].reshape(len(first_index), stamps_here, stamp_side * stamp_side)
    target = (science_stamp - template_stamp).reshape(stamps_here, stamp_side * stamp_side)
    pixel_weight = stamp_weight[:, None] / weight_stamp.reshape(stamps_here, stamp_side * stamp_side)
    weighted = images * pixel_weight[None]
    normal = jnp.einsum('bsp,csp->bc', weighted, images, precision=HIGHEST)
    right_side = jnp.einsum('bsp,sp->b', weighted, target, precision=HIGHEST)
    return (normal, right_side)

def solve_system(normal, right_side):
    factor_lower = jnp.linalg.cholesky(normal)
    middle = lax.linalg.triangular_solve(factor_lower, right_side[:, None], left_side=True, lower=True)
    answer = lax.linalg.triangular_solve(factor_lower, middle, left_side=True, lower=True, transpose_a=True)
    return answer[:, 0]

def kernel_from(coefficients, line_basis):
    first_index, second_index = pair_tables()
    kernel_taps = line_basis.shape[1]
    margin = kernel_taps // 2
    spread_part = jnp.einsum('b,bu,bv->uv', coefficients, line_basis[first_index], line_basis[second_index], precision=HIGHEST)
    positions = jnp.arange(kernel_taps)
    impulse = ((positions[:, None] == margin) & (positions[None, :] == margin)).astype(jnp.float32)
    return spread_part + impulse

def decorrelation(kernel, mean_science, mean_template):
    kernel_taps = kernel.shape[0]
    margin = kernel_taps // 2
    placing = ((jnp.arange(kernel_taps)[None, :] - margin) % PD == jnp.arange(PD)[:, None]).astype(jnp.float32)
    placed = jnp.dot(jnp.dot(placing, kernel, precision=HIGHEST), placing.T, precision=HIGHEST)
    cosine, sine = dft_tables(PD)
    kernel_re, kernel_im = spectrum(placed, cosine, sine)
    response = jnp.sqrt((mean_science + mean_template) / (mean_science + mean_template * (kernel_re * kernel_re + kernel_im * kernel_im)))
    spatial = (sandwich(cosine, response, cosine) - sandwich(sine, response, sine)) / (PD * PD)
    return jnp.dot(jnp.dot(placing.T, spatial, precision=HIGHEST), placing, precision=HIGHEST)

def slab_correlate(full_plane, kernels):
    detectors = kernels.shape[0]
    margin = kernels.shape[1] // 2
    ccd_rows = full_plane.shape[0] // detectors
    padded = jnp.pad(full_plane, ((margin, margin), (0, 0)))
    starts = (jnp.arange(detectors) * ccd_rows).astype(jnp.int32)

    def one_slab(start_row):
        return lax.dynamic_slice_in_dim(padded, start_row, ccd_rows + 2 * margin, 0)
    slabs = jax.vmap(one_slab)(starts)
    result = lax.conv_general_dilated(slabs[None], kernels[:, None], (1, 1), ((0, 0), (margin, margin)), dimension_numbers=('NCHW', 'OIHW', 'NCHW'), feature_group_count=detectors, precision=HIGHEST)
    return result[0].reshape(full_plane.shape)

def reference(science, variance, template_blocks, requests, stamp_rows, stamp_cols):
    line_basis = line_functions(KS)
    strips = requests.shape[0]
    blocks = template_blocks[requests]
    strip_planes = blocks.transpose(0, 2, 3, 1, 4).reshape(strips, 2, ROWS, W)
    template_image = strip_planes[:, 0]
    template_variance = strip_planes[:, 1]
    science_strips = science.reshape(strips, ROWS, W)
    variance_strips = variance.reshape(strips, ROWS, W)

    def per_strip(inputs):
        science_strip, variance_strip, template_strip, tvar_strip, centre_rows, centre_cols = inputs
        return stamp_system(science_strip, variance_strip + tvar_strip, template_strip, centre_rows, centre_cols, line_basis)
    normal, right_side = lax.map(per_strip, (science_strips, variance_strips, template_image, template_variance, stamp_rows, stamp_cols))
    detectors = strips // CPER
    normal = lax.optimization_barrier(jnp.sum(normal.reshape(detectors, CPER, NBASIS, NBASIS), axis=1))
    right_side = lax.optimization_barrier(jnp.sum(right_side.reshape(detectors, CPER, NBASIS), axis=1))
    pixels = CPER * ROWS * W
    mean_science = lax.optimization_barrier(jnp.sum(variance_strips.reshape(detectors, -1), axis=1)) / pixels
    mean_template = lax.optimization_barrier(jnp.sum(template_variance.reshape(detectors, -1), axis=1)) / pixels
    coefficients = jax.vmap(solve_system)(normal, right_side)

    def make_kernel(coefficient_row):
        return kernel_from(coefficient_row, line_basis)
    kernels = jax.vmap(make_kernel)(coefficients)
    filters = jax.vmap(decorrelation)(kernels, mean_science, mean_template)
    ccd_rows = CPER * ROWS
    tvar_ccd = template_variance.reshape(detectors, ccd_rows, W)
    variance_ccd = variance.reshape(detectors, ccd_rows, W)
    difference = science - slab_correlate(template_image.reshape(ROWS_ALL, W), kernels)
    decorrelated = slab_correlate(difference, filters)
    kernel_power = lax.optimization_barrier(jnp.sum(kernels * kernels, axis=(1, 2)))
    filter_power = lax.optimization_barrier(jnp.sum(filters * filters, axis=(1, 2)))
    decorrelated_variance = filter_power[:, None, None] * (variance_ccd + tvar_ccd * kernel_power[:, None, None])
    return (decorrelated, decorrelated_variance.reshape(ROWS_ALL, W))
```

```python
import functools

import jax
import jax.numpy as jnp
import numpy as np
from jax import lax
from jax.experimental import pallas as pl
from jax.experimental.pallas import tpu as pltpu
from jax.sharding import PartitionSpec as P

CPER = 4
SS = 32
KS = 21
PD = 32
MARGIN = KS // 2
HALO = 16
EXTENT = SS + 2 * MARGIN

HIGHEST = lax.Precision.HIGHEST
GAUSS_WIDTHS = (0.7, 1.5, 3.0)
GAUSS_DEGREES = (4, 2, 2)
VMEM_LIMIT = 60 * 1024 * 1024
VMEM = pltpu.MemorySpace.VMEM
SMEM = pltpu.MemorySpace.SMEM


def line_functions():
    tap_grid = np.arange(KS, dtype=np.float64) - MARGIN
    raw_list = []
    for spread, degree in zip(GAUSS_WIDTHS, GAUSS_DEGREES):
        gaussian = np.exp(-tap_grid * tap_grid / (2.0 * spread * spread))
        for degree_power in range(degree + 1):
            raw_list.append(gaussian * tap_grid**degree_power)
    result = []
    for vector in raw_list:
        for earlier in result:
            vector = vector - np.sum(vector * earlier) * earlier
        result.append(vector / np.sqrt(np.sum(vector * vector)))
    return np.stack(result)


def images_by_across():
    groups = []
    base = 0
    for degree in GAUSS_DEGREES:
        for inner in range(degree + 1):
            groups.append((base + inner, [base + outer for outer in range(degree + 1 - inner)]))
        base += degree + 1
    return groups


LINE = line_functions()
GROUPS = images_by_across()
PAIRS = [(a, b) for b, downs in GROUPS for a in downs]
NB = len(PAIRS)
NFUN = LINE.shape[0]
WROWS = 56


def block_diag(matrix, times):
    rows, cols = matrix.shape
    out = np.zeros((rows * times, cols * times))
    for k in range(times):
        out[k * rows : (k + 1) * rows, k * cols : (k + 1) * cols] = matrix
    return out


def across_table():
    table = np.zeros((256, NFUN * 128))
    for b in range(NFUN):
        for k in range(4):
            for c in range(SS):
                table[64 * k + c : 64 * k + c + KS, b * 128 + 32 * k + c] = LINE[b]
    return table.astype(np.float32)


def down_table():
    table = np.zeros((NB * SS, WROWS))
    for image, (a, _) in enumerate(PAIRS):
        for r in range(SS):
            table[image * SS + r, r : r + KS] = LINE[a]
    return table.astype(np.float32)


def dft_blocks():
    grid = np.outer(np.arange(SS), np.arange(SS)) % SS
    c, s = np.cos(2 * np.pi * grid / SS), np.sin(2 * np.pi * grid / SS)
    c, s = block_diag(c, 4), block_diag(s, 4)
    ones = block_diag(np.ones((SS, SS)), 4)
    left = np.concatenate([c, s], 0)
    right = np.block([[c, -s], [-s, -c]])
    back_left = np.block([[c, -s], [s, c]])
    back_right = np.concatenate([c, -s], 0) / (SS * SS)
    return [x.astype(np.float32) for x in (left, right, back_left, back_right, ones)]


def basis_tables():
    lv, lu = np.zeros((32, 32)), np.zeros((32, 128))
    for image, (a, b) in enumerate(PAIRS):
        lv[:KS, image] = LINE[b]
        lu[image, :KS] = LINE[a]
    return lv.astype(np.float32), lu.astype(np.float32)


def filter_tables():
    grid = np.outer(np.arange(PD), np.arange(KS) - MARGIN)
    c, s = np.zeros((PD, 32)), np.zeros((PD, 32))
    c[:, :KS], s[:, :KS] = np.cos(2 * np.pi * grid / PD), np.sin(2 * np.pi * grid / PD)
    cr, sr = np.zeros((128, 128)), np.zeros((128, 128))
    cr[:32, :PD], sr[:32, :PD] = c.T, s.T
    left = np.concatenate([c, s], 0)
    right = np.block([[cr, -sr], [-sr, -cr]])
    back_left = np.concatenate([c.T, s.T], 0) / (PD * PD)
    back_c, back_s = np.zeros((128, 128)), np.zeros((128, 128))
    back_c[:PD, :32], back_s[:PD, :32] = c, s
    back_right = np.concatenate([back_c, -back_s], 0)
    return [x.astype(np.float32) for x in (left, right, back_left, back_right)]


def pick_kernel(picks, source, out, sem):
    count = out.shape[0]

    def copy(k):
        return pltpu.make_async_copy(source.at[picks[k]], out.at[k], sem.at[k])

    def start(k, carry):
        copy(k).start()
        return carry

    def finish(k, carry):
        copy(k).wait()
        return carry

    lax.fori_loop(0, count, start, 0)
    lax.fori_loop(0, count, finish, 0)


def pick(picks, source):
    count = picks.shape[0]
    return pl.pallas_call(
        pick_kernel,
        out_shape=jax.ShapeDtypeStruct((count,) + source.shape[1:], source.dtype),
        in_specs=[pl.BlockSpec(memory_space=SMEM), pl.BlockSpec(memory_space=VMEM)],
        out_specs=pl.BlockSpec(memory_space=pl.ANY),
        scratch_shapes=[pltpu.SemaphoreType.DMA((count,))],
        compiler_params=pltpu.CompilerParams(vmem_limit_bytes=VMEM_LIMIT),
        name="pick_blocks",
    )(picks, source)


def lay_kernel(needed, width, slots, received, image, variance, sem):
    def copies(j):
        k = slots[j]
        columns = pl.ds(j * width, width)
        return [
            pltpu.make_async_copy(received.at[k, 0], image.at[:, columns], sem.at[0, j]),
            pltpu.make_async_copy(received.at[k, 1], variance.at[:, columns], sem.at[1, j]),
        ]

    for j in range(needed):
        for copy in copies(j):
            copy.start()
    for j in range(needed):
        for copy in copies(j):
            copy.wait()


def lay_strip(slots, received):
    needed = slots.shape[0]
    _, _, rows, width = received.shape
    shape = jax.ShapeDtypeStruct((rows, needed * width), received.dtype)
    return pl.pallas_call(
        functools.partial(lay_kernel, needed, width),
        out_shape=[shape, shape],
        in_specs=[pl.BlockSpec(memory_space=SMEM), pl.BlockSpec(memory_space=pl.ANY)],
        out_specs=[pl.BlockSpec(memory_space=VMEM)] * 2,
        scratch_shapes=[pltpu.SemaphoreType.DMA((2, needed))],
        compiler_params=pltpu.CompilerParams(vmem_limit_bytes=VMEM_LIMIT),
        name="lay_strip",
    )(slots, received)


def dot(a, b, contract=((1,), (0,))):
    return lax.dot_general(
        a, b, (contract, ((), ())), precision=HIGHEST, preferred_element_type=jnp.float32
    )


def split(x):
    high = x.astype(jnp.bfloat16)
    return high, (x - high.astype(jnp.float32)).astype(jnp.bfloat16)


def stamp_kernel(
    stamp_rows,
    stamp_cols,
    science,
    variance,
    template,
    template_variance,
    across_ref,
    down_ref,
    left_ref,
    right_ref,
    back_left_ref,
    back_right_ref,
    ones_ref,
    out,
    images,
    flat_x,
    flat_y,
):
    height, columns = science.shape
    stamps = stamp_rows.shape[0]
    groups = stamps // 4
    lane = lax.broadcasted_iota(jnp.int32, (1, 256), 1)

    windows, sciences, templates, weights = [], [], [], []
    for g in range(groups):
        window = sci = tmp = wgt = None
        for k in range(4):
            row = stamp_rows[g * 4 + k] - (SS // 2 + MARGIN)
            col = stamp_cols[g * 4 + k] - (SS // 2 + MARGIN)
            base = jnp.minimum(col // 128 * 128, columns - 256)
            base = pl.multiple_of(base, 128)
            off = col - base
            cols = pl.ds(base, 256)
            t = template[:, cols]
            s = science[:, cols]
            w = variance[:, cols] + template_variance[:, cols]
            up = lax.rem(height - row, height)
            up_in = height - row - MARGIN
            to64 = lax.rem(64 * k - off + 256, 256)
            to32 = lax.rem(32 * k - off - MARGIN + 512, 256)
            tw = pltpu.roll(pltpu.roll(t, to64, 1), up, 0)[:WROWS]

            def inner(x):
                return pltpu.roll(pltpu.roll(x, to32, 1)[:, :128], up_in, 0)[:SS]

            t, s, w = inner(t), inner(s), inner(w)
            if k == 0:
                window, sci, tmp, wgt = tw, s, t, w
            else:
                window = jnp.where(lane // 64 == k, tw, window)
                here = lane[:, :128] // 32 == k
                sci = jnp.where(here, s, sci)
                tmp = jnp.where(here, t, tmp)
                wgt = jnp.where(here, w, wgt)
        windows.append(window)
        sciences.append(sci)
        templates.append(tmp)
        weights.append(wgt)

    across = dot(jnp.concatenate(windows, 0), across_ref[...])
    row = 0
    for b, downs in GROUPS:
        piece = jnp.concatenate(
            [across[g * WROWS : (g + 1) * WROWS, b * 128 : (b + 1) * 128] for g in range(groups)], 1
        )
        count = len(downs) * SS
        made = dot(down_ref[row : row + count, :], piece)
        for g in range(groups):
            images[g, row : row + count, :] = made[:, g * 128 : (g + 1) * 128]
        row += count

    sci = jnp.concatenate(sciences, 0)
    tmp = jnp.concatenate(templates, 0)
    side = groups * SS
    first = dot(left_ref[...], jnp.concatenate([sci, tmp], 1))
    first = jnp.concatenate(
        [
            jnp.concatenate([first[:side, :128], first[side:, :128]], 1),
            jnp.concatenate([first[:side, 128:], first[side:, 128:]], 1),
        ],
        0,
    )
    second = dot(first, right_ref[...])
    sre, sim = second[:side, :128], second[:side, 128:]
    tre, tim = second[side:, :128], second[side:, 128:]
    cross_re = sre * tre + sim * tim
    cross_im = sim * tre - sre * tim
    magnitude = jnp.sqrt(cross_re * cross_re + cross_im * cross_im)
    mean = dot(dot(ones_ref[...], magnitude), ones_ref[...]) * (1.0 / (SS * SS))
    scaling = 1.0 / jnp.maximum(magnitude, 0.25 * (mean + 1e-06))
    unit = jnp.concatenate([cross_re * scaling, cross_im * scaling], 0)
    back = dot(back_left_ref[...], unit)
    surface = dot(jnp.concatenate([back[:side], back[side:]], 1), back_right_ref[...])
    narrow = lane[:, :128]
    target, pixel_weight = [], []
    for g in range(groups):
        best = jnp.max(surface[g * SS : (g + 1) * SS], axis=0, keepdims=True)
        best = jnp.broadcast_to(best, (8, 128))
        for step in (1, 2, 4, 8, 16):
            partner = jnp.where(
                narrow // step % 2 == 0,
                pltpu.roll(best, 128 - step, 1),
                pltpu.roll(best, step, 1),
            )
            best = jnp.maximum(best, partner)
        stamp_weight = jnp.maximum(best[:1], 0.1)
        pixel_weight.append(stamp_weight / weights[g])
        target.append(sciences[g] - templates[g])
    wide = groups * 128
    for g in range(groups):
        images[g, NB * SS : (NB + 1) * SS, :] = target[g]
        images[g, (NB + 1) * SS :, :] = jnp.zeros(((31 - NB) * SS, 128), jnp.float32)
    pixel_weight = jnp.concatenate(pixel_weight, 1)

    for r in range(SS):
        x = jnp.concatenate([images[g, pl.ds(r, 32, stride=SS), :] for g in range(groups)], 1)
        y = x * pixel_weight[r : r + 1, :]
        at = slice(r * wide, (r + 1) * wide)
        for value, ref in ((x, flat_x), (y, flat_y)):
            high = value.astype(jnp.bfloat16).astype(jnp.float32)
            ref[:, at] = jnp.concatenate([high, value - high], 0).astype(jnp.bfloat16)
    gram = lax.dot_general(
        flat_y[...], flat_x[...], (((1,), (1,)), ((), ())), preferred_element_type=jnp.float32
    )
    gram = gram[:32] + gram[32:]
    gram = gram + pltpu.roll(jnp.concatenate([gram, jnp.zeros((32, 64), jnp.float32)], 1), 96, 1)[:, :64]
    total = jnp.sum(jnp.sum(variance[...], axis=0, keepdims=True), axis=1, keepdims=True)
    total_t = jnp.sum(jnp.sum(template_variance[...], axis=0, keepdims=True), axis=1, keepdims=True)
    out[:32, :] = jnp.concatenate([gram, jnp.zeros((32, 64), jnp.float32)], 1)
    out[32:, :] = jnp.broadcast_to(jnp.where(narrow == 0, total, total_t), (8, 128))


def stamp_system(rows, cols, science, variance, template, template_variance):
    stamps = rows.shape[0]
    wide = stamps // 4 * 128
    tables = [across_table(), down_table(), *dft_blocks()]
    return pl.pallas_call(
        stamp_kernel,
        out_shape=jax.ShapeDtypeStruct((40, 128), jnp.float32),
        in_specs=[pl.BlockSpec(memory_space=SMEM)] * 2 + [pl.BlockSpec(memory_space=VMEM)] * 11,
        out_specs=pl.BlockSpec(memory_space=VMEM),
        scratch_shapes=[
            pltpu.VMEM((stamps // 4, 32 * SS, 128), jnp.float32),
            pltpu.VMEM((64, SS * wide), jnp.bfloat16),
            pltpu.VMEM((64, SS * wide), jnp.bfloat16),
        ],
        compiler_params=pltpu.CompilerParams(vmem_limit_bytes=VMEM_LIMIT),
        name="stamp_system",
    )(rows, cols, science, variance, template, template_variance, *[jnp.asarray(t) for t in tables])


def eliminate(a):
    row_index = lax.broadcasted_iota(jnp.int32, (32, 1), 0)
    for k in range(NB):
        pivot_row = a[k : k + 1, :]
        pivot_row = pivot_row / pivot_row[:, k : k + 1]
        column = a[:, k : k + 1] - (row_index == k).astype(jnp.float32)
        a = a - column * pivot_row
    return jnp.where(row_index < NB, a[:, NB : NB + 1], 0.0)


def widen(x):
    return jnp.concatenate([x, jnp.zeros((x.shape[0], 128 - x.shape[1]), jnp.float32)], 1)


def total_of(x):
    return jnp.sum(jnp.sum(x, axis=0, keepdims=True), axis=1, keepdims=True)


def correlate(kernel_t, before, own, after, stack, bands, products, out, science, column_chunk):
    height, columns = own.shape
    reach = height + 2 * MARGIN
    pad = 128
    lead = HALO - MARGIN
    for c in range(0, columns, column_chunk):
        at = slice(c, c + column_chunk)
        rows = jnp.concatenate([before[:, at], own[:, at], after[:, at]], 0)[lead : lead + reach]
        high = rows.astype(jnp.bfloat16).astype(jnp.float32)
        rest = jnp.zeros((256 - 3 * reach, column_chunk), jnp.float32)
        stack[:, at] = jnp.concatenate([high, rows - high, high, rest], 0).astype(jnp.bfloat16)
    high = kernel_t.astype(jnp.bfloat16).astype(jnp.float32)
    low = kernel_t - high
    blank = jnp.zeros_like(high)
    high, low = jnp.concatenate([high, blank], 1), jnp.concatenate([low, blank], 1)
    taps = high + pltpu.roll(high, reach, 1) + pltpu.roll(low, 2 * reach, 1)
    for v in range(KS):
        band = jnp.broadcast_to(taps[v : v + 1, :], (height, 256))
        band = pltpu.roll(band, 0, 1, stride=1, stride_axis=0)
        bands[v * height : (v + 1) * height, :] = band.astype(jnp.bfloat16)
    products[:, columns:] = jnp.zeros((KS * height, pad), jnp.float32)
    for c in range(0, columns, column_chunk):
        at = slice(c, c + column_chunk)
        products[:, at] = jnp.dot(bands[...], stack[:, at], preferred_element_type=jnp.float32)

    def finish(g, carry):
        at = pl.multiple_of(g * 8, 8)
        total = products[pl.ds((KS - 1) * height + at, 8), :]
        for v in range(KS - 2, -1, -1):
            total = pltpu.roll(total, columns + pad - 1, 1) + products[pl.ds(v * height + at, 8), :]
        total = pltpu.roll(total, MARGIN, 1)[:, :columns]
        rows = pl.ds(at, 8)
        out[rows, :] = total if science is None else science[rows, :] - total
        return carry

    lax.fori_loop(0, height // 8, finish, 0)


def first_kernel(pixels, p0, p1, p2, p3, science, before, own, after, lv, lu, left, right, back_left,
                 back_right, difference, filter_out, powers, stack, bands, products):
    sums = p0[...] + p1[...] + p2[...] + p3[...]
    coefficients = eliminate(sums[:32, :])
    mean_science = sums[32:33, 0:1] * (1.0 / pixels)
    mean_template = sums[32:33, 1:2] * (1.0 / pixels)
    kernel_t = dot(lv[...], coefficients * lu[...])
    v_index = lax.broadcasted_iota(jnp.int32, (32, 128), 0)
    u_index = lax.broadcasted_iota(jnp.int32, (32, 128), 1)
    kernel_t = kernel_t + ((v_index == MARGIN) & (u_index == MARGIN)).astype(jnp.float32)
    step = dot(left[...], kernel_t)
    both = dot(jnp.concatenate([step[:PD], step[PD:]], 1), right[...])
    re, im = both[:, :128], both[:, 128:]
    response = jnp.sqrt(
        (mean_science + mean_template) / (mean_science + mean_template * (re * re + im * im))
    )
    step = dot(back_left[...], response)
    filter_t = dot(jnp.concatenate([step[:32], step[32:]], 1), back_right[...])
    filter_out[...] = filter_t
    powers[0:1, :] = jnp.broadcast_to(total_of(kernel_t * kernel_t), (1, 128))
    powers[1:2, :] = jnp.broadcast_to(total_of(filter_t * filter_t), (1, 128))
    powers[2:, :] = jnp.zeros((6, 128), jnp.float32)
    correlate(kernel_t, before, own, after, stack, bands, products, difference, science, 512)


def second_kernel(filter_t, before, own, after, out, stack, bands, products):
    correlate(filter_t[...], before, own, after, stack, bands, products, out, None, 512)


def correlation_scratch(height, columns):
    return [
        pltpu.VMEM((256, columns), jnp.bfloat16),
        pltpu.VMEM((KS * height, 256), jnp.bfloat16),
        pltpu.VMEM((KS * height, columns + 128), jnp.float32),
    ]


def edges(strip, axis):
    devices, length = lax.axis_size(axis), strip.shape[0]
    up = [(i, i + 1) for i in range(devices - 1)]
    down = [(j, i) for i, j in up]
    before = lax.ppermute(strip[length - HALO :], axis, up)
    after = lax.ppermute(strip[:HALO], axis, down)
    return before, after


def per_device(science, variance, template_blocks, requests, stamp_rows, stamp_cols):
    height, columns = science.shape
    strips = lax.axis_size("det")
    device = lax.axis_index("det")
    held = template_blocks.shape[0]

    local = requests - device * held
    mine = (local >= 0) & (local < held)
    again = mine & jnp.pad(mine[:, :-1], ((0, 0), (1, 0)))
    first = jnp.sum(jnp.where(mine & ~again, local, 0), axis=1)
    second = jnp.sum(jnp.where(again, local, 0), axis=1)
    picks = jnp.stack([first, second], axis=1).reshape(-1).astype(jnp.int32)
    wanted = lax.dynamic_index_in_dim(requests, device, 0, keepdims=False)
    owner = wanted // held
    repeat = owner == jnp.concatenate([owner[:1] - 1, owner[:-1]])
    slots = (owner * 2 + repeat).astype(jnp.int32)

    received = lax.all_to_all(pick(picks, template_blocks), "det", 0, 0, tiled=True)
    template_image, template_variance = lay_strip(slots, received)
    before, after = edges(template_image, "det")
    partial = stamp_system(
        stamp_rows[0], stamp_cols[0], science, variance, template_image, template_variance
    )
    partials = [partial]
    for shift in range(1, CPER):
        partials.append(
            lax.ppermute(
                partial,
                "det",
                [(i, i // CPER * CPER + (i + shift) % CPER) for i in range(strips)],
            )
        )
    pixels = CPER * height * columns
    vmem = pl.BlockSpec(memory_space=VMEM)
    tables = [jnp.asarray(t) for t in (*basis_tables(), *filter_tables())]
    strip = jax.ShapeDtypeStruct((height, columns), jnp.float32)
    difference, filter_t, powers = pl.pallas_call(
        functools.partial(first_kernel, pixels),
        out_shape=[
            strip,
            jax.ShapeDtypeStruct((32, 128), jnp.float32),
            jax.ShapeDtypeStruct((8, 128), jnp.float32),
        ],
        in_specs=[vmem] * 14,
        out_specs=[vmem] * 3,
        scratch_shapes=correlation_scratch(height, columns),
        compiler_params=pltpu.CompilerParams(vmem_limit_bytes=VMEM_LIMIT),
        name="solve_and_subtract",
    )(*partials, science, before, template_image, after, *tables)
    before, after = edges(difference, "det")
    decorrelated_variance = powers[1, 0] * (variance + template_variance * powers[0, 0])
    decorrelated = pl.pallas_call(
        second_kernel,
        out_shape=strip,
        in_specs=[vmem] * 4,
        out_specs=vmem,
        scratch_shapes=correlation_scratch(height, columns),
        compiler_params=pltpu.CompilerParams(vmem_limit_bytes=VMEM_LIMIT),
        name="decorrelate",
    )(filter_t, before, difference, after)
    return (decorrelated, decorrelated_variance)


def solution(mesh):
    placed = (
        P(("group", "det"), None),
        P(("group", "det"), None),
        P(("group", "det"), None, None, None),
        P("group", None),
        P(("group", "det"), None),
        P(("group", "det"), None),
    )
    return jax.shard_map(
        per_device,
        mesh=mesh,
        in_specs=placed,
        out_specs=(P(("group", "det"), None), P(("group", "det"), None)),
        check_vma=False,
    )
```

```python
import functools

import jax
import jax.numpy as jnp
import numpy as np
from jax import lax
from jax.experimental import pallas as pl
from jax.experimental.pallas import tpu as pltpu
from jax.sharding import PartitionSpec as P

CPER = 4
SS = 32
KS = 21
PD = 32
MARGIN = KS // 2
HALO = 16
EXTENT = SS + 2 * MARGIN

HIGHEST = lax.Precision.HIGHEST
GAUSS_WIDTHS = (0.7, 1.5, 3.0)
GAUSS_DEGREES = (4, 2, 2)
VMEM_LIMIT = 60 * 1024 * 1024
VMEM = pltpu.MemorySpace.VMEM
SMEM = pltpu.MemorySpace.SMEM


def line_functions():
    tap_grid = np.arange(KS, dtype=np.float64) - MARGIN
    raw_list = []
    for spread, degree in zip(GAUSS_WIDTHS, GAUSS_DEGREES):
        gaussian = np.exp(-tap_grid * tap_grid / (2.0 * spread * spread))
        for degree_power in range(degree + 1):
            raw_list.append(gaussian * tap_grid**degree_power)
    result = []
    for vector in raw_list:
        for earlier in result:
            vector = vector - np.sum(vector * earlier) * earlier
        result.append(vector / np.sqrt(np.sum(vector * vector)))
    return np.stack(result)


def images_by_across():
    groups = []
    base = 0
    for degree in GAUSS_DEGREES:
        for inner in range(degree + 1):
            groups.append((base + inner, [base + outer for outer in range(degree + 1 - inner)]))
        base += degree + 1
    return groups


LINE = line_functions()
GROUPS = images_by_across()
PAIRS = [(a, b) for b, downs in GROUPS for a in downs]
NB = len(PAIRS)
NFUN = LINE.shape[0]
WROWS = 56
FINE, COARSE = 3, 7


def block_diag(matrix, times):
    rows, cols = matrix.shape
    out = np.zeros((rows * times, cols * times))
    for k in range(times):
        out[k * rows : (k + 1) * rows, k * cols : (k + 1) * cols] = matrix
    return out


def across_table():
    table = np.zeros((256, NFUN * 128))
    for b in range(NFUN):
        for k in range(4):
            for c in range(SS):
                table[64 * k + c : 64 * k + c + KS, b * 128 + 32 * k + c] = LINE[b]
    return table.astype(np.float32)


def down_table():
    table = np.zeros((NB * SS, WROWS))
    for image, (a, _) in enumerate(PAIRS):
        for r in range(SS):
            table[image * SS + r, r : r + KS] = LINE[a]
    return table.astype(np.float32)


def dft_blocks():
    grid = np.outer(np.arange(SS), np.arange(SS)) % SS
    c, s = np.cos(2 * np.pi * grid / SS), np.sin(2 * np.pi * grid / SS)
    c, s = block_diag(c, 4), block_diag(s, 4)
    ones = block_diag(np.ones((SS, SS)), 4)
    left = np.concatenate([c, s], 0)
    right = np.block([[c, -s], [-s, -c]])
    back_left = np.block([[c, -s], [s, c]])
    back_right = np.concatenate([c, -s], 0) / (SS * SS)
    return [x.astype(np.float32) for x in (left, right, back_left, back_right, ones)]


def basis_tables():
    lv, lu = np.zeros((32, 32)), np.zeros((32, 128))
    for image, (a, b) in enumerate(PAIRS):
        lv[:KS, image] = LINE[b]
        lu[image, :KS] = LINE[a]
    return lv.astype(np.float32), lu.astype(np.float32)


def filter_tables():
    grid = np.outer(np.arange(PD), np.arange(KS) - MARGIN)
    c, s = np.zeros((PD, 32)), np.zeros((PD, 32))
    c[:, :KS], s[:, :KS] = np.cos(2 * np.pi * grid / PD), np.sin(2 * np.pi * grid / PD)
    cr, sr = np.zeros((128, 128)), np.zeros((128, 128))
    cr[:32, :PD], sr[:32, :PD] = c.T, s.T
    left = np.concatenate([c, s], 0)
    right = np.block([[cr, -sr], [-sr, -cr]])
    back_left = np.concatenate([c.T, s.T], 0) / (PD * PD)
    back_c, back_s = np.zeros((128, 128)), np.zeros((128, 128))
    back_c[:PD, :32], back_s[:PD, :32] = c, s
    back_right = np.concatenate([back_c, -back_s], 0)
    return [x.astype(np.float32) for x in (left, right, back_left, back_right)]


def pick_kernel(picks, source, out, sem):
    count = out.shape[0]

    def copy(k):
        return pltpu.make_async_copy(source.at[picks[k]], out.at[k], sem.at[k])

    def start(k, carry):
        copy(k).start()
        return carry

    def finish(k, carry):
        copy(k).wait()
        return carry

    lax.fori_loop(0, count, start, 0)
    lax.fori_loop(0, count, finish, 0)


def pick(picks, source, flops=10**6):
    count = picks.shape[0]
    return pl.pallas_call(
        pick_kernel,
        out_shape=jax.ShapeDtypeStruct((count,) + source.shape[1:], source.dtype),
        in_specs=[pl.BlockSpec(memory_space=SMEM), pl.BlockSpec(memory_space=VMEM)],
        out_specs=pl.BlockSpec(memory_space=pl.ANY),
        scratch_shapes=[pltpu.SemaphoreType.DMA((count,))],
        compiler_params=pltpu.CompilerParams(vmem_limit_bytes=VMEM_LIMIT),
        cost_estimate=pl.CostEstimate(flops=flops, bytes_accessed=10**6, transcendentals=0),
        name="pick_blocks",
    )(picks, source)


def lay_strip(slots, is_near, near, far, plane, out, sem):
    needed = slots.shape[0]
    width = near.shape[3]
    for j in range(needed):
        columns = pl.ds(j * width, width)

        @pl.when(is_near[j] == 1)
        def _():
            pltpu.make_async_copy(near.at[slots[j], plane], out.at[:, columns], sem.at[j]).start()

        @pl.when(is_near[j] == 0)
        def _():
            pltpu.make_async_copy(far.at[slots[j]], out.at[:, columns], sem.at[j]).start()

    for j in range(needed):
        columns = pl.ds(j * width, width)
        pltpu.make_async_copy(far.at[slots[j]], out.at[:, columns], sem.at[j]).wait()


def dot(a, b, contract=((1,), (0,))):
    return lax.dot_general(
        a, b, (contract, ((), ())), precision=HIGHEST, preferred_element_type=jnp.float32
    )


def split(x):
    high = x.astype(jnp.bfloat16)
    return high, (x - high.astype(jnp.float32)).astype(jnp.bfloat16)


def stamp_place(stamp_rows, stamp_cols, stamp, columns):
    row = stamp_rows[stamp] - (SS // 2 + MARGIN)
    col = stamp_cols[stamp] - (SS // 2 + MARGIN)
    base = pl.multiple_of(jnp.minimum(col // 128 * 128, columns - 256), 128)
    return row, col - base, pl.ds(base, 256)


def inner_stamp(x, row, off, k):
    moved = pltpu.roll(x, lax.rem(32 * k - off - MARGIN + 512, 256), 1)[:, :128]
    return pltpu.roll(moved, x.shape[0] - row - MARGIN, 0)[:SS]


def image_kernel(stamp_rows, stamp_cols, slots, is_near, near, far, science, variance, across_ref,
                 down_ref, left_ref, right_ref, back_left_ref, back_right_ref, ones_ref,
                 template, flat_x, variance_stamps, stamp_weights, variance_sum, images, sem):
    lay_strip(slots, is_near, near, far, 0, template, sem)
    height, columns = science.shape
    stamps = stamp_rows.shape[0]
    groups = stamps // 4
    lane = lax.broadcasted_iota(jnp.int32, (1, 256), 1)

    windows, sciences, templates = [], [], []
    for g in range(groups):
        window = sci = tmp = var = None
        for k in range(4):
            row, off, cols = stamp_place(stamp_rows, stamp_cols, g * 4 + k, columns)
            t = template[:, cols]
            to64 = lax.rem(64 * k - off + 256, 256)
            tw = pltpu.roll(pltpu.roll(t, to64, 1), lax.rem(height - row, height), 0)[:WROWS]
            t = inner_stamp(t, row, off, k)
            s = inner_stamp(science[:, cols], row, off, k)
            v = inner_stamp(variance[:, cols], row, off, k)
            if k == 0:
                window, sci, tmp, var = tw, s, t, v
            else:
                window = jnp.where(lane // 64 == k, tw, window)
                here = lane[:, :128] // 32 == k
                sci = jnp.where(here, s, sci)
                tmp = jnp.where(here, t, tmp)
                var = jnp.where(here, v, var)
        windows.append(window)
        sciences.append(sci)
        templates.append(tmp)
        variance_stamps[g * SS : (g + 1) * SS, :] = var

    across = dot(jnp.concatenate(windows, 0), across_ref[...])
    row = 0
    for b, downs in GROUPS:
        piece = jnp.concatenate(
            [across[g * WROWS : (g + 1) * WROWS, b * 128 : (b + 1) * 128] for g in range(groups)], 1
        )
        count = len(downs) * SS
        made = dot(down_ref[row : row + count, :], piece)
        for g in range(groups):
            images[g, row : row + count, :] = made[:, g * 128 : (g + 1) * 128]
        row += count
    for g in range(groups):
        images[g, NB * SS : (NB + 1) * SS, :] = sciences[g] - templates[g]
        images[g, (NB + 1) * SS :, :] = jnp.zeros(((31 - NB) * SS, 128), jnp.float32)
    wide = groups * 128
    for r in range(SS):
        x = jnp.concatenate([images[g, pl.ds(r, 32, stride=SS), :] for g in range(groups)], 1)
        high = x.astype(jnp.bfloat16).astype(jnp.float32)
        pair = jnp.concatenate([high, x - high], 0).astype(jnp.bfloat16)
        flat_x[:, r * wide : (r + 1) * wide] = pair

    sci = jnp.concatenate(sciences, 0)
    tmp = jnp.concatenate(templates, 0)
    side = groups * SS
    first = dot(left_ref[...], jnp.concatenate([sci, tmp], 1))
    first = jnp.concatenate(
        [
            jnp.concatenate([first[:side, :128], first[side:, :128]], 1),
            jnp.concatenate([first[:side, 128:], first[side:, 128:]], 1),
        ],
        0,
    )
    second = dot(first, right_ref[...])
    sre, sim = second[:side, :128], second[:side, 128:]
    tre, tim = second[side:, :128], second[side:, 128:]
    cross_re = sre * tre + sim * tim
    cross_im = sim * tre - sre * tim
    magnitude = jnp.sqrt(cross_re * cross_re + cross_im * cross_im)
    mean = dot(dot(ones_ref[...], magnitude), ones_ref[...]) * (1.0 / (SS * SS))
    scaling = 1.0 / jnp.maximum(magnitude, 0.25 * (mean + 1e-06))
    unit = jnp.concatenate([cross_re * scaling, cross_im * scaling], 0)
    back = dot(back_left_ref[...], unit)
    surface = dot(jnp.concatenate([back[:side], back[side:]], 1), back_right_ref[...])
    narrow = lane[:, :128]
    for g in range(groups):
        best = jnp.max(surface[g * SS : (g + 1) * SS], axis=0, keepdims=True)
        best = jnp.broadcast_to(best, (8, 128))
        for step in (1, 2, 4, 8, 16):
            partner = jnp.where(
                narrow // step % 2 == 0,
                pltpu.roll(best, 128 - step, 1),
                pltpu.roll(best, step, 1),
            )
            best = jnp.maximum(best, partner)
        stamp_weights[g * 8 : (g + 1) * 8, :] = jnp.maximum(best, 0.1)
    variance_sum[...] = jnp.broadcast_to(total_of(variance[...]), (8, 128))


def normal_kernel(stamp_rows, stamp_cols, slots, is_near, near, far, flat_x, variance_stamps,
                  stamp_weights, variance_sum, template_variance, out, flat_y, sem):
    lay_strip(slots, is_near, near, far, 1, template_variance, sem)
    _, columns = template_variance.shape
    stamps = stamp_rows.shape[0]
    groups = stamps // 4
    narrow = lax.broadcasted_iota(jnp.int32, (1, 128), 1)
    pixel_weight = []
    for g in range(groups):
        weight = None
        for k in range(4):
            row, off, cols = stamp_place(stamp_rows, stamp_cols, g * 4 + k, columns)
            w = inner_stamp(template_variance[:, cols], row, off, k)
            weight = w if k == 0 else jnp.where(narrow // 32 == k, w, weight)
        weight = variance_stamps[g * SS : (g + 1) * SS, :] + weight
        pixel_weight.append(stamp_weights[g * 8 : g * 8 + 1, :] / weight)
    pixel_weight = jnp.concatenate(pixel_weight, 1)
    wide = groups * 128
    for r in range(SS):
        at = slice(r * wide, (r + 1) * wide)
        pair = flat_x[:, at].astype(jnp.float32)
        y = (pair[:32] + pair[32:]) * pixel_weight[r : r + 1, :]
        high = y.astype(jnp.bfloat16).astype(jnp.float32)
        flat_y[:, at] = jnp.concatenate([high, y - high], 0).astype(jnp.bfloat16)
    gram = lax.dot_general(
        flat_y[...], flat_x[...], (((1,), (1,)), ((), ())), preferred_element_type=jnp.float32
    )
    gram = widen(gram[:32] + gram[32:])
    out[:32, :] = gram + pltpu.roll(gram, 96, 1)
    total_t = total_of(template_variance[...])
    out[32:, :] = jnp.where(narrow == 0, variance_sum[...], jnp.broadcast_to(total_t, (8, 128)))


def eliminate(a):
    row_index = lax.broadcasted_iota(jnp.int32, (32, 1), 0)
    for k in range(NB):
        pivot_row = a[k : k + 1, :]
        pivot_row = pivot_row / pivot_row[:, k : k + 1]
        column = a[:, k : k + 1] - (row_index == k).astype(jnp.float32)
        a = a - column * pivot_row
    return jnp.where(row_index < NB, a[:, NB : NB + 1], 0.0)


def widen(x):
    return jnp.concatenate([x, jnp.zeros((x.shape[0], 128 - x.shape[1]), jnp.float32)], 1)


def total_of(x):
    return jnp.sum(jnp.sum(x, axis=0, keepdims=True), axis=1, keepdims=True)


def correlate(kernel_t, before, own, after, stack, bands, products, out, science):
    height, columns = own.shape
    reach = height + 2 * MARGIN
    lead = HALO - MARGIN
    tiles = columns // 128 + 1
    high = kernel_t.astype(jnp.bfloat16).astype(jnp.float32)
    low = kernel_t - high
    blank = jnp.zeros_like(high)
    high, low = jnp.concatenate([high, blank], 1), jnp.concatenate([low, blank], 1)
    taps = high + pltpu.roll(high, reach, 1) + pltpu.roll(low, 2 * reach, 1)
    for v in range(KS):
        w, j = v // FINE, v % FINE
        band = jnp.broadcast_to(taps[v : v + 1, :], (height, 256))
        band = pltpu.roll(band, 0, 1, stride=1, stride_axis=0)
        bands[w * height : (w + 1) * height, j * 256 : (j + 1) * 256] = band.astype(jnp.bfloat16)

    lane = lax.broadcasted_iota(jnp.int32, (1, 128), 1)
    rest = jnp.zeros((256 - 3 * reach, 128), jnp.float32)
    empty = jnp.zeros((reach, 128), jnp.float32)

    def tile(t):
        if t % tiles == tiles - 1:
            return empty
        at = slice(t % tiles * 128, (t % tiles + 1) * 128)
        return jnp.concatenate([before[:, at], own[:, at], after[:, at]], 0)[lead : lead + reach]

    left, here = tile(-1), tile(0)
    left_last = pltpu.roll(left, 1, 1)
    here_last = pltpu.roll(here, 1, 1)
    here_next = pltpu.roll(here, 127, 1)
    for t in range(tiles):
        right = tile(t + 1)
        right_last, right_next = pltpu.roll(right, 1, 1), pltpu.roll(right, 127, 1)
        moved = (
            jnp.where(lane < 1, left_last, here_last),
            here,
            jnp.where(lane < 127, here_next, right_next),
        )
        for j, x in enumerate(moved):
            high = x.astype(jnp.bfloat16).astype(jnp.float32)
            stack[j * 256 : (j + 1) * 256, t * 128 : (t + 1) * 128] = jnp.concatenate(
                [high, x - high, high, rest], 0
            ).astype(jnp.bfloat16)
        left_last, here, here_last, here_next = here_last, right, right_last, right_next
    chunk = 384 if tiles % 3 == 0 else 128
    for c in range(0, tiles * 128, chunk):
        at = slice(c, c + chunk)
        products[:, at] = jnp.dot(bands[...], stack[:, at], preferred_element_type=jnp.float32)

    def finish(g, carry):
        at = pl.multiple_of(g * 8, 8)

        def product(w):
            return products[pl.ds(w * height + at, 8), :]

        half = COARSE // 2
        ahead, behind = product(COARSE - 1), product(0)
        for w in range(half - 1):
            ahead = pltpu.roll(ahead, tiles * 128 - FINE, 1) + product(COARSE - 2 - w)
            behind = pltpu.roll(behind, FINE, 1) + product(w + 1)
        total = product(half) + pltpu.roll(ahead, tiles * 128 - FINE, 1) + pltpu.roll(behind, FINE, 1)
        total = total[:, :columns]
        rows = pl.ds(at, 8)
        out[rows, :] = total if science is None else science[rows, :] - total
        return carry

    lax.fori_loop(0, height // 8, finish, 0)


def first_kernel(pixels, p0, p1, p2, p3, science, before, own, after, lv, lu, left, right, back_left,
                 back_right, difference, filter_out, powers, stack, bands, products):
    sums = p0[...] + p1[...] + p2[...] + p3[...]
    coefficients = eliminate(sums[:32, :])
    mean_science = sums[32:33, 0:1] * (1.0 / pixels)
    mean_template = sums[32:33, 1:2] * (1.0 / pixels)
    kernel_t = dot(lv[...], coefficients * lu[...])
    v_index = lax.broadcasted_iota(jnp.int32, (32, 128), 0)
    u_index = lax.broadcasted_iota(jnp.int32, (32, 128), 1)
    kernel_t = kernel_t + ((v_index == MARGIN) & (u_index == MARGIN)).astype(jnp.float32)
    step = dot(left[...], kernel_t)
    both = dot(jnp.concatenate([step[:PD], step[PD:]], 1), right[...])
    re, im = both[:, :128], both[:, 128:]
    response = jnp.sqrt(
        (mean_science + mean_template) / (mean_science + mean_template * (re * re + im * im))
    )
    step = dot(back_left[...], response)
    filter_t = dot(jnp.concatenate([step[:32], step[32:]], 1), back_right[...])
    filter_out[...] = filter_t
    powers[0:1, :] = jnp.broadcast_to(total_of(kernel_t * kernel_t), (1, 128))
    powers[1:2, :] = jnp.broadcast_to(total_of(filter_t * filter_t), (1, 128))
    powers[2:, :] = jnp.zeros((6, 128), jnp.float32)
    correlate(kernel_t, before, own, after, stack, bands, products, difference, science)


def second_kernel(filter_t, before, own, after, out, stack, bands, products):
    correlate(filter_t[...], before, own, after, stack, bands, products, out, None)


def correlation_scratch(height, columns):
    return [
        pltpu.VMEM((FINE * 256, columns + 128), jnp.bfloat16),
        pltpu.VMEM((COARSE * height, FINE * 256), jnp.bfloat16),
        pltpu.VMEM((COARSE * height, columns + 128), jnp.float32),
    ]


def edges(strip, axis):
    devices, length = lax.axis_size(axis), strip.shape[0]
    up = [(i, i + 1) for i in range(devices - 1)]
    down = [(j, i) for i, j in up]
    before = lax.ppermute(strip[length - HALO :], axis, up)
    after = lax.ppermute(strip[:HALO], axis, down)
    return before, after


def per_device(science, variance, template_blocks, requests, stamp_rows, stamp_cols):
    height, columns = science.shape
    strips = lax.axis_size("det")
    device = lax.axis_index("det")
    held = template_blocks.shape[0]

    half = strips // 2
    here = device // half
    partner = lax.rem(device + half, strips)
    served = lax.dynamic_slice_in_dim(requests, here * half, half, 0)

    def picks_of(owner):
        local = served - owner * held
        mine = (local >= 0) & (local < held)
        again = mine & jnp.pad(mine[:, :-1], ((0, 0), (1, 0)))
        first = jnp.sum(jnp.where(mine & ~again, local, 0), axis=1)
        second = jnp.sum(jnp.where(again, local, 0), axis=1)
        return jnp.stack([first, second], axis=1).reshape(-1).astype(jnp.int32)

    wanted = lax.dynamic_index_in_dim(requests, device, 0, keepdims=False)
    owner = wanted // held
    repeat = owner == jnp.concatenate([owner[:1] - 1, owner[:-1]])
    slots = (owner % half * 2 + repeat).astype(jnp.int32)
    is_near = (owner // half == here).astype(jnp.int32)

    across_halves = [(i, (i + half) % strips) for i in range(strips)]
    halves = [list(range(half)), list(range(half, strips))]

    def serve(x):
        return lax.all_to_all(x, "det", 0, 0, axis_index_groups=halves, tiled=True)

    partner_image = lax.ppermute(template_blocks[:, 0], "det", across_halves)
    near = serve(pick(picks_of(device), template_blocks, 10**11))
    partner_planes, partner_image = lax.optimization_barrier((template_blocks[:, 1], partner_image))
    partner_variance = lax.ppermute(partner_planes, "det", across_halves)
    far_picks = picks_of(partner)
    partner_image, near = lax.optimization_barrier((partner_image, near))
    far_image = serve(pick(far_picks, partner_image))
    far_variance = serve(pick(far_picks, partner_variance))

    vmem, smem, anywhere = (pl.BlockSpec(memory_space=m) for m in (VMEM, SMEM, pl.ANY))
    rows, cols = stamp_rows[0], stamp_cols[0]
    stamps = rows.shape[0]
    flat = SS * SS * stamps
    strip = jax.ShapeDtypeStruct((height, columns), jnp.float32)
    row = jax.ShapeDtypeStruct((8, 128), jnp.float32)
    tables = [jnp.asarray(t) for t in (across_table(), down_table(), *dft_blocks())]
    params = pltpu.CompilerParams(vmem_limit_bytes=VMEM_LIMIT)
    template_image, flat_x, variance_stamps, stamp_weights, variance_sum = pl.pallas_call(
        image_kernel,
        out_shape=[
            strip,
            jax.ShapeDtypeStruct((64, flat), jnp.bfloat16),
            jax.ShapeDtypeStruct((stamps // 4 * SS, 128), jnp.float32),
            jax.ShapeDtypeStruct((stamps // 4 * 8, 128), jnp.float32),
            row,
        ],
        in_specs=[smem] * 4 + [anywhere] * 2 + [vmem] * 9,
        out_specs=[vmem] * 5,
        scratch_shapes=[
            pltpu.VMEM((stamps // 4, 32 * SS, 128), jnp.float32),
            pltpu.SemaphoreType.DMA((wanted.shape[0],)),
        ],
        compiler_params=params,
        cost_estimate=pl.CostEstimate(flops=10**10, bytes_accessed=10**7, transcendentals=0),
        name="stamp_images",
    )(rows, cols, slots, is_near, near, far_image, science, variance, *tables)
    before, after = edges(template_image, "det")
    template_variance, partial = pl.pallas_call(
        normal_kernel,
        out_shape=[strip, jax.ShapeDtypeStruct((40, 128), jnp.float32)],
        in_specs=[smem] * 4 + [anywhere] * 2 + [vmem] * 4,
        out_specs=[vmem] * 2,
        scratch_shapes=[
            pltpu.VMEM((64, flat), jnp.bfloat16),
            pltpu.SemaphoreType.DMA((wanted.shape[0],)),
        ],
        compiler_params=params,
        name="normal_equations",
    )(rows, cols, slots, is_near, near, far_variance, flat_x, variance_stamps, stamp_weights, variance_sum)
    partials = [partial]
    for shift in range(1, CPER):
        partials.append(
            lax.ppermute(
                partial,
                "det",
                [(i, i // CPER * CPER + (i + shift) % CPER) for i in range(strips)],
            )
        )
    pixels = CPER * height * columns
    tables = [jnp.asarray(t) for t in (*basis_tables(), *filter_tables())]
    difference, filter_t, powers = pl.pallas_call(
        functools.partial(first_kernel, pixels),
        out_shape=[
            strip,
            jax.ShapeDtypeStruct((32, 128), jnp.float32),
            row,
        ],
        in_specs=[vmem] * 14,
        out_specs=[vmem] * 3,
        scratch_shapes=correlation_scratch(height, columns),
        compiler_params=pltpu.CompilerParams(vmem_limit_bytes=VMEM_LIMIT),
        name="solve_and_subtract",
    )(*partials, science, before, template_image, after, *tables)
    before, after = edges(difference, "det")
    decorrelated_variance = powers[1, 0] * (variance + template_variance * powers[0, 0])
    decorrelated = pl.pallas_call(
        second_kernel,
        out_shape=strip,
        in_specs=[vmem] * 4,
        out_specs=vmem,
        scratch_shapes=correlation_scratch(height, columns),
        compiler_params=pltpu.CompilerParams(vmem_limit_bytes=VMEM_LIMIT),
        name="decorrelate",
    )(filter_t, before, difference, after)
    return (decorrelated, decorrelated_variance)


def solution(mesh):
    placed = (
        P(("group", "det"), None),
        P(("group", "det"), None),
        P(("group", "det"), None, None, None),
        P("group", None),
        P(("group", "det"), None),
        P(("group", "det"), None),
    )
    return jax.shard_map(
        per_device,
        mesh=mesh,
        in_specs=placed,
        out_specs=(P(("group", "det"), None), P(("group", "det"), None)),
        check_vma=False,
    )
```

```python
import functools

import jax
import jax.numpy as jnp
import numpy as np
from jax import lax
from jax.experimental import pallas as pl
from jax.experimental.pallas import tpu as pltpu
from jax.sharding import PartitionSpec as P

CPER = 4
SS = 32
KS = 21
PD = 32
MARGIN = KS // 2
HALO = 16
EXTENT = SS + 2 * MARGIN

HIGHEST = lax.Precision.HIGHEST
GAUSS_WIDTHS = (0.7, 1.5, 3.0)
GAUSS_DEGREES = (4, 2, 2)
VMEM_LIMIT = 60 * 1024 * 1024
VMEM_SMALL = 32 * 1024 * 1024
VMEM = pltpu.MemorySpace.VMEM
SMEM = pltpu.MemorySpace.SMEM


def line_functions():
    tap_grid = np.arange(KS, dtype=np.float64) - MARGIN
    raw_list = []
    for spread, degree in zip(GAUSS_WIDTHS, GAUSS_DEGREES):
        gaussian = np.exp(-tap_grid * tap_grid / (2.0 * spread * spread))
        for degree_power in range(degree + 1):
            raw_list.append(gaussian * tap_grid**degree_power)
    result = []
    for vector in raw_list:
        for earlier in result:
            vector = vector - np.sum(vector * earlier) * earlier
        result.append(vector / np.sqrt(np.sum(vector * vector)))
    return np.stack(result)


def images_by_across():
    groups = []
    base = 0
    for degree in GAUSS_DEGREES:
        for inner in range(degree + 1):
            groups.append((base + inner, [base + outer for outer in range(degree + 1 - inner)]))
        base += degree + 1
    return groups


LINE = line_functions()
GROUPS = images_by_across()
PAIRS = [(a, b) for b, downs in GROUPS for a in downs]
NB = len(PAIRS)
NFUN = LINE.shape[0]
WROWS = 56
FINE, COARSE = 3, 7


def block_diag(matrix, times):
    rows, cols = matrix.shape
    out = np.zeros((rows * times, cols * times))
    for k in range(times):
        out[k * rows : (k + 1) * rows, k * cols : (k + 1) * cols] = matrix
    return out


def across_table():
    table = np.zeros((256, NFUN * 128))
    for b in range(NFUN):
        for k in range(4):
            for c in range(SS):
                table[64 * k + c : 64 * k + c + KS, b * 128 + 32 * k + c] = LINE[b]
    return table.astype(np.float32)


def down_table():
    table = np.zeros((NB * SS, WROWS))
    for image, (a, _) in enumerate(PAIRS):
        for r in range(SS):
            table[image * SS + r, r : r + KS] = LINE[a]
    return table.astype(np.float32)


def dft_blocks():
    grid = np.outer(np.arange(SS), np.arange(SS)) % SS
    c, s = np.cos(2 * np.pi * grid / SS), np.sin(2 * np.pi * grid / SS)
    c, s = block_diag(c, 4), block_diag(s, 4)
    ones = block_diag(np.ones((SS, SS)), 4)
    left = np.concatenate([c, s], 0)
    right = np.block([[c, -s], [-s, -c]])
    back_left = np.block([[c, -s], [s, c]])
    back_right = np.concatenate([c, -s], 0) / (SS * SS)
    return [x.astype(np.float32) for x in (left, right, back_left, back_right, ones)]


def basis_tables():
    lv, lu = np.zeros((32, 32)), np.zeros((32, 128))
    for image, (a, b) in enumerate(PAIRS):
        lv[:KS, image] = LINE[b]
        lu[image, :KS] = LINE[a]
    return lv.astype(np.float32), lu.astype(np.float32)


def filter_tables():
    grid = np.outer(np.arange(PD), np.arange(KS) - MARGIN)
    c, s = np.zeros((PD, 32)), np.zeros((PD, 32))
    c[:, :KS], s[:, :KS] = np.cos(2 * np.pi * grid / PD), np.sin(2 * np.pi * grid / PD)
    cr, sr = np.zeros((128, 128)), np.zeros((128, 128))
    cr[:32, :PD], sr[:32, :PD] = c.T, s.T
    left = np.concatenate([c, s], 0)
    right = np.block([[cr, -sr], [-sr, -cr]])
    back_left = np.concatenate([c.T, s.T], 0) / (PD * PD)
    back_c, back_s = np.zeros((128, 128)), np.zeros((128, 128))
    back_c[:PD, :32], back_s[:PD, :32] = c, s
    back_right = np.concatenate([back_c, -back_s], 0)
    return [x.astype(np.float32) for x in (left, right, back_left, back_right)]


def pick_kernel(plane, picks, source, out, sem):
    count = out.shape[0]

    def copy(k):
        block = source.at[picks[k]] if plane is None else source.at[picks[k], plane]
        return pltpu.make_async_copy(block, out.at[k], sem.at[k])

    def start(k, carry):
        copy(k).start()
        return carry

    def finish(k, carry):
        copy(k).wait()
        return carry

    lax.fori_loop(0, count, start, 0)
    lax.fori_loop(0, count, finish, 0)


def pick(picks, source, plane=None):
    count = picks.shape[0]
    shape = source.shape[1:] if plane is None else source.shape[2:]
    return pl.pallas_call(
        functools.partial(pick_kernel, plane),
        out_shape=jax.ShapeDtypeStruct((count,) + shape, source.dtype),
        in_specs=[pl.BlockSpec(memory_space=SMEM), pl.BlockSpec(memory_space=VMEM)],
        out_specs=pl.BlockSpec(memory_space=pl.ANY),
        scratch_shapes=[pltpu.SemaphoreType.DMA((count,))],
        compiler_params=pltpu.CompilerParams(vmem_limit_bytes=VMEM_LIMIT),
        name="pick_blocks",
    )(picks, source)


def lay_strip(slots, is_near, near, far, plane, out, sem):
    needed = slots.shape[0]
    width = near.shape[3]
    for j in range(needed):
        columns = pl.ds(j * width, width)

        @pl.when(is_near[j] == 1)
        def _():
            pltpu.make_async_copy(near.at[slots[j], plane], out.at[:, columns], sem.at[j]).start()

        @pl.when(is_near[j] == 0)
        def _():
            pltpu.make_async_copy(far.at[slots[j]], out.at[:, columns], sem.at[j]).start()

    for j in range(needed):
        columns = pl.ds(j * width, width)
        pltpu.make_async_copy(far.at[slots[j]], out.at[:, columns], sem.at[j]).wait()


def dot(a, b, contract=((1,), (0,))):
    return lax.dot_general(
        a, b, (contract, ((), ())), precision=HIGHEST, preferred_element_type=jnp.float32
    )


def split(x):
    high = x.astype(jnp.bfloat16)
    return high, (x - high.astype(jnp.float32)).astype(jnp.bfloat16)


def stamp_place(stamp_rows, stamp_cols, stamp, columns):
    row = stamp_rows[stamp] - (SS // 2 + MARGIN)
    col = stamp_cols[stamp] - (SS // 2 + MARGIN)
    base = pl.multiple_of(jnp.minimum(col // 128 * 128, columns - 256), 128)
    return row, col - base, pl.ds(base, 256)


def inner_stamp(x, row, off, k):
    moved = pltpu.roll(x, lax.rem(32 * k - off - MARGIN + 512, 256), 1)[:, :128]
    return pltpu.roll(moved, x.shape[0] - row - MARGIN, 0)[:SS]


def image_kernel(stamp_rows, stamp_cols, slots, is_near, near, far, science, variance, across_ref,
                 down_ref, left_ref, right_ref, back_left_ref, back_right_ref, ones_ref,
                 template, top, bottom, flat_x, variance_stamps, stamp_weights, variance_sum, images, sem):
    lay_strip(slots, is_near, near, far, 0, template, sem)
    top[...] = template[:HALO, :]
    bottom[...] = template[template.shape[0] - HALO :, :]
    height, columns = science.shape
    stamps = stamp_rows.shape[0]
    groups = stamps // 4
    lane = lax.broadcasted_iota(jnp.int32, (1, 256), 1)

    windows, sciences, templates = [], [], []
    for g in range(groups):
        window = sci = tmp = var = None
        for k in range(4):
            row, off, cols = stamp_place(stamp_rows, stamp_cols, g * 4 + k, columns)
            t = template[:, cols]
            to64 = lax.rem(64 * k - off + 256, 256)
            tw = pltpu.roll(pltpu.roll(t, to64, 1), lax.rem(height - row, height), 0)[:WROWS]
            t = inner_stamp(t, row, off, k)
            s = inner_stamp(science[:, cols], row, off, k)
            v = inner_stamp(variance[:, cols], row, off, k)
            if k == 0:
                window, sci, tmp, var = tw, s, t, v
            else:
                window = jnp.where(lane // 64 == k, tw, window)
                here = lane[:, :128] // 32 == k
                sci = jnp.where(here, s, sci)
                tmp = jnp.where(here, t, tmp)
                var = jnp.where(here, v, var)
        windows.append(window)
        sciences.append(sci)
        templates.append(tmp)
        variance_stamps[g * SS : (g + 1) * SS, :] = var

    across = dot(jnp.concatenate(windows, 0), across_ref[...])
    row = 0
    for b, downs in GROUPS:
        piece = jnp.concatenate(
            [across[g * WROWS : (g + 1) * WROWS, b * 128 : (b + 1) * 128] for g in range(groups)], 1
        )
        count = len(downs) * SS
        made = dot(down_ref[row : row + count, :], piece)
        for g in range(groups):
            images[g, row : row + count, :] = made[:, g * 128 : (g + 1) * 128]
        row += count
    for g in range(groups):
        images[g, NB * SS : (NB + 1) * SS, :] = sciences[g] - templates[g]
        images[g, (NB + 1) * SS :, :] = jnp.zeros(((31 - NB) * SS, 128), jnp.float32)
    wide = groups * 128
    for r in range(SS):
        x = jnp.concatenate([images[g, pl.ds(r, 32, stride=SS), :] for g in range(groups)], 1)
        high = x.astype(jnp.bfloat16).astype(jnp.float32)
        pair = jnp.concatenate([high, x - high], 0).astype(jnp.bfloat16)
        flat_x[:, r * wide : (r + 1) * wide] = pair

    sci = jnp.concatenate(sciences, 0)
    tmp = jnp.concatenate(templates, 0)
    side = groups * SS
    first = dot(left_ref[...], jnp.concatenate([sci, tmp], 1))
    first = jnp.concatenate(
        [
            jnp.concatenate([first[:side, :128], first[side:, :128]], 1),
            jnp.concatenate([first[:side, 128:], first[side:, 128:]], 1),
        ],
        0,
    )
    second = dot(first, right_ref[...])
    sre, sim = second[:side, :128], second[:side, 128:]
    tre, tim = second[side:, :128], second[side:, 128:]
    cross_re = sre * tre + sim * tim
    cross_im = sim * tre - sre * tim
    magnitude = jnp.sqrt(cross_re * cross_re + cross_im * cross_im)
    mean = dot(dot(ones_ref[...], magnitude), ones_ref[...]) * (1.0 / (SS * SS))
    scaling = 1.0 / jnp.maximum(magnitude, 0.25 * (mean + 1e-06))
    unit = jnp.concatenate([cross_re * scaling, cross_im * scaling], 0)
    back = dot(back_left_ref[...], unit)
    surface = dot(jnp.concatenate([back[:side], back[side:]], 1), back_right_ref[...])
    narrow = lane[:, :128]
    for g in range(groups):
        best = jnp.max(surface[g * SS : (g + 1) * SS], axis=0, keepdims=True)
        best = jnp.broadcast_to(best, (8, 128))
        for step in (1, 2, 4, 8, 16):
            partner = jnp.where(
                narrow // step % 2 == 0,
                pltpu.roll(best, 128 - step, 1),
                pltpu.roll(best, step, 1),
            )
            best = jnp.maximum(best, partner)
        stamp_weights[g * 8 : (g + 1) * 8, :] = jnp.maximum(best, 0.1)
    variance_sum[...] = jnp.broadcast_to(total_of(variance[...]), (8, 128))


def normal_kernel(stamp_rows, stamp_cols, slots, is_near, near, far, flat_x, variance_stamps,
                  stamp_weights, variance_sum, template_variance, out, flat_y, sem):
    lay_strip(slots, is_near, near, far, 1, template_variance, sem)
    _, columns = template_variance.shape
    stamps = stamp_rows.shape[0]
    groups = stamps // 4
    narrow = lax.broadcasted_iota(jnp.int32, (1, 128), 1)
    pixel_weight = []
    for g in range(groups):
        weight = None
        for k in range(4):
            row, off, cols = stamp_place(stamp_rows, stamp_cols, g * 4 + k, columns)
            w = inner_stamp(template_variance[:, cols], row, off, k)
            weight = w if k == 0 else jnp.where(narrow // 32 == k, w, weight)
        weight = variance_stamps[g * SS : (g + 1) * SS, :] + weight
        pixel_weight.append(stamp_weights[g * 8 : g * 8 + 1, :] / weight)
    pixel_weight = jnp.concatenate(pixel_weight, 1)
    wide = groups * 128
    for r in range(SS):
        at = slice(r * wide, (r + 1) * wide)
        pair = flat_x[:, at].astype(jnp.float32)
        y = (pair[:32] + pair[32:]) * pixel_weight[r : r + 1, :]
        high = y.astype(jnp.bfloat16).astype(jnp.float32)
        flat_y[:, at] = jnp.concatenate([high, y - high], 0).astype(jnp.bfloat16)
    gram = lax.dot_general(
        flat_y[...], flat_x[...], (((1,), (1,)), ((), ())), preferred_element_type=jnp.float32
    )
    gram = widen(gram[:32] + gram[32:])
    out[:32, :] = gram + pltpu.roll(gram, 96, 1)
    total_t = total_of(template_variance[...])
    out[32:, :] = jnp.where(narrow == 0, variance_sum[...], jnp.broadcast_to(total_t, (8, 128)))


def eliminate(a):
    row_index = lax.broadcasted_iota(jnp.int32, (32, 1), 0)
    for k in range(NB):
        pivot_row = a[k : k + 1, :]
        pivot_row = pivot_row / pivot_row[:, k : k + 1]
        column = a[:, k : k + 1] - (row_index == k).astype(jnp.float32)
        a = a - column * pivot_row
    return jnp.where(row_index < NB, a[:, NB : NB + 1], 0.0)


def widen(x):
    return jnp.concatenate([x, jnp.zeros((x.shape[0], 128 - x.shape[1]), jnp.float32)], 1)


def total_of(x):
    return jnp.sum(jnp.sum(x, axis=0, keepdims=True), axis=1, keepdims=True)


def correlate(kernel_t, before, own, after, stack, bands, products, out, science):
    height, columns = own.shape
    reach = height + 2 * MARGIN
    lead = HALO - MARGIN
    tiles = columns // 128 + 1
    high = kernel_t.astype(jnp.bfloat16).astype(jnp.float32)
    low = kernel_t - high
    blank = jnp.zeros_like(high)
    high, low = jnp.concatenate([high, blank], 1), jnp.concatenate([low, blank], 1)
    taps = high + pltpu.roll(high, reach, 1) + pltpu.roll(low, 2 * reach, 1)
    for v in range(KS):
        w, j = v // FINE, v % FINE
        band = jnp.broadcast_to(taps[v : v + 1, :], (height, 256))
        band = pltpu.roll(band, 0, 1, stride=1, stride_axis=0)
        bands[w * height : (w + 1) * height, j * 256 : (j + 1) * 256] = band.astype(jnp.bfloat16)

    lane = lax.broadcasted_iota(jnp.int32, (1, 128), 1)
    rest = jnp.zeros((256 - 3 * reach, 128), jnp.float32)
    empty = jnp.zeros((reach, 128), jnp.float32)

    def tile(t):
        if t % tiles == tiles - 1:
            return empty
        at = slice(t % tiles * 128, (t % tiles + 1) * 128)
        return jnp.concatenate([before[:, at], own[:, at], after[:, at]], 0)[lead : lead + reach]

    left, here = tile(-1), tile(0)
    left_last = pltpu.roll(left, 1, 1)
    here_last = pltpu.roll(here, 1, 1)
    here_next = pltpu.roll(here, 127, 1)
    for t in range(tiles):
        right = tile(t + 1)
        right_last, right_next = pltpu.roll(right, 1, 1), pltpu.roll(right, 127, 1)
        moved = (
            jnp.where(lane < 1, left_last, here_last),
            here,
            jnp.where(lane < 127, here_next, right_next),
        )
        for j, x in enumerate(moved):
            high = x.astype(jnp.bfloat16).astype(jnp.float32)
            stack[j * 256 : (j + 1) * 256, t * 128 : (t + 1) * 128] = jnp.concatenate(
                [high, x - high, high, rest], 0
            ).astype(jnp.bfloat16)
        left_last, here, here_last, here_next = here_last, right, right_last, right_next
    chunk = 384 if tiles % 3 == 0 else 128
    for c in range(0, tiles * 128, chunk):
        at = slice(c, c + chunk)
        products[:, at] = jnp.dot(bands[...], stack[:, at], preferred_element_type=jnp.float32)

    def finish(g, carry):
        at = pl.multiple_of(g * 8, 8)

        def product(w):
            return products[pl.ds(w * height + at, 8), :]

        half = COARSE // 2
        total = product(half)
        for w in range(COARSE):
            if w != half:
                total = total + pltpu.roll(product(w), FINE * (half - w) % (tiles * 128), 1)
        total = total[:, :columns]
        rows = pl.ds(at, 8)
        out[rows, :] = total if science is None else science[rows, :] - total
        return carry

    lax.fori_loop(0, height // 8, finish, 0, unroll=True)


def first_kernel(pixels, p0, p1, p2, p3, science, before, own, after, lv, lu, left, right, back_left,
                 back_right, difference, top, bottom, filter_out, powers, stack, bands, products):
    sums = p0[...] + p1[...] + p2[...] + p3[...]
    coefficients = eliminate(sums[:32, :])
    mean_science = sums[32:33, 0:1] * (1.0 / pixels)
    mean_template = sums[32:33, 1:2] * (1.0 / pixels)
    kernel_t = dot(lv[...], coefficients * lu[...])
    v_index = lax.broadcasted_iota(jnp.int32, (32, 128), 0)
    u_index = lax.broadcasted_iota(jnp.int32, (32, 128), 1)
    kernel_t = kernel_t + ((v_index == MARGIN) & (u_index == MARGIN)).astype(jnp.float32)
    step = dot(left[...], kernel_t)
    both = dot(jnp.concatenate([step[:PD], step[PD:]], 1), right[...])
    re, im = both[:, :128], both[:, 128:]
    response = jnp.sqrt(
        (mean_science + mean_template) / (mean_science + mean_template * (re * re + im * im))
    )
    step = dot(back_left[...], response)
    filter_t = dot(jnp.concatenate([step[:32], step[32:]], 1), back_right[...])
    filter_out[...] = filter_t
    powers[0:1, :] = jnp.broadcast_to(total_of(kernel_t * kernel_t), (1, 128))
    powers[1:2, :] = jnp.broadcast_to(total_of(filter_t * filter_t), (1, 128))
    powers[2:, :] = jnp.zeros((6, 128), jnp.float32)
    correlate(kernel_t, before, own, after, stack, bands, products, difference, science)
    top[...] = difference[:HALO, :]
    bottom[...] = difference[difference.shape[0] - HALO :, :]


def second_kernel(filter_t, before, own, after, out, stack, bands, products):
    correlate(filter_t[...], before, own, after, stack, bands, products, out, None)


def correlation_scratch(height, columns):
    return [
        pltpu.VMEM((FINE * 256, columns + 128), jnp.bfloat16),
        pltpu.VMEM((COARSE * height, FINE * 256), jnp.bfloat16),
        pltpu.VMEM((COARSE * height, columns + 128), jnp.float32),
    ]


def edges(top, bottom, axis):
    devices = lax.axis_size(axis)
    up = [(i, i + 1) for i in range(devices - 1)]
    down = [(j, i) for i, j in up]
    before = lax.ppermute(bottom, axis, up)
    after = lax.ppermute(top, axis, down)
    return before, after


def per_device(science, variance, template_blocks, requests, stamp_rows, stamp_cols):
    height, columns = science.shape
    strips = lax.axis_size("det")
    device = lax.axis_index("det")
    held = template_blocks.shape[0]

    half = strips // 2
    here = device // half
    partner = lax.rem(device + half, strips)
    served = lax.dynamic_slice_in_dim(requests, here * half, half, 0)

    def picks_of(owner):
        local = served - owner * held
        mine = (local >= 0) & (local < held)
        again = mine & jnp.pad(mine[:, :-1], ((0, 0), (1, 0)))
        first = jnp.sum(jnp.where(mine & ~again, local, 0), axis=1)
        second = jnp.sum(jnp.where(again, local, 0), axis=1)
        return jnp.stack([first, second], axis=1).reshape(-1).astype(jnp.int32)

    wanted = lax.dynamic_index_in_dim(requests, device, 0, keepdims=False)
    owner = wanted // held
    repeat = owner == jnp.concatenate([owner[:1] - 1, owner[:-1]])
    slots = (owner % half * 2 + repeat).astype(jnp.int32)
    is_near = (owner // half == here).astype(jnp.int32)

    across_halves = [(i, (i + half) % strips) for i in range(strips)]
    halves = [list(range(half)), list(range(half, strips))]

    def serve(x):
        return lax.all_to_all(x, "det", 0, 0, axis_index_groups=halves, tiled=True)

    partner_blocks = lax.ppermute(template_blocks, "det", across_halves)
    near = serve(pick(picks_of(device), template_blocks))
    far_picks = picks_of(partner)
    partner_blocks, near = lax.optimization_barrier((partner_blocks, near))
    far_image = serve(pick(far_picks, partner_blocks, 0))
    partner_blocks, far_image = lax.optimization_barrier((partner_blocks, far_image))
    far_variance = serve(pick(far_picks, partner_blocks, 1))

    vmem, smem, anywhere = (pl.BlockSpec(memory_space=m) for m in (VMEM, SMEM, pl.ANY))
    rows, cols = stamp_rows[0], stamp_cols[0]
    stamps = rows.shape[0]
    flat = SS * SS * stamps
    strip = jax.ShapeDtypeStruct((height, columns), jnp.float32)
    row = jax.ShapeDtypeStruct((8, 128), jnp.float32)
    edge = jax.ShapeDtypeStruct((HALO, columns), jnp.float32)
    tables = [jnp.asarray(t) for t in (across_table(), down_table(), *dft_blocks())]
    params = pltpu.CompilerParams(vmem_limit_bytes=VMEM_LIMIT)
    small = pltpu.CompilerParams(vmem_limit_bytes=VMEM_SMALL)
    template_image, template_top, template_bottom, flat_x, variance_stamps, stamp_weights, variance_sum = pl.pallas_call(
        image_kernel,
        out_shape=[
            strip,
            edge,
            edge,
            jax.ShapeDtypeStruct((64, flat), jnp.bfloat16),
            jax.ShapeDtypeStruct((stamps // 4 * SS, 128), jnp.float32),
            jax.ShapeDtypeStruct((stamps // 4 * 8, 128), jnp.float32),
            row,
        ],
        in_specs=[smem] * 4 + [anywhere] * 2 + [vmem] * 9,
        out_specs=[vmem] * 7,
        scratch_shapes=[
            pltpu.VMEM((stamps // 4, 32 * SS, 128), jnp.float32),
            pltpu.SemaphoreType.DMA((wanted.shape[0],)),
        ],
        compiler_params=params,
        cost_estimate=pl.CostEstimate(flops=10**10, bytes_accessed=10**7, transcendentals=0),
        name="stamp_images",
    )(rows, cols, slots, is_near, near, far_image, science, variance, *tables)
    before, after = edges(template_top, template_bottom, "det")
    template_variance, partial = pl.pallas_call(
        normal_kernel,
        out_shape=[strip, jax.ShapeDtypeStruct((40, 128), jnp.float32)],
        in_specs=[smem] * 4 + [anywhere] * 2 + [vmem] * 4,
        out_specs=[vmem] * 2,
        scratch_shapes=[
            pltpu.VMEM((64, flat), jnp.bfloat16),
            pltpu.SemaphoreType.DMA((wanted.shape[0],)),
        ],
        compiler_params=small,
        name="normal_equations",
    )(rows, cols, slots, is_near, near, far_variance, flat_x, variance_stamps, stamp_weights, variance_sum)
    partials = [partial]
    for shift in range(1, CPER):
        partials.append(
            lax.ppermute(
                partial,
                "det",
                [(i, i // CPER * CPER + (i + shift) % CPER) for i in range(strips)],
            )
        )
    pixels = CPER * height * columns
    tables = [jnp.asarray(t) for t in (*basis_tables(), *filter_tables())]
    difference, top, bottom, filter_t, powers = pl.pallas_call(
        functools.partial(first_kernel, pixels),
        out_shape=[
            strip,
            edge,
            edge,
            jax.ShapeDtypeStruct((32, 128), jnp.float32),
            row,
        ],
        in_specs=[vmem] * 14,
        out_specs=[vmem] * 5,
        scratch_shapes=correlation_scratch(height, columns),
        compiler_params=small,
        name="solve_and_subtract",
    )(*partials, science, before, template_image, after, *tables)
    before, after = edges(top, bottom, "det")
    decorrelated_variance = powers[1, 0] * (variance + template_variance * powers[0, 0])
    decorrelated = pl.pallas_call(
        second_kernel,
        out_shape=strip,
        in_specs=[vmem] * 4,
        out_specs=vmem,
        scratch_shapes=correlation_scratch(height, columns),
        compiler_params=small,
        name="decorrelate",
    )(filter_t, before, difference, after)
    return (decorrelated, decorrelated_variance)


def solution(mesh):
    placed = (
        P(("group", "det"), None),
        P(("group", "det"), None),
        P(("group", "det"), None, None, None),
        P("group", None),
        P(("group", "det"), None),
        P(("group", "det"), None),
    )
    return jax.shard_map(
        per_device,
        mesh=mesh,
        in_specs=placed,
        out_specs=(P(("group", "det"), None), P(("group", "det"), None)),
        check_vma=False,
    )
```

```python
import functools

import jax
import jax.numpy as jnp
import numpy as np
from jax import lax
from jax.experimental import pallas as pl
from jax.experimental.pallas import tpu as pltpu
from jax.sharding import PartitionSpec as P

CPER = 4
SS = 32
KS = 21
PD = 32
MARGIN = KS // 2
HALO = 16
EXTENT = SS + 2 * MARGIN

HIGHEST = lax.Precision.HIGHEST
GAUSS_WIDTHS = (0.7, 1.5, 3.0)
GAUSS_DEGREES = (4, 2, 2)
VMEM_LIMIT = 60 * 1024 * 1024
VMEM_SMALL = 32 * 1024 * 1024
VMEM = pltpu.MemorySpace.VMEM
SMEM = pltpu.MemorySpace.SMEM


def line_functions():
    tap_grid = np.arange(KS, dtype=np.float64) - MARGIN
    raw_list = []
    for spread, degree in zip(GAUSS_WIDTHS, GAUSS_DEGREES):
        gaussian = np.exp(-tap_grid * tap_grid / (2.0 * spread * spread))
        for degree_power in range(degree + 1):
            raw_list.append(gaussian * tap_grid**degree_power)
    result = []
    for vector in raw_list:
        for earlier in result:
            vector = vector - np.sum(vector * earlier) * earlier
        result.append(vector / np.sqrt(np.sum(vector * vector)))
    return np.stack(result)


def images_by_across():
    groups = []
    base = 0
    for degree in GAUSS_DEGREES:
        for inner in range(degree + 1):
            groups.append((base + inner, [base + outer for outer in range(degree + 1 - inner)]))
        base += degree + 1
    return groups


LINE = line_functions()
GROUPS = images_by_across()
PAIRS = [(a, b) for b, downs in GROUPS for a in downs]
NB = len(PAIRS)
NFUN = LINE.shape[0]
WROWS = 56
TABLES = 7
FINE, COARSE = 3, 7


def block_diag(matrix, times):
    rows, cols = matrix.shape
    out = np.zeros((rows * times, cols * times))
    for k in range(times):
        out[k * rows : (k + 1) * rows, k * cols : (k + 1) * cols] = matrix
    return out


def across_table():
    table = np.zeros((256, NFUN * 128))
    for b in range(NFUN):
        for k in range(4):
            for c in range(SS):
                table[64 * k + c : 64 * k + c + KS, b * 128 + 32 * k + c] = LINE[b]
    return table.astype(np.float32)


def down_table():
    table = np.zeros((NB * SS, WROWS))
    for image, (a, _) in enumerate(PAIRS):
        for r in range(SS):
            table[image * SS + r, r : r + KS] = LINE[a]
    return table.astype(np.float32)


def dft_blocks():
    grid = np.outer(np.arange(SS), np.arange(SS)) % SS
    c, s = np.cos(2 * np.pi * grid / SS), np.sin(2 * np.pi * grid / SS)
    c, s = block_diag(c, 4), block_diag(s, 4)
    ones = block_diag(np.ones((SS, SS)), 4)
    left = np.concatenate([c, s], 0)
    right = np.block([[c, -s], [-s, -c]])
    back_left = np.block([[c, -s], [s, c]])
    back_right = np.concatenate([c, -s], 0) / (SS * SS)
    return [x.astype(np.float32) for x in (left, right, back_left, back_right, ones)]


def basis_tables():
    lv, lu = np.zeros((32, 32)), np.zeros((32, 128))
    for image, (a, b) in enumerate(PAIRS):
        lv[:KS, image] = LINE[b]
        lu[image, :KS] = LINE[a]
    return lv.astype(np.float32), lu.astype(np.float32)


def filter_tables():
    grid = np.outer(np.arange(PD), np.arange(KS) - MARGIN)
    c, s = np.zeros((PD, 32)), np.zeros((PD, 32))
    c[:, :KS], s[:, :KS] = np.cos(2 * np.pi * grid / PD), np.sin(2 * np.pi * grid / PD)
    cr, sr = np.zeros((128, 128)), np.zeros((128, 128))
    cr[:32, :PD], sr[:32, :PD] = c.T, s.T
    left = np.concatenate([c, s], 0)
    right = np.block([[cr, -sr], [-sr, -cr]])
    back_left = np.concatenate([c.T, s.T], 0) / (PD * PD)
    back_c, back_s = np.zeros((128, 128)), np.zeros((128, 128))
    back_c[:PD, :32], back_s[:PD, :32] = c, s
    back_right = np.concatenate([back_c, -back_s], 0)
    return [x.astype(np.float32) for x in (left, right, back_left, back_right)]


def pick_kernel(plane, picks, source, out, sem):
    count = out.shape[0]

    def copy(k):
        block = source.at[picks[k]] if plane is None else source.at[picks[k], plane]
        return pltpu.make_async_copy(block, out.at[k], sem.at[k])

    def start(k, carry):
        copy(k).start()
        return carry

    def finish(k, carry):
        copy(k).wait()
        return carry

    lax.fori_loop(0, count, start, 0)
    lax.fori_loop(0, count, finish, 0)


def pick(picks, source, plane=None):
    count = picks.shape[0]
    shape = source.shape[1:] if plane is None else source.shape[2:]
    return pl.pallas_call(
        functools.partial(pick_kernel, plane),
        out_shape=jax.ShapeDtypeStruct((count,) + shape, source.dtype),
        in_specs=[pl.BlockSpec(memory_space=SMEM), pl.BlockSpec(memory_space=VMEM)],
        out_specs=pl.BlockSpec(memory_space=pl.ANY),
        scratch_shapes=[pltpu.SemaphoreType.DMA((count,))],
        compiler_params=pltpu.CompilerParams(vmem_limit_bytes=VMEM_LIMIT),
        name="pick_blocks",
    )(picks, source)


def lay_strip(slots, is_near, near, far, plane, out, sem):
    needed = slots.shape[0]
    width = near.shape[3]
    for j in range(needed):
        columns = pl.ds(j * width, width)

        @pl.when(is_near[j] == 1)
        def _():
            pltpu.make_async_copy(near.at[slots[j], plane], out.at[:, columns], sem.at[j]).start()

        @pl.when(is_near[j] == 0)
        def _():
            pltpu.make_async_copy(far.at[slots[j]], out.at[:, columns], sem.at[j]).start()

    for j in range(needed):
        columns = pl.ds(j * width, width)
        pltpu.make_async_copy(far.at[slots[j]], out.at[:, columns], sem.at[j]).wait()


def dot(a, b, contract=((1,), (0,))):
    return lax.dot_general(
        a, b, (contract, ((), ())), precision=HIGHEST, preferred_element_type=jnp.float32
    )


def split(x):
    high = x.astype(jnp.bfloat16)
    return high, (x - high.astype(jnp.float32)).astype(jnp.bfloat16)


def stamp_place(stamp_rows, stamp_cols, stamp, columns):
    row = stamp_rows[stamp] - (SS // 2 + MARGIN)
    col = stamp_cols[stamp] - (SS // 2 + MARGIN)
    base = pl.multiple_of(jnp.minimum(col // 128 * 128, columns - 256), 128)
    return row, col - base, pl.ds(base, 256)


def inner_stamp(x, row, off, k):
    moved = pltpu.roll(x, lax.rem(32 * k - off - MARGIN + 512, 256), 1)[:, :128]
    return pltpu.roll(moved, x.shape[0] - row - MARGIN, 0)[:SS]


def science_kernel(stamp_rows, stamp_cols, science, variance, science_stamps, variance_stamps, variance_sum):
    _, columns = science.shape
    narrow = lax.broadcasted_iota(jnp.int32, (1, 128), 1)
    for g in range(stamp_rows.shape[0] // 4):
        sci = var = None
        for k in range(4):
            row, off, cols = stamp_place(stamp_rows, stamp_cols, g * 4 + k, columns)
            s = inner_stamp(science[:, cols], row, off, k)
            v = inner_stamp(variance[:, cols], row, off, k)
            here = narrow // 32 == k
            sci, var = (s, v) if k == 0 else (jnp.where(here, s, sci), jnp.where(here, v, var))
        science_stamps[g * SS : (g + 1) * SS, :] = sci
        variance_stamps[g * SS : (g + 1) * SS, :] = var
    variance_sum[...] = jnp.broadcast_to(total_of(variance[...]), (8, 128))


def image_kernel(stamp_rows, stamp_cols, slots, is_near, near, far, science_stamps, *refs):
    tables_in, refs = refs[:TABLES], refs[TABLES:]
    template, top, bottom, flat_x, stamp_weights, images, sem, table_sem = refs[:8]
    tables = refs[8:]
    loads = [
        pltpu.make_async_copy(source, table, table_sem.at[i])
        for i, (source, table) in enumerate(zip(tables_in, tables))
    ]
    for load in loads:
        load.start()
    across_ref, down_ref, left_ref, right_ref, back_left_ref, back_right_ref, ones_ref = tables
    lay_strip(slots, is_near, near, far, 0, template, sem)
    height, columns = template.shape
    top[...] = template[:HALO, :]
    bottom[...] = template[height - HALO :, :]
    stamps = stamp_rows.shape[0]
    groups = stamps // 4
    lane = lax.broadcasted_iota(jnp.int32, (1, 256), 1)

    windows, sciences, templates = [], [], []
    for g in range(groups):
        window = tmp = None
        for k in range(4):
            row, off, cols = stamp_place(stamp_rows, stamp_cols, g * 4 + k, columns)
            t = template[:, cols]
            to64 = lax.rem(64 * k - off + 256, 256)
            tw = pltpu.roll(pltpu.roll(t, to64, 1), lax.rem(height - row, height), 0)[:WROWS]
            t = inner_stamp(t, row, off, k)
            if k == 0:
                window, tmp = tw, t
            else:
                window = jnp.where(lane // 64 == k, tw, window)
                tmp = jnp.where(lane[:, :128] // 32 == k, t, tmp)
        windows.append(window)
        templates.append(tmp)
        sciences.append(science_stamps[g * SS : (g + 1) * SS, :])
    for load in loads:
        load.wait()

    across = dot(jnp.concatenate(windows, 0), across_ref[...])
    row = 0
    for b, downs in GROUPS:
        piece = jnp.concatenate(
            [across[g * WROWS : (g + 1) * WROWS, b * 128 : (b + 1) * 128] for g in range(groups)], 1
        )
        count = len(downs) * SS
        made = dot(down_ref[row : row + count, :], piece)
        for g in range(groups):
            images[g, row : row + count, :] = made[:, g * 128 : (g + 1) * 128]
        row += count
    for g in range(groups):
        images[g, NB * SS : (NB + 1) * SS, :] = sciences[g] - templates[g]
        images[g, (NB + 1) * SS :, :] = jnp.zeros(((31 - NB) * SS, 128), jnp.float32)
    wide = groups * 128
    for r in range(SS):
        x = jnp.concatenate([images[g, pl.ds(r, 32, stride=SS), :] for g in range(groups)], 1)
        high = x.astype(jnp.bfloat16).astype(jnp.float32)
        pair = jnp.concatenate([high, x - high], 0).astype(jnp.bfloat16)
        flat_x[:, r * wide : (r + 1) * wide] = pair

    sci = jnp.concatenate(sciences, 0)
    tmp = jnp.concatenate(templates, 0)
    side = groups * SS
    first = dot(left_ref[...], jnp.concatenate([sci, tmp], 1))
    first = jnp.concatenate(
        [
            jnp.concatenate([first[:side, :128], first[side:, :128]], 1),
            jnp.concatenate([first[:side, 128:], first[side:, 128:]], 1),
        ],
        0,
    )
    second = dot(first, right_ref[...])
    sre, sim = second[:side, :128], second[:side, 128:]
    tre, tim = second[side:, :128], second[side:, 128:]
    cross_re = sre * tre + sim * tim
    cross_im = sim * tre - sre * tim
    magnitude = jnp.sqrt(cross_re * cross_re + cross_im * cross_im)
    mean = dot(dot(ones_ref[...], magnitude), ones_ref[...]) * (1.0 / (SS * SS))
    scaling = 1.0 / jnp.maximum(magnitude, 0.25 * (mean + 1e-06))
    unit = jnp.concatenate([cross_re * scaling, cross_im * scaling], 0)
    back = dot(back_left_ref[...], unit)
    surface = dot(jnp.concatenate([back[:side], back[side:]], 1), back_right_ref[...])
    narrow = lane[:, :128]
    for g in range(groups):
        best = jnp.max(surface[g * SS : (g + 1) * SS], axis=0, keepdims=True)
        best = jnp.broadcast_to(best, (8, 128))
        for step in (1, 2, 4, 8, 16):
            partner = jnp.where(
                narrow // step % 2 == 0,
                pltpu.roll(best, 128 - step, 1),
                pltpu.roll(best, step, 1),
            )
            best = jnp.maximum(best, partner)
        stamp_weights[g * 8 : (g + 1) * 8, :] = jnp.maximum(best, 0.1)


def normal_kernel(stamp_rows, stamp_cols, slots, is_near, near, far, flat_x, variance_stamps,
                  stamp_weights, variance_sum, template_variance, out, flat_y, sem):
    lay_strip(slots, is_near, near, far, 1, template_variance, sem)
    _, columns = template_variance.shape
    stamps = stamp_rows.shape[0]
    groups = stamps // 4
    narrow = lax.broadcasted_iota(jnp.int32, (1, 128), 1)
    pixel_weight = []
    for g in range(groups):
        weight = None
        for k in range(4):
            row, off, cols = stamp_place(stamp_rows, stamp_cols, g * 4 + k, columns)
            w = inner_stamp(template_variance[:, cols], row, off, k)
            weight = w if k == 0 else jnp.where(narrow // 32 == k, w, weight)
        weight = variance_stamps[g * SS : (g + 1) * SS, :] + weight
        pixel_weight.append(stamp_weights[g * 8 : g * 8 + 1, :] / weight)
    pixel_weight = jnp.concatenate(pixel_weight, 1)
    wide = groups * 128
    for r in range(SS):
        at = slice(r * wide, (r + 1) * wide)
        pair = flat_x[:, at].astype(jnp.float32)
        y = (pair[:32] + pair[32:]) * pixel_weight[r : r + 1, :]
        high = y.astype(jnp.bfloat16).astype(jnp.float32)
        flat_y[:, at] = jnp.concatenate([high, y - high], 0).astype(jnp.bfloat16)
    gram = lax.dot_general(
        flat_y[...], flat_x[...], (((1,), (1,)), ((), ())), preferred_element_type=jnp.float32
    )
    gram = widen(gram[:32] + gram[32:])
    out[:32, :] = gram + pltpu.roll(gram, 96, 1)
    total_t = total_of(template_variance[...])
    out[32:, :] = jnp.where(narrow == 0, variance_sum[...], jnp.broadcast_to(total_t, (8, 128)))


def eliminate(a):
    row_index = lax.broadcasted_iota(jnp.int32, (32, 1), 0)
    for k in range(NB):
        pivot_row = a[k : k + 1, :]
        pivot_row = pivot_row / pivot_row[:, k : k + 1]
        column = a[:, k : k + 1] - (row_index == k).astype(jnp.float32)
        a = a - column * pivot_row
    return jnp.where(row_index < NB, a[:, NB : NB + 1], 0.0)


def widen(x):
    return jnp.concatenate([x, jnp.zeros((x.shape[0], 128 - x.shape[1]), jnp.float32)], 1)


def total_of(x):
    return jnp.sum(jnp.sum(x, axis=0, keepdims=True), axis=1, keepdims=True)


def correlate(kernel_t, before, own, after, stack, bands, products, out, science):
    height, columns = own.shape
    reach = height + 2 * MARGIN
    lead = HALO - MARGIN
    tiles = columns // 128 + 1
    high = kernel_t.astype(jnp.bfloat16).astype(jnp.float32)
    low = kernel_t - high
    blank = jnp.zeros_like(high)
    high, low = jnp.concatenate([high, blank], 1), jnp.concatenate([low, blank], 1)
    taps = high + pltpu.roll(high, reach, 1) + pltpu.roll(low, 2 * reach, 1)
    for v in range(KS):
        w, j = v // FINE, v % FINE
        band = jnp.broadcast_to(taps[v : v + 1, :], (height, 256))
        band = pltpu.roll(band, 0, 1, stride=1, stride_axis=0)
        bands[w * height : (w + 1) * height, j * 256 : (j + 1) * 256] = band.astype(jnp.bfloat16)

    lane = lax.broadcasted_iota(jnp.int32, (1, 128), 1)
    rest = jnp.zeros((256 - 3 * reach, 128), jnp.float32)
    empty = jnp.zeros((reach, 128), jnp.float32)

    def tile(t):
        if t % tiles == tiles - 1:
            return empty
        at = slice(t % tiles * 128, (t % tiles + 1) * 128)
        return jnp.concatenate([before[:, at], own[:, at], after[:, at]], 0)[lead : lead + reach]

    left, here = tile(-1), tile(0)
    left_last = pltpu.roll(left, 1, 1)
    here_last = pltpu.roll(here, 1, 1)
    here_next = pltpu.roll(here, 127, 1)
    for t in range(tiles):
        right = tile(t + 1)
        right_last, right_next = pltpu.roll(right, 1, 1), pltpu.roll(right, 127, 1)
        moved = (
            jnp.where(lane < 1, left_last, here_last),
            here,
            jnp.where(lane < 127, here_next, right_next),
        )
        for j, x in enumerate(moved):
            high = x.astype(jnp.bfloat16).astype(jnp.float32)
            stack[j * 256 : (j + 1) * 256, t * 128 : (t + 1) * 128] = jnp.concatenate(
                [high, x - high, high, rest], 0
            ).astype(jnp.bfloat16)
        left_last, here, here_last, here_next = here_last, right, right_last, right_next
    chunk = 384 if tiles % 3 == 0 else 128
    for c in range(0, tiles * 128, chunk):
        at = slice(c, c + chunk)
        products[:, at] = jnp.dot(bands[...], stack[:, at], preferred_element_type=jnp.float32)

    def finish(g, carry):
        at = pl.multiple_of(g * 8, 8)

        def product(w):
            return products[pl.ds(w * height + at, 8), :]

        half = COARSE // 2
        total = product(half)
        for w in range(COARSE):
            if w != half:
                total = total + pltpu.roll(product(w), FINE * (half - w) % (tiles * 128), 1)
        total = total[:, :columns]
        rows = pl.ds(at, 8)
        out[rows, :] = total if science is None else science[rows, :] - total
        return carry

    lax.fori_loop(0, height // 8, finish, 0, unroll=True)


def first_kernel(pixels, p0, p1, p2, p3, science, before, own, after, lv, lu, left, right, back_left,
                 back_right, difference, top, bottom, filter_out, powers, stack, bands, products):
    sums = p0[...] + p1[...] + p2[...] + p3[...]
    coefficients = eliminate(sums[:32, :])
    mean_science = sums[32:33, 0:1] * (1.0 / pixels)
    mean_template = sums[32:33, 1:2] * (1.0 / pixels)
    kernel_t = dot(lv[...], coefficients * lu[...])
    v_index = lax.broadcasted_iota(jnp.int32, (32, 128), 0)
    u_index = lax.broadcasted_iota(jnp.int32, (32, 128), 1)
    kernel_t = kernel_t + ((v_index == MARGIN) & (u_index == MARGIN)).astype(jnp.float32)
    step = dot(left[...], kernel_t)
    both = dot(jnp.concatenate([step[:PD], step[PD:]], 1), right[...])
    re, im = both[:, :128], both[:, 128:]
    response = jnp.sqrt(
        (mean_science + mean_template) / (mean_science + mean_template * (re * re + im * im))
    )
    step = dot(back_left[...], response)
    filter_t = dot(jnp.concatenate([step[:32], step[32:]], 1), back_right[...])
    filter_out[...] = filter_t
    powers[0:1, :] = jnp.broadcast_to(total_of(kernel_t * kernel_t), (1, 128))
    powers[1:2, :] = jnp.broadcast_to(total_of(filter_t * filter_t), (1, 128))
    powers[2:, :] = jnp.zeros((6, 128), jnp.float32)
    correlate(kernel_t, before, own, after, stack, bands, products, difference, science)
    top[...] = difference[:HALO, :]
    bottom[...] = difference[difference.shape[0] - HALO :, :]


def second_kernel(filter_t, before, own, after, out, stack, bands, products):
    correlate(filter_t[...], before, own, after, stack, bands, products, out, None)


def correlation_scratch(height, columns):
    return [
        pltpu.VMEM((FINE * 256, columns + 128), jnp.bfloat16),
        pltpu.VMEM((COARSE * height, FINE * 256), jnp.bfloat16),
        pltpu.VMEM((COARSE * height, columns + 128), jnp.float32),
    ]


def edges(top, bottom, axis):
    devices = lax.axis_size(axis)
    up = [(i, i + 1) for i in range(devices - 1)]
    down = [(j, i) for i, j in up]
    before = lax.ppermute(bottom, axis, up)
    after = lax.ppermute(top, axis, down)
    return before, after


def per_device(science, variance, template_blocks, requests, stamp_rows, stamp_cols):
    height, columns = science.shape
    strips = lax.axis_size("det")
    device = lax.axis_index("det")
    held = template_blocks.shape[0]

    half = strips // 2
    here = device // half
    partner = lax.rem(device + half, strips)
    served = lax.dynamic_slice_in_dim(requests, here * half, half, 0)

    def picks_of(owner):
        local = served - owner * held
        mine = (local >= 0) & (local < held)
        again = mine & jnp.pad(mine[:, :-1], ((0, 0), (1, 0)))
        first = jnp.sum(jnp.where(mine & ~again, local, 0), axis=1)
        second = jnp.sum(jnp.where(again, local, 0), axis=1)
        return jnp.stack([first, second], axis=1).reshape(-1).astype(jnp.int32)

    wanted = lax.dynamic_index_in_dim(requests, device, 0, keepdims=False)
    owner = wanted // held
    repeat = owner == jnp.concatenate([owner[:1] - 1, owner[:-1]])
    slots = (owner % half * 2 + repeat).astype(jnp.int32)
    is_near = (owner // half == here).astype(jnp.int32)

    across_halves = [(i, (i + half) % strips) for i in range(strips)]
    halves = [list(range(half)), list(range(half, strips))]

    def serve(x):
        return lax.all_to_all(x, "det", 0, 0, axis_index_groups=halves, tiled=True)

    partner_blocks = lax.ppermute(template_blocks, "det", across_halves)
    near = serve(pick(picks_of(device), template_blocks))
    far_picks = picks_of(partner)
    vmem, smem, anywhere = (pl.BlockSpec(memory_space=m) for m in (VMEM, SMEM, pl.ANY))
    rows, cols = stamp_rows[0], stamp_cols[0]
    stamps = rows.shape[0]
    flat = SS * SS * stamps
    strip = jax.ShapeDtypeStruct((height, columns), jnp.float32)
    row = jax.ShapeDtypeStruct((8, 128), jnp.float32)
    edge = jax.ShapeDtypeStruct((HALO, columns), jnp.float32)
    tables = [jnp.asarray(t) for t in (across_table(), down_table(), *dft_blocks())]
    params = pltpu.CompilerParams(vmem_limit_bytes=VMEM_LIMIT)
    small = pltpu.CompilerParams(vmem_limit_bytes=VMEM_SMALL)
    stamp_rows_shape = jax.ShapeDtypeStruct((stamps // 4 * SS, 128), jnp.float32)
    science_stamps, variance_stamps, variance_sum = pl.pallas_call(
        science_kernel,
        out_shape=[stamp_rows_shape, stamp_rows_shape, row],
        in_specs=[smem] * 2 + [vmem] * 2,
        out_specs=[vmem] * 3,
        compiler_params=params,
        name="science_stamps",
    )(rows, cols, science, variance)
    partner_blocks, near, slots, is_near, science_stamps, variance_stamps, variance_sum = (
        lax.optimization_barrier(
            (partner_blocks, near, slots, is_near, science_stamps, variance_stamps, variance_sum)
        )
    )
    far_image = serve(pick(far_picks, partner_blocks, 0))
    partner_blocks, far_image = lax.optimization_barrier((partner_blocks, far_image))
    far_variance = serve(pick(far_picks, partner_blocks, 1))

    template_image, template_top, template_bottom, flat_x, stamp_weights = pl.pallas_call(
        image_kernel,
        out_shape=[
            strip,
            edge,
            edge,
            jax.ShapeDtypeStruct((64, flat), jnp.bfloat16),
            jax.ShapeDtypeStruct((stamps // 4 * 8, 128), jnp.float32),
        ],
        in_specs=[smem] * 4 + [anywhere] * 2 + [vmem] + [anywhere] * TABLES,
        out_specs=[vmem] * 5,
        scratch_shapes=[
            pltpu.VMEM((stamps // 4, 32 * SS, 128), jnp.float32),
            pltpu.SemaphoreType.DMA((wanted.shape[0],)),
            pltpu.SemaphoreType.DMA((TABLES,)),
            *[pltpu.VMEM(t.shape, t.dtype) for t in tables],
        ],
        compiler_params=params,
        name="stamp_images",
    )(rows, cols, slots, is_near, near, far_image, science_stamps, *tables)
    before, after = edges(template_top, template_bottom, "det")
    template_variance, partial = pl.pallas_call(
        normal_kernel,
        out_shape=[strip, jax.ShapeDtypeStruct((40, 128), jnp.float32)],
        in_specs=[smem] * 4 + [anywhere] * 2 + [vmem] * 4,
        out_specs=[vmem] * 2,
        scratch_shapes=[
            pltpu.VMEM((64, flat), jnp.bfloat16),
            pltpu.SemaphoreType.DMA((wanted.shape[0],)),
        ],
        compiler_params=small,
        name="normal_equations",
    )(rows, cols, slots, is_near, near, far_variance, flat_x, variance_stamps, stamp_weights, variance_sum)
    partials = [partial]
    for shift in range(1, CPER):
        partials.append(
            lax.ppermute(
                partial,
                "det",
                [(i, i // CPER * CPER + (i + shift) % CPER) for i in range(strips)],
            )
        )
    pixels = CPER * height * columns
    tables = [jnp.asarray(t) for t in (*basis_tables(), *filter_tables())]
    difference, top, bottom, filter_t, powers = pl.pallas_call(
        functools.partial(first_kernel, pixels),
        out_shape=[
            strip,
            edge,
            edge,
            jax.ShapeDtypeStruct((32, 128), jnp.float32),
            row,
        ],
        in_specs=[vmem] * 14,
        out_specs=[vmem] * 5,
        scratch_shapes=correlation_scratch(height, columns),
        compiler_params=small,
        name="solve_and_subtract",
    )(*partials, science, before, template_image, after, *tables)
    before, after = edges(top, bottom, "det")
    decorrelated_variance = powers[1, 0] * (variance + template_variance * powers[0, 0])
    decorrelated = pl.pallas_call(
        second_kernel,
        out_shape=strip,
        in_specs=[vmem] * 4,
        out_specs=vmem,
        scratch_shapes=correlation_scratch(height, columns),
        compiler_params=small,
        name="decorrelate",
    )(filter_t, before, difference, after)
    return (decorrelated, decorrelated_variance)


def solution(mesh):
    placed = (
        P(("group", "det"), None),
        P(("group", "det"), None),
        P(("group", "det"), None, None, None),
        P("group", None),
        P(("group", "det"), None),
        P(("group", "det"), None),
    )
    return jax.shard_map(
        per_device,
        mesh=mesh,
        in_specs=placed,
        out_specs=(P(("group", "det"), None), P(("group", "det"), None)),
        check_vma=False,
    )
```

```python
import functools

import jax
import jax.numpy as jnp
import numpy as np
from jax import lax
from jax.experimental import pallas as pl
from jax.experimental.pallas import tpu as pltpu
from jax.sharding import PartitionSpec as P

CPER = 4
SS = 32
KS = 21
PD = 32
MARGIN = KS // 2
HALO = 16
EXTENT = SS + 2 * MARGIN

HIGHEST = lax.Precision.HIGHEST
GAUSS_WIDTHS = (0.7, 1.5, 3.0)
GAUSS_DEGREES = (4, 2, 2)
VMEM_LIMIT = 60 * 1024 * 1024
VMEM_SMALL = 32 * 1024 * 1024
VMEM = pltpu.MemorySpace.VMEM
SMEM = pltpu.MemorySpace.SMEM


def line_functions():
    tap_grid = np.arange(KS, dtype=np.float64) - MARGIN
    raw_list = []
    for spread, degree in zip(GAUSS_WIDTHS, GAUSS_DEGREES):
        gaussian = np.exp(-tap_grid * tap_grid / (2.0 * spread * spread))
        for degree_power in range(degree + 1):
            raw_list.append(gaussian * tap_grid**degree_power)
    result = []
    for vector in raw_list:
        for earlier in result:
            vector = vector - np.sum(vector * earlier) * earlier
        result.append(vector / np.sqrt(np.sum(vector * vector)))
    return np.stack(result)


def images_by_across():
    groups = []
    base = 0
    for degree in GAUSS_DEGREES:
        for inner in range(degree + 1):
            groups.append((base + inner, [base + outer for outer in range(degree + 1 - inner)]))
        base += degree + 1
    return groups


LINE = line_functions()
GROUPS = images_by_across()
PAIRS = [(a, b) for b, downs in GROUPS for a in downs]
NB = len(PAIRS)
NFUN = LINE.shape[0]
WROWS = 64
TABLES = 7
FINE, COARSE = 3, 7


def block_diag(matrix, times):
    rows, cols = matrix.shape
    out = np.zeros((rows * times, cols * times))
    for k in range(times):
        out[k * rows : (k + 1) * rows, k * cols : (k + 1) * cols] = matrix
    return out


def across_table():
    table = np.zeros((256, NFUN * 128))
    for b in range(NFUN):
        for k in range(4):
            for c in range(SS):
                table[64 * k + c : 64 * k + c + KS, b * 128 + 32 * k + c] = LINE[b]
    return np.concatenate(split_host(table), 1)


def split_host(table):
    high = table.astype(np.float32).astype(jnp.bfloat16)
    return high, (table - high.astype(np.float64)).astype(np.float32).astype(jnp.bfloat16)


def down_table():
    table = np.zeros((NB * SS, WROWS))
    for image, (a, _) in enumerate(PAIRS):
        for r in range(SS):
            table[image * SS + r, r : r + KS] = LINE[a]
    high, low = split_host(table)
    return np.concatenate([high, high, low], 1)


def dft_blocks():
    grid = np.outer(np.arange(SS), np.arange(SS)) % SS
    c, s = np.cos(2 * np.pi * grid / SS), np.sin(2 * np.pi * grid / SS)
    c, s = block_diag(c, 4), block_diag(s, 4)
    ones = block_diag(np.ones((SS, SS)), 4)
    left = np.concatenate([c, s], 0)
    right = np.block([[c, -s], [-s, -c]])
    back_left = np.block([[c, -s], [s, c]])
    back_right = np.concatenate([c, -s], 0) / (SS * SS)
    return [x.astype(np.float32) for x in (left, right, back_left, back_right, ones)]


def basis_tables():
    lv, lu = np.zeros((32, 32)), np.zeros((32, 128))
    for image, (a, b) in enumerate(PAIRS):
        lv[:KS, image] = LINE[b]
        lu[image, :KS] = LINE[a]
    return lv.astype(np.float32), lu.astype(np.float32)


def filter_tables():
    grid = np.outer(np.arange(PD), np.arange(KS) - MARGIN)
    c, s = np.zeros((PD, 32)), np.zeros((PD, 32))
    c[:, :KS], s[:, :KS] = np.cos(2 * np.pi * grid / PD), np.sin(2 * np.pi * grid / PD)
    cr, sr = np.zeros((128, 128)), np.zeros((128, 128))
    cr[:32, :PD], sr[:32, :PD] = c.T, s.T
    left = np.concatenate([c, s], 0)
    right = np.block([[cr, -sr], [-sr, -cr]])
    back_left = np.concatenate([c.T, s.T], 0) / (PD * PD)
    back_c, back_s = np.zeros((128, 128)), np.zeros((128, 128))
    back_c[:PD, :32], back_s[:PD, :32] = c, s
    back_right = np.concatenate([back_c, -back_s], 0)
    return [x.astype(np.float32) for x in (left, right, back_left, back_right)]


def pick_kernel(plane, picks, source, out, sem):
    count = out.shape[0]

    def copy(k):
        block = source.at[picks[k]] if plane is None else source.at[picks[k], plane]
        return pltpu.make_async_copy(block, out.at[k], sem.at[k])

    def start(k, carry):
        copy(k).start()
        return carry

    def finish(k, carry):
        copy(k).wait()
        return carry

    lax.fori_loop(0, count, start, 0)
    lax.fori_loop(0, count, finish, 0)


def pick(picks, source, plane=None):
    count = picks.shape[0]
    shape = source.shape[1:] if plane is None else source.shape[2:]
    return pl.pallas_call(
        functools.partial(pick_kernel, plane),
        out_shape=jax.ShapeDtypeStruct((count,) + shape, source.dtype),
        in_specs=[pl.BlockSpec(memory_space=SMEM), pl.BlockSpec(memory_space=VMEM)],
        out_specs=pl.BlockSpec(memory_space=pl.ANY),
        scratch_shapes=[pltpu.SemaphoreType.DMA((count,))],
        compiler_params=pltpu.CompilerParams(vmem_limit_bytes=VMEM_LIMIT),
        name="pick_blocks",
    )(picks, source)


def lay_strip(slots, is_near, near, far, plane, out, sem):
    needed = slots.shape[0]
    width = near.shape[3]
    for j in range(needed):
        columns = pl.ds(j * width, width)

        @pl.when(is_near[j] == 1)
        def _():
            pltpu.make_async_copy(near.at[slots[j], plane], out.at[:, columns], sem.at[j]).start()

        @pl.when(is_near[j] == 0)
        def _():
            pltpu.make_async_copy(far.at[slots[j]], out.at[:, columns], sem.at[j]).start()

    for j in range(needed):
        columns = pl.ds(j * width, width)
        pltpu.make_async_copy(far.at[slots[j]], out.at[:, columns], sem.at[j]).wait()


def dot(a, b, contract=((1,), (0,))):
    return lax.dot_general(
        a, b, (contract, ((), ())), precision=HIGHEST, preferred_element_type=jnp.float32
    )


def dot16(a, b):
    return jnp.dot(a, b, preferred_element_type=jnp.float32)


def split(x):
    high = x.astype(jnp.bfloat16)
    return high, (x - high.astype(jnp.float32)).astype(jnp.bfloat16)


def stamp_place(stamp_rows, stamp_cols, stamp, columns):
    row = stamp_rows[stamp] - (SS // 2 + MARGIN)
    col = stamp_cols[stamp] - (SS // 2 + MARGIN)
    base = pl.multiple_of(jnp.minimum(col // 128 * 128, columns - 256), 128)
    return row, col - base, pl.ds(base, 256)


def inner_stamp(x, row, off, k):
    moved = pltpu.roll(x, lax.rem(32 * k - off - MARGIN + 512, 256), 1)[:, :128]
    return pltpu.roll(moved, x.shape[0] - row - MARGIN, 0)[:SS]


def science_kernel(stamp_rows, stamp_cols, science, variance, science_stamps, variance_stamps, variance_sum):
    _, columns = science.shape
    narrow = lax.broadcasted_iota(jnp.int32, (1, 128), 1)
    for g in range(stamp_rows.shape[0] // 4):
        sci = var = None
        for k in range(4):
            row, off, cols = stamp_place(stamp_rows, stamp_cols, g * 4 + k, columns)
            s = inner_stamp(science[:, cols], row, off, k)
            v = inner_stamp(variance[:, cols], row, off, k)
            here = narrow // 32 == k
            sci, var = (s, v) if k == 0 else (jnp.where(here, s, sci), jnp.where(here, v, var))
        science_stamps[g * SS : (g + 1) * SS, :] = sci
        variance_stamps[g * SS : (g + 1) * SS, :] = var
    variance_sum[...] = jnp.broadcast_to(total_of(variance[...]), (8, 128))


def image_kernel(stamp_rows, stamp_cols, slots, is_near, near, far, science_stamps, *refs):
    tables_in, refs = refs[:TABLES], refs[TABLES:]
    template, top, bottom, flat_x, stamp_weights, images, sem, table_sem = refs[:8]
    tables = refs[8:]
    loads = [
        pltpu.make_async_copy(source, table, table_sem.at[i])
        for i, (source, table) in enumerate(zip(tables_in, tables))
    ]
    for load in loads:
        load.start()
    across_ref, down_ref, left_ref, right_ref, back_left_ref, back_right_ref, ones_ref = tables
    lay_strip(slots, is_near, near, far, 0, template, sem)
    height, columns = template.shape
    top[...] = template[:HALO, :]
    bottom[...] = template[height - HALO :, :]
    stamps = stamp_rows.shape[0]
    groups = stamps // 4
    lane = lax.broadcasted_iota(jnp.int32, (1, 256), 1)

    windows, sciences, templates = [], [], []
    for g in range(groups):
        window = tmp = None
        for k in range(4):
            row, off, cols = stamp_place(stamp_rows, stamp_cols, g * 4 + k, columns)
            t = template[:, cols]
            to64 = lax.rem(64 * k - off + 256, 256)
            tw = pltpu.roll(pltpu.roll(t, to64, 1), lax.rem(height - row, height), 0)[:WROWS]
            t = inner_stamp(t, row, off, k)
            if k == 0:
                window, tmp = tw, t
            else:
                window = jnp.where(lane // 64 == k, tw, window)
                tmp = jnp.where(lane[:, :128] // 32 == k, t, tmp)
        windows.append(window)
        templates.append(tmp)
        sciences.append(science_stamps[g * SS : (g + 1) * SS, :])
    for load in loads:
        load.wait()

    high, low = split(jnp.concatenate(windows, 0))
    table_high, table_low = across_ref[:, : NFUN * 128], across_ref[:, NFUN * 128 :]
    across = dot16(high, table_high) + (dot16(low, table_high) + dot16(high, table_low))
    row = 0
    for b, downs in GROUPS:
        piece = jnp.concatenate(
            [across[g * WROWS : (g + 1) * WROWS, b * 128 : (b + 1) * 128] for g in range(groups)], 1
        )
        count = len(downs) * SS
        high = piece.astype(jnp.bfloat16).astype(jnp.float32)
        stacked = jnp.concatenate([high, piece - high, high], 0).astype(jnp.bfloat16)
        made = dot16(down_ref[row : row + count, :], stacked)
        for g in range(groups):
            images[g, row : row + count, :] = made[:, g * 128 : (g + 1) * 128]
        row += count
    for g in range(groups):
        images[g, NB * SS : (NB + 1) * SS, :] = sciences[g] - templates[g]
        images[g, (NB + 1) * SS :, :] = jnp.zeros(((31 - NB) * SS, 128), jnp.float32)
    wide = groups * 128
    for r in range(SS):
        x = jnp.concatenate([images[g, pl.ds(r, 32, stride=SS), :] for g in range(groups)], 1)
        high = x.astype(jnp.bfloat16).astype(jnp.float32)
        pair = jnp.concatenate([high, x - high], 0).astype(jnp.bfloat16)
        flat_x[:, r * wide : (r + 1) * wide] = pair

    sci = jnp.concatenate(sciences, 0)
    tmp = jnp.concatenate(templates, 0)
    side = groups * SS
    first = dot(left_ref[...], jnp.concatenate([sci, tmp], 1))
    first = jnp.concatenate(
        [
            jnp.concatenate([first[:side, :128], first[side:, :128]], 1),
            jnp.concatenate([first[:side, 128:], first[side:, 128:]], 1),
        ],
        0,
    )
    second = dot(first, right_ref[...])
    sre, sim = second[:side, :128], second[:side, 128:]
    tre, tim = second[side:, :128], second[side:, 128:]
    cross_re = sre * tre + sim * tim
    cross_im = sim * tre - sre * tim
    magnitude = jnp.sqrt(cross_re * cross_re + cross_im * cross_im)
    mean = dot(dot(ones_ref[...], magnitude), ones_ref[...]) * (1.0 / (SS * SS))
    scaling = 1.0 / jnp.maximum(magnitude, 0.25 * (mean + 1e-06))
    unit = jnp.concatenate([cross_re * scaling, cross_im * scaling], 0)
    back = dot(back_left_ref[...], unit)
    surface = dot(jnp.concatenate([back[:side], back[side:]], 1), back_right_ref[...])
    narrow = lane[:, :128]
    for g in range(groups):
        best = jnp.max(surface[g * SS : (g + 1) * SS], axis=0, keepdims=True)
        best = jnp.broadcast_to(best, (8, 128))
        for step in (1, 2, 4, 8, 16):
            partner = jnp.where(
                narrow // step % 2 == 0,
                pltpu.roll(best, 128 - step, 1),
                pltpu.roll(best, step, 1),
            )
            best = jnp.maximum(best, partner)
        stamp_weights[g * 8 : (g + 1) * 8, :] = jnp.maximum(best, 0.1)


def normal_kernel(stamp_rows, stamp_cols, slots, is_near, near, far, flat_x, variance_stamps,
                  stamp_weights, variance_sum, template_variance, out, flat_y, sem):
    lay_strip(slots, is_near, near, far, 1, template_variance, sem)
    _, columns = template_variance.shape
    stamps = stamp_rows.shape[0]
    groups = stamps // 4
    narrow = lax.broadcasted_iota(jnp.int32, (1, 128), 1)
    pixel_weight = []
    for g in range(groups):
        weight = None
        for k in range(4):
            row, off, cols = stamp_place(stamp_rows, stamp_cols, g * 4 + k, columns)
            w = inner_stamp(template_variance[:, cols], row, off, k)
            weight = w if k == 0 else jnp.where(narrow // 32 == k, w, weight)
        weight = variance_stamps[g * SS : (g + 1) * SS, :] + weight
        pixel_weight.append(stamp_weights[g * 8 : g * 8 + 1, :] / weight)
    pixel_weight = jnp.concatenate(pixel_weight, 1)
    wide = groups * 128
    for r in range(SS):
        at = slice(r * wide, (r + 1) * wide)
        pair = flat_x[:, at].astype(jnp.float32)
        y = (pair[:32] + pair[32:]) * pixel_weight[r : r + 1, :]
        high = y.astype(jnp.bfloat16).astype(jnp.float32)
        flat_y[:, at] = jnp.concatenate([high, y - high], 0).astype(jnp.bfloat16)
    gram = lax.dot_general(
        flat_y[...], flat_x[...], (((1,), (1,)), ((), ())), preferred_element_type=jnp.float32
    )
    gram = widen(gram[:32] + gram[32:])
    out[:32, :] = gram + pltpu.roll(gram, 96, 1)
    total_t = total_of(template_variance[...])
    out[32:, :] = jnp.where(narrow == 0, variance_sum[...], jnp.broadcast_to(total_t, (8, 128)))


def eliminate(a):
    row_index = lax.broadcasted_iota(jnp.int32, (32, 1), 0)
    for k in range(NB):
        pivot_row = a[k : k + 1, :]
        pivot_row = pivot_row / pivot_row[:, k : k + 1]
        column = a[:, k : k + 1] - (row_index == k).astype(jnp.float32)
        a = a - column * pivot_row
    return jnp.where(row_index < NB, a[:, NB : NB + 1], 0.0)


def widen(x):
    return jnp.concatenate([x, jnp.zeros((x.shape[0], 128 - x.shape[1]), jnp.float32)], 1)


def total_of(x):
    return jnp.sum(jnp.sum(x, axis=0, keepdims=True), axis=1, keepdims=True)


def correlate(kernel_t, before, own, after, stack, bands, products, out, science):
    height, columns = own.shape
    reach = height + 2 * MARGIN
    lead = HALO - MARGIN
    tiles = columns // 128 + 1
    high = kernel_t.astype(jnp.bfloat16).astype(jnp.float32)
    low = kernel_t - high
    blank = jnp.zeros_like(high)
    high, low = jnp.concatenate([high, blank], 1), jnp.concatenate([low, blank], 1)
    taps = high + pltpu.roll(high, reach, 1) + pltpu.roll(low, 2 * reach, 1)
    for v in range(KS):
        w, j = v // FINE, v % FINE
        band = jnp.broadcast_to(taps[v : v + 1, :], (height, 256))
        band = pltpu.roll(band, 0, 1, stride=1, stride_axis=0)
        bands[w * height : (w + 1) * height, j * 256 : (j + 1) * 256] = band.astype(jnp.bfloat16)

    lane = lax.broadcasted_iota(jnp.int32, (1, 128), 1)
    rest = jnp.zeros((256 - 3 * reach, 128), jnp.float32)
    empty = jnp.zeros((reach, 128), jnp.float32)

    def tile(t):
        if t % tiles == tiles - 1:
            return empty
        at = slice(t % tiles * 128, (t % tiles + 1) * 128)
        return jnp.concatenate([before[:, at], own[:, at], after[:, at]], 0)[lead : lead + reach]

    left, here = tile(-1), tile(0)
    left_last = pltpu.roll(left, 1, 1)
    here_last = pltpu.roll(here, 1, 1)
    here_next = pltpu.roll(here, 127, 1)
    for t in range(tiles):
        right = tile(t + 1)
        right_last, right_next = pltpu.roll(right, 1, 1), pltpu.roll(right, 127, 1)
        moved = (
            jnp.where(lane < 1, left_last, here_last),
            here,
            jnp.where(lane < 127, here_next, right_next),
        )
        for j, x in enumerate(moved):
            high = x.astype(jnp.bfloat16).astype(jnp.float32)
            stack[j * 256 : (j + 1) * 256, t * 128 : (t + 1) * 128] = jnp.concatenate(
                [high, x - high, high, rest], 0
            ).astype(jnp.bfloat16)
        left_last, here, here_last, here_next = here_last, right, right_last, right_next
    chunk = 384 if tiles % 3 == 0 else 128
    for c in range(0, tiles * 128, chunk):
        at = slice(c, c + chunk)
        products[:, at] = jnp.dot(bands[...], stack[:, at], preferred_element_type=jnp.float32)

    def finish(g, carry):
        at = pl.multiple_of(g * 8, 8)

        def product(w):
            return products[pl.ds(w * height + at, 8), :]

        half = COARSE // 2
        total = product(half)
        for w in range(COARSE):
            if w != half:
                total = total + pltpu.roll(product(w), FINE * (half - w) % (tiles * 128), 1)
        total = total[:, :columns]
        rows = pl.ds(at, 8)
        out[rows, :] = total if science is None else science[rows, :] - total
        return carry

    lax.fori_loop(0, height // 8, finish, 0, unroll=True)


def first_kernel(pixels, p0, p1, p2, p3, science, before, own, after, lv, lu, left, right, back_left,
                 back_right, difference, top, bottom, filter_out, powers, stack, bands, products):
    sums = p0[...] + p1[...] + p2[...] + p3[...]
    coefficients = eliminate(sums[:32, :])
    mean_science = sums[32:33, 0:1] * (1.0 / pixels)
    mean_template = sums[32:33, 1:2] * (1.0 / pixels)
    kernel_t = dot(lv[...], coefficients * lu[...])
    v_index = lax.broadcasted_iota(jnp.int32, (32, 128), 0)
    u_index = lax.broadcasted_iota(jnp.int32, (32, 128), 1)
    kernel_t = kernel_t + ((v_index == MARGIN) & (u_index == MARGIN)).astype(jnp.float32)
    step = dot(left[...], kernel_t)
    both = dot(jnp.concatenate([step[:PD], step[PD:]], 1), right[...])
    re, im = both[:, :128], both[:, 128:]
    response = jnp.sqrt(
        (mean_science + mean_template) / (mean_science + mean_template * (re * re + im * im))
    )
    step = dot(back_left[...], response)
    filter_t = dot(jnp.concatenate([step[:32], step[32:]], 1), back_right[...])
    filter_out[...] = filter_t
    powers[0:1, :] = jnp.broadcast_to(total_of(kernel_t * kernel_t), (1, 128))
    powers[1:2, :] = jnp.broadcast_to(total_of(filter_t * filter_t), (1, 128))
    powers[2:, :] = jnp.zeros((6, 128), jnp.float32)
    correlate(kernel_t, before, own, after, stack, bands, products, difference, science)
    top[...] = difference[:HALO, :]
    bottom[...] = difference[difference.shape[0] - HALO :, :]


def second_kernel(filter_t, before, own, after, out, stack, bands, products):
    correlate(filter_t[...], before, own, after, stack, bands, products, out, None)


def correlation_scratch(height, columns):
    return [
        pltpu.VMEM((FINE * 256, columns + 128), jnp.bfloat16),
        pltpu.VMEM((COARSE * height, FINE * 256), jnp.bfloat16),
        pltpu.VMEM((COARSE * height, columns + 128), jnp.float32),
    ]


def edges(top, bottom, axis):
    devices = lax.axis_size(axis)
    up = [(i, i + 1) for i in range(devices - 1)]
    down = [(j, i) for i, j in up]
    before = lax.ppermute(bottom, axis, up)
    after = lax.ppermute(top, axis, down)
    return before, after


def per_device(science, variance, template_blocks, requests, stamp_rows, stamp_cols):
    height, columns = science.shape
    strips = lax.axis_size("det")
    device = lax.axis_index("det")
    held = template_blocks.shape[0]

    half = strips // 2
    here = device // half
    partner = lax.rem(device + half, strips)
    served = lax.dynamic_slice_in_dim(requests, here * half, half, 0)

    def picks_of(owner):
        local = served - owner * held
        mine = (local >= 0) & (local < held)
        again = mine & jnp.pad(mine[:, :-1], ((0, 0), (1, 0)))
        first = jnp.sum(jnp.where(mine & ~again, local, 0), axis=1)
        second = jnp.sum(jnp.where(again, local, 0), axis=1)
        return jnp.stack([first, second], axis=1).reshape(-1).astype(jnp.int32)

    wanted = lax.dynamic_index_in_dim(requests, device, 0, keepdims=False)
    owner = wanted // held
    repeat = owner == jnp.concatenate([owner[:1] - 1, owner[:-1]])
    slots = (owner % half * 2 + repeat).astype(jnp.int32)
    is_near = (owner // half == here).astype(jnp.int32)

    across_halves = [(i, (i + half) % strips) for i in range(strips)]
    halves = [list(range(half)), list(range(half, strips))]

    def serve(x):
        return lax.all_to_all(x, "det", 0, 0, axis_index_groups=halves, tiled=True)

    partner_blocks = lax.ppermute(template_blocks, "det", across_halves)
    near = serve(pick(picks_of(device), template_blocks))
    far_picks = picks_of(partner)
    vmem, smem, anywhere = (pl.BlockSpec(memory_space=m) for m in (VMEM, SMEM, pl.ANY))
    rows, cols = stamp_rows[0], stamp_cols[0]
    stamps = rows.shape[0]
    flat = SS * SS * stamps
    strip = jax.ShapeDtypeStruct((height, columns), jnp.float32)
    row = jax.ShapeDtypeStruct((8, 128), jnp.float32)
    edge = jax.ShapeDtypeStruct((HALO, columns), jnp.float32)
    tables = [jnp.asarray(t) for t in (across_table(), down_table(), *dft_blocks())]
    params = pltpu.CompilerParams(vmem_limit_bytes=VMEM_LIMIT)
    small = pltpu.CompilerParams(vmem_limit_bytes=VMEM_SMALL)
    stamp_rows_shape = jax.ShapeDtypeStruct((stamps // 4 * SS, 128), jnp.float32)
    science_stamps, variance_stamps, variance_sum = pl.pallas_call(
        science_kernel,
        out_shape=[stamp_rows_shape, stamp_rows_shape, row],
        in_specs=[smem] * 2 + [vmem] * 2,
        out_specs=[vmem] * 3,
        compiler_params=params,
        name="science_stamps",
    )(rows, cols, science, variance)
    partner_blocks, near, slots, is_near, science_stamps, variance_stamps, variance_sum = (
        lax.optimization_barrier(
            (partner_blocks, near, slots, is_near, science_stamps, variance_stamps, variance_sum)
        )
    )
    far_image = serve(pick(far_picks, partner_blocks, 0))
    picked_variance, far_image = lax.optimization_barrier(
        (pick(far_picks, partner_blocks, 1), far_image)
    )
    far_variance = serve(picked_variance)

    template_image, template_top, template_bottom, flat_x, stamp_weights = pl.pallas_call(
        image_kernel,
        out_shape=[
            strip,
            edge,
            edge,
            jax.ShapeDtypeStruct((64, flat), jnp.bfloat16),
            jax.ShapeDtypeStruct((stamps // 4 * 8, 128), jnp.float32),
        ],
        in_specs=[smem] * 4 + [anywhere] * 2 + [vmem] + [anywhere] * TABLES,
        out_specs=[vmem] * 5,
        scratch_shapes=[
            pltpu.VMEM((stamps // 4, 32 * SS, 128), jnp.float32),
            pltpu.SemaphoreType.DMA((wanted.shape[0],)),
            pltpu.SemaphoreType.DMA((TABLES,)),
            *[pltpu.VMEM(t.shape, t.dtype) for t in tables],
        ],
        compiler_params=params,
        name="stamp_images",
    )(rows, cols, slots, is_near, near, far_image, science_stamps, *tables)
    before, after = edges(template_top, template_bottom, "det")
    template_variance, partial = pl.pallas_call(
        normal_kernel,
        out_shape=[strip, jax.ShapeDtypeStruct((40, 128), jnp.float32)],
        in_specs=[smem] * 4 + [anywhere] * 2 + [vmem] * 4,
        out_specs=[vmem] * 2,
        scratch_shapes=[
            pltpu.VMEM((64, flat), jnp.bfloat16),
            pltpu.SemaphoreType.DMA((wanted.shape[0],)),
        ],
        compiler_params=small,
        name="normal_equations",
    )(rows, cols, slots, is_near, near, far_variance, flat_x, variance_stamps, stamp_weights, variance_sum)
    partials = [partial]
    for shift in range(1, CPER):
        partials.append(
            lax.ppermute(
                partial,
                "det",
                [(i, i // CPER * CPER + (i + shift) % CPER) for i in range(strips)],
            )
        )
    pixels = CPER * height * columns
    tables = [jnp.asarray(t) for t in (*basis_tables(), *filter_tables())]
    difference, top, bottom, filter_t, powers = pl.pallas_call(
        functools.partial(first_kernel, pixels),
        out_shape=[
            strip,
            edge,
            edge,
            jax.ShapeDtypeStruct((32, 128), jnp.float32),
            row,
        ],
        in_specs=[vmem] * 14,
        out_specs=[vmem] * 5,
        scratch_shapes=correlation_scratch(height, columns),
        compiler_params=small,
        name="solve_and_subtract",
    )(*partials, science, before, template_image, after, *tables)
    before, after = edges(top, bottom, "det")
    decorrelated_variance = powers[1, 0] * (variance + template_variance * powers[0, 0])
    decorrelated = pl.pallas_call(
        second_kernel,
        out_shape=strip,
        in_specs=[vmem] * 4,
        out_specs=vmem,
        scratch_shapes=correlation_scratch(height, columns),
        compiler_params=small,
        name="decorrelate",
    )(filter_t, before, difference, after)
    return (decorrelated, decorrelated_variance)


def solution(mesh):
    placed = (
        P(("group", "det"), None),
        P(("group", "det"), None),
        P(("group", "det"), None, None, None),
        P("group", None),
        P(("group", "det"), None),
        P(("group", "det"), None),
    )
    return jax.shard_map(
        per_device,
        mesh=mesh,
        in_specs=placed,
        out_specs=(P(("group", "det"), None), P(("group", "det"), None)),
        check_vma=False,
    )
```

```python
import functools

import jax
import jax.numpy as jnp
import numpy as np
from jax import lax
from jax.experimental import pallas as pl
from jax.experimental.pallas import tpu as pltpu
from jax.sharding import PartitionSpec as P

CPER = 4
SS = 32
KS = 21
PD = 32
MARGIN = KS // 2
HALO = 16
EXTENT = SS + 2 * MARGIN

HIGHEST = lax.Precision.HIGHEST
GAUSS_WIDTHS = (0.7, 1.5, 3.0)
GAUSS_DEGREES = (4, 2, 2)
VMEM_LIMIT = 60 * 1024 * 1024
VMEM_SMALL = 32 * 1024 * 1024
VMEM = pltpu.MemorySpace.VMEM
SMEM = pltpu.MemorySpace.SMEM


def line_functions():
    tap_grid = np.arange(KS, dtype=np.float64) - MARGIN
    raw_list = []
    for spread, degree in zip(GAUSS_WIDTHS, GAUSS_DEGREES):
        gaussian = np.exp(-tap_grid * tap_grid / (2.0 * spread * spread))
        for degree_power in range(degree + 1):
            raw_list.append(gaussian * tap_grid**degree_power)
    result = []
    for vector in raw_list:
        for earlier in result:
            vector = vector - np.sum(vector * earlier) * earlier
        result.append(vector / np.sqrt(np.sum(vector * vector)))
    return np.stack(result)


def images_by_across():
    groups = []
    base = 0
    for degree in GAUSS_DEGREES:
        for inner in range(degree + 1):
            groups.append((base + inner, [base + outer for outer in range(degree + 1 - inner)]))
        base += degree + 1
    return groups


LINE = line_functions()
GROUPS = images_by_across()
PAIRS = [(a, b) for b, downs in GROUPS for a in downs]
NB = len(PAIRS)
NFUN = LINE.shape[0]
WROWS = 64
TABLES = 7
FINE, COARSE = 3, 7


def block_diag(matrix, times):
    rows, cols = matrix.shape
    out = np.zeros((rows * times, cols * times))
    for k in range(times):
        out[k * rows : (k + 1) * rows, k * cols : (k + 1) * cols] = matrix
    return out


def across_table():
    table = np.zeros((256, NFUN * 128))
    for b in range(NFUN):
        for k in range(4):
            for c in range(SS):
                table[64 * k + c : 64 * k + c + KS, b * 128 + 32 * k + c] = LINE[b]
    return np.concatenate(split_host(table), 1)


def split_host(table):
    high = table.astype(np.float32).astype(jnp.bfloat16)
    return high, (table - high.astype(np.float64)).astype(np.float32).astype(jnp.bfloat16)


def down_table():
    table = np.zeros((NB * SS, WROWS))
    for image, (a, _) in enumerate(PAIRS):
        for r in range(SS):
            table[image * SS + r, r : r + KS] = LINE[a]
    high, low = split_host(table)
    return np.concatenate([high, high, low], 1)


def dft_blocks():
    grid = np.outer(np.arange(SS), np.arange(SS)) % SS
    c, s = np.cos(2 * np.pi * grid / SS), np.sin(2 * np.pi * grid / SS)
    c, s = block_diag(c, 4), block_diag(s, 4)
    ones = block_diag(np.ones((SS, SS)), 4)
    left = np.concatenate([c, s], 0)
    right = np.block([[c, -s], [-s, -c]])
    back_left = np.block([[c, -s], [s, c]])
    back_right = np.concatenate([c, -s], 0) / (SS * SS)
    return [np.concatenate(split_host(x), 0) for x in (left, right, back_left, back_right, ones)]


def basis_tables():
    lv, lu = np.zeros((32, 32)), np.zeros((32, 128))
    for image, (a, b) in enumerate(PAIRS):
        lv[:KS, image] = LINE[b]
        lu[image, :KS] = LINE[a]
    return lv.astype(np.float32), lu.astype(np.float32)


def filter_tables():
    grid = np.outer(np.arange(PD), np.arange(KS) - MARGIN)
    c, s = np.zeros((PD, 32)), np.zeros((PD, 32))
    c[:, :KS], s[:, :KS] = np.cos(2 * np.pi * grid / PD), np.sin(2 * np.pi * grid / PD)
    cr, sr = np.zeros((128, 128)), np.zeros((128, 128))
    cr[:32, :PD], sr[:32, :PD] = c.T, s.T
    left = np.concatenate([c, s], 0)
    right = np.block([[cr, -sr], [-sr, -cr]])
    back_left = np.concatenate([c.T, s.T], 0) / (PD * PD)
    back_c, back_s = np.zeros((128, 128)), np.zeros((128, 128))
    back_c[:PD, :32], back_s[:PD, :32] = c, s
    back_right = np.concatenate([back_c, -back_s], 0)
    return [x.astype(np.float32) for x in (left, right, back_left, back_right)]


def pick_kernel(plane, picks, source, out, sem):
    count = out.shape[0]

    def copy(k):
        block = source.at[picks[k]] if plane is None else source.at[picks[k], plane]
        return pltpu.make_async_copy(block, out.at[k], sem.at[k])

    def start(k, carry):
        copy(k).start()
        return carry

    def finish(k, carry):
        copy(k).wait()
        return carry

    lax.fori_loop(0, count, start, 0)
    lax.fori_loop(0, count, finish, 0)


def pick(picks, source, plane=None):
    count = picks.shape[0]
    shape = source.shape[1:] if plane is None else source.shape[2:]
    return pl.pallas_call(
        functools.partial(pick_kernel, plane),
        out_shape=jax.ShapeDtypeStruct((count,) + shape, source.dtype),
        in_specs=[pl.BlockSpec(memory_space=SMEM), pl.BlockSpec(memory_space=VMEM)],
        out_specs=pl.BlockSpec(memory_space=pl.ANY),
        scratch_shapes=[pltpu.SemaphoreType.DMA((count,))],
        compiler_params=pltpu.CompilerParams(vmem_limit_bytes=VMEM_LIMIT),
        name="pick_blocks",
    )(picks, source)


def pick_near_kernel(axis, half, requests, source, out, sem):
    owner = lax.axis_index(axis)
    held = source.shape[0]
    base = owner // half * half

    def copies(d):
        first = second = found = jnp.int32(0)
        for j in range(requests.shape[1]):
            local = requests[base + d, j] - owner * held
            mine = (local >= 0) & (local < held)
            first = jnp.where(mine & (found == 0), local, first)
            second = jnp.where(mine & (found > 0), local, second)
            found = jnp.where(mine, 1, found)
        return [
            pltpu.make_async_copy(source.at[block], out.at[2 * d + t], sem.at[2 * d + t])
            for t, block in enumerate((first, second))
        ]

    started = []
    for d in range(half):
        started += copies(d)
        started[-2].start()
        started[-1].start()
    for copy in started:
        copy.wait()


def pick_near(axis, half, requests, source):
    count = 2 * half
    return pl.pallas_call(
        functools.partial(pick_near_kernel, axis, half),
        out_shape=jax.ShapeDtypeStruct((count,) + source.shape[1:], source.dtype),
        in_specs=[pl.BlockSpec(memory_space=SMEM), pl.BlockSpec(memory_space=VMEM)],
        out_specs=pl.BlockSpec(memory_space=pl.ANY),
        scratch_shapes=[pltpu.SemaphoreType.DMA((count,))],
        compiler_params=pltpu.CompilerParams(vmem_limit_bytes=VMEM_LIMIT),
        name="pick_near_blocks",
    )(requests, source)


def lay_strip(slots, is_near, near, far, plane, out, sem):
    needed = slots.shape[0]
    width = near.shape[3]
    for j in range(needed):
        columns = pl.ds(j * width, width)

        @pl.when(is_near[j] == 1)
        def _():
            pltpu.make_async_copy(near.at[slots[j], plane], out.at[:, columns], sem.at[j]).start()

        @pl.when(is_near[j] == 0)
        def _():
            pltpu.make_async_copy(far.at[slots[j]], out.at[:, columns], sem.at[j]).start()

    for j in range(needed):
        columns = pl.ds(j * width, width)
        pltpu.make_async_copy(far.at[slots[j]], out.at[:, columns], sem.at[j]).wait()


def dot(a, b, contract=((1,), (0,))):
    return lax.dot_general(
        a, b, (contract, ((), ())), precision=HIGHEST, preferred_element_type=jnp.float32
    )


def dot16(a, b):
    return jnp.dot(a, b, preferred_element_type=jnp.float32)


def split(x):
    high = x.astype(jnp.bfloat16)
    return high, (x - high.astype(jnp.float32)).astype(jnp.bfloat16)


def dot_left(table, x):
    half = table.shape[0] // 2
    high, low = split(x)
    return dot16(table[:half, :], high) + (dot16(table[half:, :], high) + dot16(table[:half, :], low))


def dot_right(x, table):
    half = table.shape[0] // 2
    high, low = split(x)
    return dot16(high, table[:half, :]) + (dot16(low, table[:half, :]) + dot16(high, table[half:, :]))


def stamp_place(stamp_rows, stamp_cols, stamp, columns):
    row = stamp_rows[stamp] - (SS // 2 + MARGIN)
    col = stamp_cols[stamp] - (SS // 2 + MARGIN)
    base = pl.multiple_of(jnp.minimum(col // 128 * 128, columns - 256), 128)
    return row, col - base, pl.ds(base, 256)


def inner_stamp(x, row, off, k):
    moved = pltpu.roll(x, lax.rem(32 * k - off - MARGIN + 512, 256), 1)[:, :128]
    return pltpu.roll(moved, x.shape[0] - row - MARGIN, 0)[:SS]


def science_kernel(stamp_rows, stamp_cols, science, variance, science_stamps, variance_stamps, variance_sum):
    _, columns = science.shape
    narrow = lax.broadcasted_iota(jnp.int32, (1, 128), 1)
    for g in range(stamp_rows.shape[0] // 4):
        sci = var = None
        for k in range(4):
            row, off, cols = stamp_place(stamp_rows, stamp_cols, g * 4 + k, columns)
            s = inner_stamp(science[:, cols], row, off, k)
            v = inner_stamp(variance[:, cols], row, off, k)
            here = narrow // 32 == k
            sci, var = (s, v) if k == 0 else (jnp.where(here, s, sci), jnp.where(here, v, var))
        science_stamps[g * SS : (g + 1) * SS, :] = sci
        variance_stamps[g * SS : (g + 1) * SS, :] = var
    variance_sum[...] = jnp.broadcast_to(total_of(variance[...]), (8, 128))


def image_kernel(stamp_rows, stamp_cols, slots, is_near, near, far, science_stamps, *refs):
    tables_in, refs = refs[:TABLES], refs[TABLES:]
    template, top, bottom, flat_x, stamp_weights, images, sem, table_sem = refs[:8]
    tables = refs[8:]
    loads = [
        pltpu.make_async_copy(source, table, table_sem.at[i])
        for i, (source, table) in enumerate(zip(tables_in, tables))
    ]
    for load in loads:
        load.start()
    across_ref, down_ref, left_ref, right_ref, back_left_ref, back_right_ref, ones_ref = tables
    lay_strip(slots, is_near, near, far, 0, template, sem)
    height, columns = template.shape
    top[...] = template[:HALO, :]
    bottom[...] = template[height - HALO :, :]
    stamps = stamp_rows.shape[0]
    groups = stamps // 4
    lane = lax.broadcasted_iota(jnp.int32, (1, 256), 1)

    windows, sciences, templates = [], [], []
    for g in range(groups):
        window = tmp = None
        for k in range(4):
            row, off, cols = stamp_place(stamp_rows, stamp_cols, g * 4 + k, columns)
            t = template[:, cols]
            to64 = lax.rem(64 * k - off + 256, 256)
            tw = pltpu.roll(pltpu.roll(t, to64, 1), lax.rem(height - row, height), 0)[:WROWS]
            t = inner_stamp(t, row, off, k)
            if k == 0:
                window, tmp = tw, t
            else:
                window = jnp.where(lane // 64 == k, tw, window)
                tmp = jnp.where(lane[:, :128] // 32 == k, t, tmp)
        windows.append(window)
        templates.append(tmp)
        sciences.append(science_stamps[g * SS : (g + 1) * SS, :])
    for load in loads:
        load.wait()

    high, low = split(jnp.concatenate(windows, 0))
    table_high, table_low = across_ref[:, : NFUN * 128], across_ref[:, NFUN * 128 :]
    across = dot16(high, table_high) + (dot16(low, table_high) + dot16(high, table_low))
    row = 0
    for b, downs in GROUPS:
        piece = jnp.concatenate(
            [across[g * WROWS : (g + 1) * WROWS, b * 128 : (b + 1) * 128] for g in range(groups)], 1
        )
        count = len(downs) * SS
        high = piece.astype(jnp.bfloat16).astype(jnp.float32)
        stacked = jnp.concatenate([high, piece - high, high], 0).astype(jnp.bfloat16)
        made = dot16(down_ref[row : row + count, :], stacked)
        for g in range(groups):
            images[g, row : row + count, :] = made[:, g * 128 : (g + 1) * 128]
        row += count
    for g in range(groups):
        images[g, NB * SS : (NB + 1) * SS, :] = sciences[g] - templates[g]
        images[g, (NB + 1) * SS :, :] = jnp.zeros(((31 - NB) * SS, 128), jnp.float32)
    wide = groups * 128
    for r in range(SS):
        x = jnp.concatenate([images[g, pl.ds(r, 32, stride=SS), :] for g in range(groups)], 1)
        high = x.astype(jnp.bfloat16).astype(jnp.float32)
        pair = jnp.concatenate([high, x - high], 0).astype(jnp.bfloat16)
        flat_x[:, r * wide : (r + 1) * wide] = pair

    sci = jnp.concatenate(sciences, 0)
    tmp = jnp.concatenate(templates, 0)
    side = groups * SS
    first = dot_left(left_ref, jnp.concatenate([sci, tmp], 1))
    first = jnp.concatenate(
        [
            jnp.concatenate([first[:side, :128], first[side:, :128]], 1),
            jnp.concatenate([first[:side, 128:], first[side:, 128:]], 1),
        ],
        0,
    )
    second = dot_right(first, right_ref)
    sre, sim = second[:side, :128], second[:side, 128:]
    tre, tim = second[side:, :128], second[side:, 128:]
    cross_re = sre * tre + sim * tim
    cross_im = sim * tre - sre * tim
    magnitude = jnp.sqrt(cross_re * cross_re + cross_im * cross_im)
    mean = dot_right(dot_left(ones_ref, magnitude), ones_ref) * (1.0 / (SS * SS))
    scaling = 1.0 / jnp.maximum(magnitude, 0.25 * (mean + 1e-06))
    unit = jnp.concatenate([cross_re * scaling, cross_im * scaling], 0)
    back = dot_left(back_left_ref, unit)
    surface = dot_right(jnp.concatenate([back[:side], back[side:]], 1), back_right_ref)
    narrow = lane[:, :128]
    for g in range(groups):
        best = jnp.max(surface[g * SS : (g + 1) * SS], axis=0, keepdims=True)
        best = jnp.broadcast_to(best, (8, 128))
        for step in (1, 2, 4, 8, 16):
            partner = jnp.where(
                narrow // step % 2 == 0,
                pltpu.roll(best, 128 - step, 1),
                pltpu.roll(best, step, 1),
            )
            best = jnp.maximum(best, partner)
        stamp_weights[g * 8 : (g + 1) * 8, :] = jnp.maximum(best, 0.1)


def normal_kernel(stamp_rows, stamp_cols, slots, is_near, near, far, flat_x, variance_stamps,
                  stamp_weights, variance_sum, template_variance, out, images, flat_y, sem, images_sem):
    load = pltpu.make_async_copy(flat_x, images, images_sem)
    load.start()
    lay_strip(slots, is_near, near, far, 1, template_variance, sem)
    _, columns = template_variance.shape
    stamps = stamp_rows.shape[0]
    groups = stamps // 4
    narrow = lax.broadcasted_iota(jnp.int32, (1, 128), 1)
    pixel_weight = []
    for g in range(groups):
        weight = None
        for k in range(4):
            row, off, cols = stamp_place(stamp_rows, stamp_cols, g * 4 + k, columns)
            w = inner_stamp(template_variance[:, cols], row, off, k)
            weight = w if k == 0 else jnp.where(narrow // 32 == k, w, weight)
        weight = variance_stamps[g * SS : (g + 1) * SS, :] + weight
        pixel_weight.append(stamp_weights[g * 8 : g * 8 + 1, :] / weight)
    pixel_weight = jnp.concatenate(pixel_weight, 1)
    wide = groups * 128
    load.wait()
    for r in range(SS):
        at = slice(r * wide, (r + 1) * wide)
        pair = images[:, at].astype(jnp.float32)
        y = (pair[:32] + pair[32:]) * pixel_weight[r : r + 1, :]
        high = y.astype(jnp.bfloat16).astype(jnp.float32)
        flat_y[:, at] = jnp.concatenate([high, y - high], 0).astype(jnp.bfloat16)
    gram = lax.dot_general(
        flat_y[...], images[...], (((1,), (1,)), ((), ())), preferred_element_type=jnp.float32
    )
    gram = widen(gram[:32] + gram[32:])
    out[:32, :] = gram + pltpu.roll(gram, 96, 1)
    total_t = total_of(template_variance[...])
    out[32:, :] = jnp.where(narrow == 0, variance_sum[...], jnp.broadcast_to(total_t, (8, 128)))


def eliminate(a):
    row_index = lax.broadcasted_iota(jnp.int32, (32, 1), 0)
    for k in range(NB):
        pivot_row = a[k : k + 1, :]
        pivot_row = pivot_row / pivot_row[:, k : k + 1]
        column = a[:, k : k + 1] - (row_index == k).astype(jnp.float32)
        a = a - column * pivot_row
    return jnp.where(row_index < NB, a[:, NB : NB + 1], 0.0)


def widen(x):
    return jnp.concatenate([x, jnp.zeros((x.shape[0], 128 - x.shape[1]), jnp.float32)], 1)


def total_of(x):
    return jnp.sum(jnp.sum(x, axis=0, keepdims=True), axis=1, keepdims=True)


def correlate(kernel_t, before, own, after, stack, bands, products, out, science):
    height, columns = own.shape
    reach = height + 2 * MARGIN
    lead = HALO - MARGIN
    tiles = columns // 128 + 1
    high = kernel_t.astype(jnp.bfloat16).astype(jnp.float32)
    low = kernel_t - high
    blank = jnp.zeros_like(high)
    high, low = jnp.concatenate([high, blank], 1), jnp.concatenate([low, blank], 1)
    taps = high + pltpu.roll(high, reach, 1) + pltpu.roll(low, 2 * reach, 1)
    for v in range(KS):
        w, j = v // FINE, v % FINE
        band = jnp.broadcast_to(taps[v : v + 1, :], (height, 256))
        band = pltpu.roll(band, 0, 1, stride=1, stride_axis=0)
        bands[w * height : (w + 1) * height, j * 256 : (j + 1) * 256] = band.astype(jnp.bfloat16)

    lane = lax.broadcasted_iota(jnp.int32, (1, 128), 1)
    rest = jnp.zeros((256 - 3 * reach, 128), jnp.float32)
    empty = jnp.zeros((reach, 128), jnp.float32)

    def tile(t):
        if t % tiles == tiles - 1:
            return empty
        at = slice(t % tiles * 128, (t % tiles + 1) * 128)
        return jnp.concatenate([before[:, at], own[:, at], after[:, at]], 0)[lead : lead + reach]

    left, here = tile(-1), tile(0)
    left_last = pltpu.roll(left, 1, 1)
    here_last = pltpu.roll(here, 1, 1)
    here_next = pltpu.roll(here, 127, 1)
    for t in range(tiles):
        right = tile(t + 1)
        right_last, right_next = pltpu.roll(right, 1, 1), pltpu.roll(right, 127, 1)
        moved = (
            jnp.where(lane < 1, left_last, here_last),
            here,
            jnp.where(lane < 127, here_next, right_next),
        )
        for j, x in enumerate(moved):
            high = x.astype(jnp.bfloat16).astype(jnp.float32)
            stack[j * 256 : (j + 1) * 256, t * 128 : (t + 1) * 128] = jnp.concatenate(
                [high, x - high, high, rest], 0
            ).astype(jnp.bfloat16)
        left_last, here, here_last, here_next = here_last, right, right_last, right_next
    chunk = 384 if tiles % 3 == 0 else 128
    for c in range(0, tiles * 128, chunk):
        at = slice(c, c + chunk)
        products[:, at] = jnp.dot(bands[...], stack[:, at], preferred_element_type=jnp.float32)

    def finish(g, carry):
        at = pl.multiple_of(g * 8, 8)

        def product(w):
            return products[pl.ds(w * height + at, 8), :]

        half = COARSE // 2
        total = product(half)
        for w in range(COARSE):
            if w != half:
                total = total + pltpu.roll(product(w), FINE * (half - w) % (tiles * 128), 1)
        total = total[:, :columns]
        rows = pl.ds(at, 8)
        out[rows, :] = total if science is None else science[rows, :] - total
        return carry

    lax.fori_loop(0, height // 8, finish, 0, unroll=True)


def first_kernel(pixels, p0, p1, p2, p3, science, before, own, after, lv, lu, left, right, back_left,
                 back_right, difference, top, bottom, filter_out, powers, stack, bands, products):
    sums = p0[...] + p1[...] + p2[...] + p3[...]
    coefficients = eliminate(sums[:32, :])
    mean_science = sums[32:33, 0:1] * (1.0 / pixels)
    mean_template = sums[32:33, 1:2] * (1.0 / pixels)
    kernel_t = dot(lv[...], coefficients * lu[...])
    v_index = lax.broadcasted_iota(jnp.int32, (32, 128), 0)
    u_index = lax.broadcasted_iota(jnp.int32, (32, 128), 1)
    kernel_t = kernel_t + ((v_index == MARGIN) & (u_index == MARGIN)).astype(jnp.float32)
    step = dot(left[...], kernel_t)
    both = dot(jnp.concatenate([step[:PD], step[PD:]], 1), right[...])
    re, im = both[:, :128], both[:, 128:]
    response = jnp.sqrt(
        (mean_science + mean_template) / (mean_science + mean_template * (re * re + im * im))
    )
    step = dot(back_left[...], response)
    filter_t = dot(jnp.concatenate([step[:32], step[32:]], 1), back_right[...])
    filter_out[...] = filter_t
    powers[0:1, :] = jnp.broadcast_to(total_of(kernel_t * kernel_t), (1, 128))
    powers[1:2, :] = jnp.broadcast_to(total_of(filter_t * filter_t), (1, 128))
    powers[2:, :] = jnp.zeros((6, 128), jnp.float32)
    correlate(kernel_t, before, own, after, stack, bands, products, difference, science)
    top[...] = difference[:HALO, :]
    bottom[...] = difference[difference.shape[0] - HALO :, :]


def second_kernel(filter_t, before, own, after, out, stack, bands, products):
    correlate(filter_t[...], before, own, after, stack, bands, products, out, None)


def correlation_scratch(height, columns):
    return [
        pltpu.VMEM((FINE * 256, columns + 128), jnp.bfloat16),
        pltpu.VMEM((COARSE * height, FINE * 256), jnp.bfloat16),
        pltpu.VMEM((COARSE * height, columns + 128), jnp.float32),
    ]


def edges(top, bottom, axis):
    devices = lax.axis_size(axis)
    up = [(i, i + 1) for i in range(devices - 1)]
    down = [(j, i) for i, j in up]
    before = lax.ppermute(bottom, axis, up)
    after = lax.ppermute(top, axis, down)
    return before, after


def per_device(science, variance, template_blocks, requests, stamp_rows, stamp_cols):
    height, columns = science.shape
    strips = lax.axis_size("det")
    device = lax.axis_index("det")
    held = template_blocks.shape[0]

    half = strips // 2
    here = device // half
    partner = lax.rem(device + half, strips)
    served = lax.dynamic_slice_in_dim(requests, here * half, half, 0)

    def picks_of(owner):
        local = served - owner * held
        mine = (local >= 0) & (local < held)
        again = mine & jnp.pad(mine[:, :-1], ((0, 0), (1, 0)))
        first = jnp.sum(jnp.where(mine & ~again, local, 0), axis=1)
        second = jnp.sum(jnp.where(again, local, 0), axis=1)
        return jnp.stack([first, second], axis=1).reshape(-1).astype(jnp.int32)

    wanted = lax.dynamic_index_in_dim(requests, device, 0, keepdims=False)
    owner = wanted // held
    repeat = owner == jnp.concatenate([owner[:1] - 1, owner[:-1]])
    slots = (owner % half * 2 + repeat).astype(jnp.int32)
    is_near = (owner // half == here).astype(jnp.int32)

    across_halves = [(i, (i + half) % strips) for i in range(strips)]
    halves = [list(range(half)), list(range(half, strips))]

    def serve(x):
        return lax.all_to_all(x, "det", 0, 0, axis_index_groups=halves, tiled=True)

    partner_blocks = lax.ppermute(template_blocks, "det", across_halves)
    near = serve(pick_near("det", half, requests, template_blocks))
    far_picks = picks_of(partner)
    vmem, smem, anywhere = (pl.BlockSpec(memory_space=m) for m in (VMEM, SMEM, pl.ANY))
    rows, cols = stamp_rows[0], stamp_cols[0]
    stamps = rows.shape[0]
    flat = SS * SS * stamps
    strip = jax.ShapeDtypeStruct((height, columns), jnp.float32)
    row = jax.ShapeDtypeStruct((8, 128), jnp.float32)
    edge = jax.ShapeDtypeStruct((HALO, columns), jnp.float32)
    tables = [jnp.asarray(t) for t in (across_table(), down_table(), *dft_blocks())]
    params = pltpu.CompilerParams(vmem_limit_bytes=VMEM_LIMIT)
    small = pltpu.CompilerParams(vmem_limit_bytes=VMEM_SMALL)
    stamp_rows_shape = jax.ShapeDtypeStruct((stamps // 4 * SS, 128), jnp.float32)
    science_stamps, variance_stamps, variance_sum = pl.pallas_call(
        science_kernel,
        out_shape=[stamp_rows_shape, stamp_rows_shape, row],
        in_specs=[smem] * 2 + [vmem] * 2,
        out_specs=[vmem] * 3,
        compiler_params=params,
        name="science_stamps",
    )(rows, cols, science, variance)
    partner_blocks, near, slots, is_near, science_stamps, variance_stamps, variance_sum = (
        lax.optimization_barrier(
            (partner_blocks, near, slots, is_near, science_stamps, variance_stamps, variance_sum)
        )
    )
    far_image = serve(pick(far_picks, partner_blocks, 0))
    picked_variance, far_image = lax.optimization_barrier(
        (pick(far_picks, partner_blocks, 1), far_image)
    )
    far_variance = serve(picked_variance)

    template_image, template_top, template_bottom, flat_x, stamp_weights = pl.pallas_call(
        image_kernel,
        out_shape=[
            strip,
            edge,
            edge,
            jax.ShapeDtypeStruct((64, flat), jnp.bfloat16),
            jax.ShapeDtypeStruct((stamps // 4 * 8, 128), jnp.float32),
        ],
        in_specs=[smem] * 4 + [anywhere] * 2 + [vmem] + [anywhere] * TABLES,
        out_specs=[vmem] * 5,
        scratch_shapes=[
            pltpu.VMEM((stamps // 4, 32 * SS, 128), jnp.float32),
            pltpu.SemaphoreType.DMA((wanted.shape[0],)),
            pltpu.SemaphoreType.DMA((TABLES,)),
            *[pltpu.VMEM(t.shape, t.dtype) for t in tables],
        ],
        compiler_params=params,
        name="stamp_images",
    )(rows, cols, slots, is_near, near, far_image, science_stamps, *tables)
    before, after = edges(template_top, template_bottom, "det")
    template_variance, partial = pl.pallas_call(
        normal_kernel,
        out_shape=[strip, jax.ShapeDtypeStruct((40, 128), jnp.float32)],
        in_specs=[smem] * 4 + [anywhere] * 3 + [vmem] * 3,
        out_specs=[vmem] * 2,
        scratch_shapes=[
            pltpu.VMEM((64, flat), jnp.bfloat16),
            pltpu.VMEM((64, flat), jnp.bfloat16),
            pltpu.SemaphoreType.DMA((wanted.shape[0],)),
            pltpu.SemaphoreType.DMA,
        ],
        compiler_params=params,
        name="normal_equations",
    )(rows, cols, slots, is_near, near, far_variance, flat_x, variance_stamps, stamp_weights, variance_sum)
    partials = [partial]
    for shift in range(1, CPER):
        partials.append(
            lax.ppermute(
                partial,
                "det",
                [(i, i // CPER * CPER + (i + shift) % CPER) for i in range(strips)],
            )
        )
    pixels = CPER * height * columns
    tables = [jnp.asarray(t) for t in (*basis_tables(), *filter_tables())]
    difference, top, bottom, filter_t, powers = pl.pallas_call(
        functools.partial(first_kernel, pixels),
        out_shape=[
            strip,
            edge,
            edge,
            jax.ShapeDtypeStruct((32, 128), jnp.float32),
            row,
        ],
        in_specs=[vmem] * 14,
        out_specs=[vmem] * 5,
        scratch_shapes=correlation_scratch(height, columns),
        compiler_params=small,
        name="solve_and_subtract",
    )(*partials, science, before, template_image, after, *tables)
    before, after = edges(top, bottom, "det")
    decorrelated_variance = powers[1, 0] * (variance + template_variance * powers[0, 0])
    decorrelated = pl.pallas_call(
        second_kernel,
        out_shape=strip,
        in_specs=[vmem] * 4,
        out_specs=vmem,
        scratch_shapes=correlation_scratch(height, columns),
        compiler_params=small,
        name="decorrelate",
    )(filter_t, before, difference, after)
    return (decorrelated, decorrelated_variance)


def solution(mesh):
    placed = (
        P(("group", "det"), None),
        P(("group", "det"), None),
        P(("group", "det"), None, None, None),
        P("group", None),
        P(("group", "det"), None),
        P(("group", "det"), None),
    )
    return jax.shard_map(
        per_device,
        mesh=mesh,
        in_specs=placed,
        out_specs=(P(("group", "det"), None), P(("group", "det"), None)),
        check_vma=False,
    )
```

```python
import functools

import jax
import jax.numpy as jnp
import numpy as np
from jax import lax
from jax.experimental import pallas as pl
from jax.experimental.pallas import tpu as pltpu
from jax.sharding import PartitionSpec as P

CPER = 4
SS = 32
KS = 21
PD = 32
MARGIN = KS // 2
HALO = 16
EXTENT = SS + 2 * MARGIN

HIGHEST = lax.Precision.HIGHEST
GAUSS_WIDTHS = (0.7, 1.5, 3.0)
GAUSS_DEGREES = (4, 2, 2)
VMEM_LIMIT = 60 * 1024 * 1024
VMEM_SMALL = 32 * 1024 * 1024
VMEM = pltpu.MemorySpace.VMEM
SMEM = pltpu.MemorySpace.SMEM


def line_functions():
    tap_grid = np.arange(KS, dtype=np.float64) - MARGIN
    raw_list = []
    for spread, degree in zip(GAUSS_WIDTHS, GAUSS_DEGREES):
        gaussian = np.exp(-tap_grid * tap_grid / (2.0 * spread * spread))
        for degree_power in range(degree + 1):
            raw_list.append(gaussian * tap_grid**degree_power)
    result = []
    for vector in raw_list:
        for earlier in result:
            vector = vector - np.sum(vector * earlier) * earlier
        result.append(vector / np.sqrt(np.sum(vector * vector)))
    return np.stack(result)


def images_by_across():
    groups = []
    base = 0
    for degree in GAUSS_DEGREES:
        for inner in range(degree + 1):
            groups.append((base + inner, [base + outer for outer in range(degree + 1 - inner)]))
        base += degree + 1
    return groups


LINE = line_functions()
GROUPS = images_by_across()
PAIRS = [(a, b) for b, downs in GROUPS for a in downs]
NB = len(PAIRS)
NFUN = LINE.shape[0]
WROWS = 64
TABLES = 7
FINE, COARSE = 3, 7


def block_diag(matrix, times):
    rows, cols = matrix.shape
    out = np.zeros((rows * times, cols * times))
    for k in range(times):
        out[k * rows : (k + 1) * rows, k * cols : (k + 1) * cols] = matrix
    return out


def across_table():
    table = np.zeros((256, NFUN * 128))
    for b in range(NFUN):
        for k in range(4):
            for c in range(SS):
                table[64 * k + c : 64 * k + c + KS, b * 128 + 32 * k + c] = LINE[b]
    return np.concatenate(split_host(table), 1)


def split_host(table):
    high = table.astype(np.float32).astype(jnp.bfloat16)
    return high, (table - high.astype(np.float64)).astype(np.float32).astype(jnp.bfloat16)


def down_table():
    table = np.zeros((NB * SS, WROWS))
    for image, (a, _) in enumerate(PAIRS):
        for r in range(SS):
            table[image * SS + r, r : r + KS] = LINE[a]
    high, low = split_host(table)
    return np.concatenate([high, high, low], 1)


def dft_blocks():
    grid = np.outer(np.arange(SS), np.arange(SS)) % SS
    c, s = np.cos(2 * np.pi * grid / SS), np.sin(2 * np.pi * grid / SS)
    c, s = block_diag(c, 4), block_diag(s, 4)
    ones = block_diag(np.ones((SS, SS)), 4)
    left = np.concatenate([c, s], 0)
    right = np.block([[c, -s], [-s, -c]])
    back_left = np.block([[c, -s], [s, c]])
    back_right = np.concatenate([c, -s], 0) / (SS * SS)
    return [np.concatenate(split_host(x), 0) for x in (left, right, back_left, back_right, ones)]


def basis_tables():
    lv, lu = np.zeros((32, 32)), np.zeros((32, 128))
    for image, (a, b) in enumerate(PAIRS):
        lv[:KS, image] = LINE[b]
        lu[image, :KS] = LINE[a]
    return np.concatenate(split_host(lv), 0), lu.astype(np.float32)


def filter_tables():
    grid = np.outer(np.arange(PD), np.arange(KS) - MARGIN)
    c, s = np.zeros((PD, 32)), np.zeros((PD, 32))
    c[:, :KS], s[:, :KS] = np.cos(2 * np.pi * grid / PD), np.sin(2 * np.pi * grid / PD)
    cr, sr = np.zeros((128, 128)), np.zeros((128, 128))
    cr[:32, :PD], sr[:32, :PD] = c.T, s.T
    left = np.concatenate([c, s], 0)
    right = np.block([[cr, -sr], [-sr, -cr]])
    back_left = np.concatenate([c.T, s.T], 0) / (PD * PD)
    back_c, back_s = np.zeros((128, 128)), np.zeros((128, 128))
    back_c[:PD, :32], back_s[:PD, :32] = c, s
    back_right = np.concatenate([back_c, -back_s], 0)
    return [np.concatenate(split_host(x), 0) for x in (left, right, back_left, back_right)]


def pick_kernel(plane, picks, source, out, sem):
    count = out.shape[0]

    def copy(k):
        block = source.at[picks[k]] if plane is None else source.at[picks[k], plane]
        return pltpu.make_async_copy(block, out.at[k], sem.at[k])

    def start(k, carry):
        copy(k).start()
        return carry

    def finish(k, carry):
        copy(k).wait()
        return carry

    lax.fori_loop(0, count, start, 0)
    lax.fori_loop(0, count, finish, 0)


def pick(picks, source, plane=None):
    count = picks.shape[0]
    shape = source.shape[1:] if plane is None else source.shape[2:]
    return pl.pallas_call(
        functools.partial(pick_kernel, plane),
        out_shape=jax.ShapeDtypeStruct((count,) + shape, source.dtype),
        in_specs=[pl.BlockSpec(memory_space=SMEM), pl.BlockSpec(memory_space=VMEM)],
        out_specs=pl.BlockSpec(memory_space=pl.ANY),
        scratch_shapes=[pltpu.SemaphoreType.DMA((count,))],
        compiler_params=pltpu.CompilerParams(vmem_limit_bytes=VMEM_LIMIT),
        name="pick_blocks",
    )(picks, source)


def pick_near_kernel(axis, half, requests, source, out, sem):
    owner = lax.axis_index(axis)
    held = source.shape[0]
    base = owner // half * half

    def copies(d):
        first = second = found = jnp.int32(0)
        for j in range(requests.shape[1]):
            local = requests[base + d, j] - owner * held
            mine = (local >= 0) & (local < held)
            first = jnp.where(mine & (found == 0), local, first)
            second = jnp.where(mine & (found > 0), local, second)
            found = jnp.where(mine, 1, found)
        return [
            pltpu.make_async_copy(source.at[block], out.at[2 * d + t], sem.at[2 * d + t])
            for t, block in enumerate((first, second))
        ]

    started = []
    for d in range(half):
        started += copies(d)
        started[-2].start()
        started[-1].start()
    for copy in started:
        copy.wait()


def pick_near(axis, half, requests, source):
    count = 2 * half
    return pl.pallas_call(
        functools.partial(pick_near_kernel, axis, half),
        out_shape=jax.ShapeDtypeStruct((count,) + source.shape[1:], source.dtype),
        in_specs=[pl.BlockSpec(memory_space=SMEM), pl.BlockSpec(memory_space=VMEM)],
        out_specs=pl.BlockSpec(memory_space=pl.ANY),
        scratch_shapes=[pltpu.SemaphoreType.DMA((count,))],
        compiler_params=pltpu.CompilerParams(vmem_limit_bytes=VMEM_LIMIT),
        name="pick_near_blocks",
    )(requests, source)


def lay_strip(slots, is_near, near, far, plane, out, sem):
    needed = slots.shape[0]
    width = near.shape[3]
    for j in range(needed):
        columns = pl.ds(j * width, width)

        @pl.when(is_near[j] == 1)
        def _():
            pltpu.make_async_copy(near.at[slots[j], plane], out.at[:, columns], sem.at[j]).start()

        @pl.when(is_near[j] == 0)
        def _():
            pltpu.make_async_copy(far.at[slots[j]], out.at[:, columns], sem.at[j]).start()

    for j in range(needed):
        columns = pl.ds(j * width, width)
        pltpu.make_async_copy(far.at[slots[j]], out.at[:, columns], sem.at[j]).wait()


def dot(a, b, contract=((1,), (0,))):
    return lax.dot_general(
        a, b, (contract, ((), ())), precision=HIGHEST, preferred_element_type=jnp.float32
    )


def dot16(a, b):
    return jnp.dot(a, b, preferred_element_type=jnp.float32)


def split(x):
    high = x.astype(jnp.bfloat16)
    return high, (x - high.astype(jnp.float32)).astype(jnp.bfloat16)


def dot_left(table, x):
    half = table.shape[0] // 2
    high, low = split(x)
    return dot16(table[:half, :], high) + (dot16(table[half:, :], high) + dot16(table[:half, :], low))


def dot_right(x, table):
    half = table.shape[0] // 2
    high, low = split(x)
    return dot16(high, table[:half, :]) + (dot16(low, table[:half, :]) + dot16(high, table[half:, :]))


def stamp_place(stamp_rows, stamp_cols, stamp, columns):
    row = stamp_rows[stamp] - (SS // 2 + MARGIN)
    col = stamp_cols[stamp] - (SS // 2 + MARGIN)
    base = pl.multiple_of(jnp.minimum(col // 128 * 128, columns - 256), 128)
    return row, col - base, pl.ds(base, 256)


def inner_stamp(x, row, off, k):
    moved = pltpu.roll(x, lax.rem(32 * k - off - MARGIN + 512, 256), 1)[:, :128]
    return pltpu.roll(moved, x.shape[0] - row - MARGIN, 0)[:SS]


def science_kernel(stamp_rows, stamp_cols, science, variance, science_stamps, variance_stamps, variance_sum):
    _, columns = science.shape
    narrow = lax.broadcasted_iota(jnp.int32, (1, 128), 1)
    for g in range(stamp_rows.shape[0] // 4):
        sci = var = None
        for k in range(4):
            row, off, cols = stamp_place(stamp_rows, stamp_cols, g * 4 + k, columns)
            s = inner_stamp(science[:, cols], row, off, k)
            v = inner_stamp(variance[:, cols], row, off, k)
            here = narrow // 32 == k
            sci, var = (s, v) if k == 0 else (jnp.where(here, s, sci), jnp.where(here, v, var))
        science_stamps[g * SS : (g + 1) * SS, :] = sci
        variance_stamps[g * SS : (g + 1) * SS, :] = var
    variance_sum[...] = jnp.broadcast_to(total_of(variance[...]), (8, 128))


def image_kernel(stamp_rows, stamp_cols, slots, is_near, near, far, science_stamps, *refs):
    tables_in, refs = refs[:TABLES], refs[TABLES:]
    template, top, bottom, flat_x, stamp_weights, images, sem, table_sem = refs[:8]
    tables = refs[8:]
    loads = [
        pltpu.make_async_copy(source, table, table_sem.at[i])
        for i, (source, table) in enumerate(zip(tables_in, tables))
    ]
    for load in loads:
        load.start()
    across_ref, down_ref, left_ref, right_ref, back_left_ref, back_right_ref, ones_ref = tables
    lay_strip(slots, is_near, near, far, 0, template, sem)
    height, columns = template.shape
    top[...] = template[:HALO, :]
    bottom[...] = template[height - HALO :, :]
    stamps = stamp_rows.shape[0]
    groups = stamps // 4
    lane = lax.broadcasted_iota(jnp.int32, (1, 256), 1)

    windows, sciences, templates = [], [], []
    for g in range(groups):
        window = tmp = None
        for k in range(4):
            row, off, cols = stamp_place(stamp_rows, stamp_cols, g * 4 + k, columns)
            t = template[:, cols]
            to64 = lax.rem(64 * k - off + 256, 256)
            tw = pltpu.roll(pltpu.roll(t, to64, 1), lax.rem(height - row, height), 0)[:WROWS]
            t = inner_stamp(t, row, off, k)
            if k == 0:
                window, tmp = tw, t
            else:
                window = jnp.where(lane // 64 == k, tw, window)
                tmp = jnp.where(lane[:, :128] // 32 == k, t, tmp)
        windows.append(window)
        templates.append(tmp)
        sciences.append(science_stamps[g * SS : (g + 1) * SS, :])
    for load in loads:
        load.wait()

    high, low = split(jnp.concatenate(windows, 0))
    table_high, table_low = across_ref[:, : NFUN * 128], across_ref[:, NFUN * 128 :]
    across = dot16(high, table_high) + (dot16(low, table_high) + dot16(high, table_low))
    row = 0
    for b, downs in GROUPS:
        piece = jnp.concatenate(
            [across[g * WROWS : (g + 1) * WROWS, b * 128 : (b + 1) * 128] for g in range(groups)], 1
        )
        count = len(downs) * SS
        high = piece.astype(jnp.bfloat16).astype(jnp.float32)
        stacked = jnp.concatenate([high, piece - high, high], 0).astype(jnp.bfloat16)
        made = dot16(down_ref[row : row + count, :], stacked)
        for g in range(groups):
            images[g, row : row + count, :] = made[:, g * 128 : (g + 1) * 128]
        row += count
    for g in range(groups):
        images[g, NB * SS : (NB + 1) * SS, :] = sciences[g] - templates[g]
        images[g, (NB + 1) * SS :, :] = jnp.zeros(((31 - NB) * SS, 128), jnp.float32)
    wide = groups * 128
    for r in range(SS):
        x = jnp.concatenate([images[g, pl.ds(r, 32, stride=SS), :] for g in range(groups)], 1)
        high = x.astype(jnp.bfloat16).astype(jnp.float32)
        pair = jnp.concatenate([high, x - high], 0).astype(jnp.bfloat16)
        flat_x[:, r * wide : (r + 1) * wide] = pair

    sci = jnp.concatenate(sciences, 0)
    tmp = jnp.concatenate(templates, 0)
    side = groups * SS
    first = dot_left(left_ref, jnp.concatenate([sci, tmp], 1))
    first = jnp.concatenate(
        [
            jnp.concatenate([first[:side, :128], first[side:, :128]], 1),
            jnp.concatenate([first[:side, 128:], first[side:, 128:]], 1),
        ],
        0,
    )
    second = dot_right(first, right_ref)
    sre, sim = second[:side, :128], second[:side, 128:]
    tre, tim = second[side:, :128], second[side:, 128:]
    cross_re = sre * tre + sim * tim
    cross_im = sim * tre - sre * tim
    magnitude = jnp.sqrt(cross_re * cross_re + cross_im * cross_im)
    mean = dot_right(dot_left(ones_ref, magnitude), ones_ref) * (1.0 / (SS * SS))
    scaling = 1.0 / jnp.maximum(magnitude, 0.25 * (mean + 1e-06))
    unit = jnp.concatenate([cross_re * scaling, cross_im * scaling], 0)
    back = dot_left(back_left_ref, unit)
    surface = dot_right(jnp.concatenate([back[:side], back[side:]], 1), back_right_ref)
    narrow = lane[:, :128]
    for g in range(groups):
        best = jnp.max(surface[g * SS : (g + 1) * SS], axis=0, keepdims=True)
        best = jnp.broadcast_to(best, (8, 128))
        for step in (1, 2, 4, 8, 16):
            partner = jnp.where(
                narrow // step % 2 == 0,
                pltpu.roll(best, 128 - step, 1),
                pltpu.roll(best, step, 1),
            )
            best = jnp.maximum(best, partner)
        stamp_weights[g * 8 : (g + 1) * 8, :] = jnp.maximum(best, 0.1)


def normal_kernel(stamp_rows, stamp_cols, slots, is_near, near, far, flat_x, variance_stamps,
                  stamp_weights, variance_sum, template_variance, out, images, flat_y, sem, images_sem):
    load = pltpu.make_async_copy(flat_x, images, images_sem)
    load.start()
    lay_strip(slots, is_near, near, far, 1, template_variance, sem)
    _, columns = template_variance.shape
    stamps = stamp_rows.shape[0]
    groups = stamps // 4
    narrow = lax.broadcasted_iota(jnp.int32, (1, 128), 1)
    pixel_weight = []
    for g in range(groups):
        weight = None
        for k in range(4):
            row, off, cols = stamp_place(stamp_rows, stamp_cols, g * 4 + k, columns)
            w = inner_stamp(template_variance[:, cols], row, off, k)
            weight = w if k == 0 else jnp.where(narrow // 32 == k, w, weight)
        weight = variance_stamps[g * SS : (g + 1) * SS, :] + weight
        pixel_weight.append(stamp_weights[g * 8 : g * 8 + 1, :] / weight)
    pixel_weight = jnp.concatenate(pixel_weight, 1)
    wide = groups * 128
    load.wait()
    for r in range(SS):
        at = slice(r * wide, (r + 1) * wide)
        pair = images[:, at].astype(jnp.float32)
        y = (pair[:32] + pair[32:]) * pixel_weight[r : r + 1, :]
        high = y.astype(jnp.bfloat16).astype(jnp.float32)
        flat_y[:, at] = jnp.concatenate([high, y - high], 0).astype(jnp.bfloat16)
    gram = lax.dot_general(
        flat_y[...], images[...], (((1,), (1,)), ((), ())), preferred_element_type=jnp.float32
    )
    gram = widen(gram[:32] + gram[32:])
    out[:32, :] = gram + pltpu.roll(gram, 96, 1)
    total_t = total_of(template_variance[...])
    out[32:, :] = jnp.where(narrow == 0, variance_sum[...], jnp.broadcast_to(total_t, (8, 128)))


def eliminate(a):
    row_index = lax.broadcasted_iota(jnp.int32, (32, 1), 0)
    for k in range(NB):
        pivot_row = a[k : k + 1, :]
        pivot_row = pivot_row / pivot_row[:, k : k + 1]
        column = a[:, k : k + 1] - (row_index == k).astype(jnp.float32)
        a = a - column * pivot_row
    return jnp.where(row_index < NB, a[:, NB : NB + 1], 0.0)


def widen(x):
    return jnp.concatenate([x, jnp.zeros((x.shape[0], 128 - x.shape[1]), jnp.float32)], 1)


def total_of(x):
    return jnp.sum(jnp.sum(x, axis=0, keepdims=True), axis=1, keepdims=True)


def correlate(kernel_t, before, own, after, stack, bands, products, out, science):
    height, columns = own.shape
    reach = height + 2 * MARGIN
    lead = HALO - MARGIN
    tiles = columns // 128 + 1
    high = kernel_t.astype(jnp.bfloat16).astype(jnp.float32)
    low = kernel_t - high
    blank = jnp.zeros_like(high)
    high, low = jnp.concatenate([high, blank], 1), jnp.concatenate([low, blank], 1)
    taps = high + pltpu.roll(high, reach, 1) + pltpu.roll(low, 2 * reach, 1)
    for v in range(KS):
        w, j = v // FINE, v % FINE
        band = jnp.broadcast_to(taps[v : v + 1, :], (height, 256))
        band = pltpu.roll(band, 0, 1, stride=1, stride_axis=0)
        bands[w * height : (w + 1) * height, j * 256 : (j + 1) * 256] = band.astype(jnp.bfloat16)

    lane = lax.broadcasted_iota(jnp.int32, (1, 128), 1)
    rest = jnp.zeros((256 - 3 * reach, 128), jnp.float32)
    empty = jnp.zeros((reach, 128), jnp.float32)

    def tile(t):
        if t % tiles == tiles - 1:
            return empty
        at = slice(t % tiles * 128, (t % tiles + 1) * 128)
        return jnp.concatenate([before[:, at], own[:, at], after[:, at]], 0)[lead : lead + reach]

    left, here = tile(-1), tile(0)
    left_last = pltpu.roll(left, 1, 1)
    here_last = pltpu.roll(here, 1, 1)
    here_next = pltpu.roll(here, 127, 1)
    for t in range(tiles):
        right = tile(t + 1)
        right_last, right_next = pltpu.roll(right, 1, 1), pltpu.roll(right, 127, 1)
        moved = (
            jnp.where(lane < 1, left_last, here_last),
            here,
            jnp.where(lane < 127, here_next, right_next),
        )
        for j, x in enumerate(moved):
            high = x.astype(jnp.bfloat16).astype(jnp.float32)
            stack[j * 256 : (j + 1) * 256, t * 128 : (t + 1) * 128] = jnp.concatenate(
                [high, x - high, high, rest], 0
            ).astype(jnp.bfloat16)
        left_last, here, here_last, here_next = here_last, right, right_last, right_next
    chunk = 384 if tiles % 3 == 0 else 128
    for c in range(0, tiles * 128, chunk):
        at = slice(c, c + chunk)
        products[:, at] = jnp.dot(bands[...], stack[:, at], preferred_element_type=jnp.float32)

    def finish(g, carry):
        at = pl.multiple_of(g * 8, 8)

        def product(w):
            return products[pl.ds(w * height + at, 8), :]

        half = COARSE // 2
        total = product(half)
        for w in range(COARSE):
            if w != half:
                total = total + pltpu.roll(product(w), FINE * (half - w) % (tiles * 128), 1)
        total = total[:, :columns]
        rows = pl.ds(at, 8)
        out[rows, :] = total if science is None else science[rows, :] - total
        return carry

    lax.fori_loop(0, height // 8, finish, 0, unroll=True)


def first_kernel(pixels, p0, p1, p2, p3, science, before, own, after, lv, lu, left, right, back_left,
                 back_right, difference, top, bottom, filter_out, powers, stack, bands, products):
    sums = p0[...] + p1[...] + p2[...] + p3[...]
    coefficients = eliminate(sums[:32, :])
    mean_science = sums[32:33, 0:1] * (1.0 / pixels)
    mean_template = sums[32:33, 1:2] * (1.0 / pixels)
    kernel_t = dot_left(lv, coefficients * lu[...])
    v_index = lax.broadcasted_iota(jnp.int32, (32, 128), 0)
    u_index = lax.broadcasted_iota(jnp.int32, (32, 128), 1)
    kernel_t = kernel_t + ((v_index == MARGIN) & (u_index == MARGIN)).astype(jnp.float32)
    step = dot_left(left, kernel_t)
    both = dot_right(jnp.concatenate([step[:PD], step[PD:]], 1), right)
    re, im = both[:, :128], both[:, 128:]
    response = jnp.sqrt(
        (mean_science + mean_template) / (mean_science + mean_template * (re * re + im * im))
    )
    step = dot_left(back_left, response)
    filter_t = dot_right(jnp.concatenate([step[:32], step[32:]], 1), back_right)
    filter_out[...] = filter_t
    powers[0:1, :] = jnp.broadcast_to(total_of(kernel_t * kernel_t), (1, 128))
    powers[1:2, :] = jnp.broadcast_to(total_of(filter_t * filter_t), (1, 128))
    powers[2:, :] = jnp.zeros((6, 128), jnp.float32)
    correlate(kernel_t, before, own, after, stack, bands, products, difference, science)
    top[...] = difference[:HALO, :]
    bottom[...] = difference[difference.shape[0] - HALO :, :]


def second_kernel(filter_t, before, own, after, out, stack, bands, products):
    correlate(filter_t[...], before, own, after, stack, bands, products, out, None)


def correlation_scratch(height, columns):
    return [
        pltpu.VMEM((FINE * 256, columns + 128), jnp.bfloat16),
        pltpu.VMEM((COARSE * height, FINE * 256), jnp.bfloat16),
        pltpu.VMEM((COARSE * height, columns + 128), jnp.float32),
    ]


def edges(top, bottom, axis):
    devices = lax.axis_size(axis)
    up = [(i, i + 1) for i in range(devices - 1)]
    down = [(j, i) for i, j in up]
    before = lax.ppermute(bottom, axis, up)
    after = lax.ppermute(top, axis, down)
    return before, after


def per_device(science, variance, template_blocks, requests, stamp_rows, stamp_cols):
    height, columns = science.shape
    strips = lax.axis_size("det")
    device = lax.axis_index("det")
    held = template_blocks.shape[0]

    half = strips // 2
    here = device // half
    partner = lax.rem(device + half, strips)
    served = lax.dynamic_slice_in_dim(requests, here * half, half, 0)

    def picks_of(owner):
        local = served - owner * held
        mine = (local >= 0) & (local < held)
        again = mine & jnp.pad(mine[:, :-1], ((0, 0), (1, 0)))
        first = jnp.sum(jnp.where(mine & ~again, local, 0), axis=1)
        second = jnp.sum(jnp.where(again, local, 0), axis=1)
        return jnp.stack([first, second], axis=1).reshape(-1).astype(jnp.int32)

    wanted = lax.dynamic_index_in_dim(requests, device, 0, keepdims=False)
    owner = wanted // held
    repeat = owner == jnp.concatenate([owner[:1] - 1, owner[:-1]])
    slots = (owner % half * 2 + repeat).astype(jnp.int32)
    is_near = (owner // half == here).astype(jnp.int32)

    across_halves = [(i, (i + half) % strips) for i in range(strips)]
    halves = [list(range(half)), list(range(half, strips))]

    def serve(x):
        return lax.all_to_all(x, "det", 0, 0, axis_index_groups=halves, tiled=True)

    partner_blocks = lax.ppermute(template_blocks, "det", across_halves)
    near = serve(pick_near("det", half, requests, template_blocks))
    far_picks = picks_of(partner)
    vmem, smem, anywhere = (pl.BlockSpec(memory_space=m) for m in (VMEM, SMEM, pl.ANY))
    rows, cols = stamp_rows[0], stamp_cols[0]
    stamps = rows.shape[0]
    flat = SS * SS * stamps
    strip = jax.ShapeDtypeStruct((height, columns), jnp.float32)
    row = jax.ShapeDtypeStruct((8, 128), jnp.float32)
    edge = jax.ShapeDtypeStruct((HALO, columns), jnp.float32)
    tables = [jnp.asarray(t) for t in (across_table(), down_table(), *dft_blocks())]
    params = pltpu.CompilerParams(vmem_limit_bytes=VMEM_LIMIT)
    small = pltpu.CompilerParams(vmem_limit_bytes=VMEM_SMALL)
    stamp_rows_shape = jax.ShapeDtypeStruct((stamps // 4 * SS, 128), jnp.float32)
    science_stamps, variance_stamps, variance_sum = pl.pallas_call(
        science_kernel,
        out_shape=[stamp_rows_shape, stamp_rows_shape, row],
        in_specs=[smem] * 2 + [vmem] * 2,
        out_specs=[vmem] * 3,
        compiler_params=params,
        name="science_stamps",
    )(rows, cols, science, variance)
    partner_blocks, near, slots, is_near, science_stamps, variance_stamps, variance_sum = (
        lax.optimization_barrier(
            (partner_blocks, near, slots, is_near, science_stamps, variance_stamps, variance_sum)
        )
    )
    far_image = serve(pick(far_picks, partner_blocks, 0))
    picked_variance, far_image = lax.optimization_barrier(
        (pick(far_picks, partner_blocks, 1), far_image)
    )
    far_variance = serve(picked_variance)

    template_image, template_top, template_bottom, flat_x, stamp_weights = pl.pallas_call(
        image_kernel,
        out_shape=[
            strip,
            edge,
            edge,
            jax.ShapeDtypeStruct((64, flat), jnp.bfloat16),
            jax.ShapeDtypeStruct((stamps // 4 * 8, 128), jnp.float32),
        ],
        in_specs=[smem] * 4 + [anywhere] * 2 + [vmem] + [anywhere] * TABLES,
        out_specs=[vmem] * 5,
        scratch_shapes=[
            pltpu.VMEM((stamps // 4, 32 * SS, 128), jnp.float32),
            pltpu.SemaphoreType.DMA((wanted.shape[0],)),
            pltpu.SemaphoreType.DMA((TABLES,)),
            *[pltpu.VMEM(t.shape, t.dtype) for t in tables],
        ],
        compiler_params=params,
        name="stamp_images",
    )(rows, cols, slots, is_near, near, far_image, science_stamps, *tables)
    before, after = edges(template_top, template_bottom, "det")
    template_variance, partial = pl.pallas_call(
        normal_kernel,
        out_shape=[strip, jax.ShapeDtypeStruct((40, 128), jnp.float32)],
        in_specs=[smem] * 4 + [anywhere] * 3 + [vmem] * 3,
        out_specs=[vmem] * 2,
        scratch_shapes=[
            pltpu.VMEM((64, flat), jnp.bfloat16),
            pltpu.VMEM((64, flat), jnp.bfloat16),
            pltpu.SemaphoreType.DMA((wanted.shape[0],)),
            pltpu.SemaphoreType.DMA,
        ],
        compiler_params=params,
        name="normal_equations",
    )(rows, cols, slots, is_near, near, far_variance, flat_x, variance_stamps, stamp_weights, variance_sum)
    partials = [partial]
    for shift in range(1, CPER):
        partials.append(
            lax.ppermute(
                partial,
                "det",
                [(i, i // CPER * CPER + (i + shift) % CPER) for i in range(strips)],
            )
        )
    pixels = CPER * height * columns
    tables = [jnp.asarray(t) for t in (*basis_tables(), *filter_tables())]
    difference, top, bottom, filter_t, powers = pl.pallas_call(
        functools.partial(first_kernel, pixels),
        out_shape=[
            strip,
            edge,
            edge,
            jax.ShapeDtypeStruct((32, 128), jnp.float32),
            row,
        ],
        in_specs=[vmem] * 14,
        out_specs=[vmem] * 5,
        scratch_shapes=correlation_scratch(height, columns),
        compiler_params=small,
        name="solve_and_subtract",
    )(*partials, science, before, template_image, after, *tables)
    before, after = edges(top, bottom, "det")
    decorrelated_variance = powers[1:2, :1] * (variance + template_variance * powers[:1, :1])
    decorrelated = pl.pallas_call(
        second_kernel,
        out_shape=strip,
        in_specs=[vmem] * 4,
        out_specs=vmem,
        scratch_shapes=correlation_scratch(height, columns),
        compiler_params=small,
        name="decorrelate",
    )(filter_t, before, difference, after)
    return (decorrelated, decorrelated_variance)


def solution(mesh):
    placed = (
        P(("group", "det"), None),
        P(("group", "det"), None),
        P(("group", "det"), None, None, None),
        P("group", None),
        P(("group", "det"), None),
        P(("group", "det"), None),
    )
    return jax.shard_map(
        per_device,
        mesh=mesh,
        in_specs=placed,
        out_specs=(P(("group", "det"), None), P(("group", "det"), None)),
        check_vma=False,
    )
```

```python
import functools

import jax
import jax.numpy as jnp
import numpy as np
from jax import lax
from jax.experimental import pallas as pl
from jax.experimental.pallas import tpu as pltpu
from jax.sharding import PartitionSpec as P

CPER = 4
SS = 32
KS = 21
PD = 32
MARGIN = KS // 2
HALO = 16
EXTENT = SS + 2 * MARGIN

HIGHEST = lax.Precision.HIGHEST
GAUSS_WIDTHS = (0.7, 1.5, 3.0)
GAUSS_DEGREES = (4, 2, 2)
VMEM_LIMIT = 60 * 1024 * 1024
VMEM_SMALL = 32 * 1024 * 1024
VMEM = pltpu.MemorySpace.VMEM
SMEM = pltpu.MemorySpace.SMEM


def line_functions():
    tap_grid = np.arange(KS, dtype=np.float64) - MARGIN
    raw_list = []
    for spread, degree in zip(GAUSS_WIDTHS, GAUSS_DEGREES):
        gaussian = np.exp(-tap_grid * tap_grid / (2.0 * spread * spread))
        for degree_power in range(degree + 1):
            raw_list.append(gaussian * tap_grid**degree_power)
    result = []
    for vector in raw_list:
        for earlier in result:
            vector = vector - np.sum(vector * earlier) * earlier
        result.append(vector / np.sqrt(np.sum(vector * vector)))
    return np.stack(result)


def images_by_across():
    groups = []
    base = 0
    for degree in GAUSS_DEGREES:
        for inner in range(degree + 1):
            groups.append((base + inner, [base + outer for outer in range(degree + 1 - inner)]))
        base += degree + 1
    return groups


LINE = line_functions()
GROUPS = images_by_across()
PAIRS = [(a, b) for b, downs in GROUPS for a in downs]
NB = len(PAIRS)
NFUN = LINE.shape[0]
WROWS = 64
TABLES = 7
FINE, COARSE = 3, 7


def block_diag(matrix, times):
    rows, cols = matrix.shape
    out = np.zeros((rows * times, cols * times))
    for k in range(times):
        out[k * rows : (k + 1) * rows, k * cols : (k + 1) * cols] = matrix
    return out


def across_table():
    table = np.zeros((256, NFUN * 128))
    for b in range(NFUN):
        for k in range(4):
            for c in range(SS):
                table[64 * k + c : 64 * k + c + KS, b * 128 + 32 * k + c] = LINE[b]
    return np.concatenate(split_host(table), 1)


def split_host(table):
    high = table.astype(np.float32).astype(jnp.bfloat16)
    return high, (table - high.astype(np.float64)).astype(np.float32).astype(jnp.bfloat16)


def down_table():
    table = np.zeros((NB * SS, WROWS))
    for image, (a, _) in enumerate(PAIRS):
        for r in range(SS):
            table[image * SS + r, r : r + KS] = LINE[a]
    high, low = split_host(table)
    return np.concatenate([high, high, low], 1)


def dft_blocks():
    grid = np.outer(np.arange(SS), np.arange(SS)) % SS
    c, s = np.cos(2 * np.pi * grid / SS), np.sin(2 * np.pi * grid / SS)
    c, s = block_diag(c, 4), block_diag(s, 4)
    ones = block_diag(np.ones((SS, SS)), 4)
    left = np.concatenate([c, s], 0)
    right = np.block([[c, -s], [-s, -c]])
    back_left = np.block([[c, -s], [s, c]])
    back_right = np.concatenate([c, -s], 0) / (SS * SS)
    return [np.concatenate(split_host(x), 0) for x in (left, right, back_left, back_right, ones)]


def basis_tables():
    lv, lu = np.zeros((32, 32)), np.zeros((32, 128))
    for image, (a, b) in enumerate(PAIRS):
        lv[:KS, image] = LINE[b]
        lu[image, :KS] = LINE[a]
    return np.concatenate(split_host(lv), 0), lu.astype(np.float32)


def filter_tables():
    grid = np.outer(np.arange(PD), np.arange(KS) - MARGIN)
    c, s = np.zeros((PD, 32)), np.zeros((PD, 32))
    c[:, :KS], s[:, :KS] = np.cos(2 * np.pi * grid / PD), np.sin(2 * np.pi * grid / PD)
    cr, sr = np.zeros((128, 128)), np.zeros((128, 128))
    cr[:32, :PD], sr[:32, :PD] = c.T, s.T
    left = np.concatenate([c, s], 0)
    right = np.block([[cr, -sr], [-sr, -cr]])
    back_left = np.concatenate([c.T, s.T], 0) / (PD * PD)
    back_c, back_s = np.zeros((128, 128)), np.zeros((128, 128))
    back_c[:PD, :32], back_s[:PD, :32] = c, s
    back_right = np.concatenate([back_c, -back_s], 0)
    return [np.concatenate(split_host(x), 0) for x in (left, right, back_left, back_right)]


def pick_kernel(plane, picks, source, out, sem):
    count = out.shape[0]

    def copy(k):
        block = source.at[picks[k]] if plane is None else source.at[picks[k], plane]
        return pltpu.make_async_copy(block, out.at[k], sem.at[k])

    def start(k, carry):
        copy(k).start()
        return carry

    def finish(k, carry):
        copy(k).wait()
        return carry

    lax.fori_loop(0, count, start, 0)
    lax.fori_loop(0, count, finish, 0)


def pick(picks, source, plane=None):
    count = picks.shape[0]
    shape = source.shape[1:] if plane is None else source.shape[2:]
    return pl.pallas_call(
        functools.partial(pick_kernel, plane),
        out_shape=jax.ShapeDtypeStruct((count,) + shape, source.dtype),
        in_specs=[pl.BlockSpec(memory_space=SMEM), pl.BlockSpec(memory_space=VMEM)],
        out_specs=pl.BlockSpec(memory_space=pl.ANY),
        scratch_shapes=[pltpu.SemaphoreType.DMA((count,))],
        compiler_params=pltpu.CompilerParams(vmem_limit_bytes=VMEM_LIMIT),
        name="pick_blocks",
    )(picks, source)


def pick_near_kernel(axis, half, requests, source, out, sem):
    owner = lax.axis_index(axis)
    held = source.shape[0]
    base = owner // half * half

    def copies(d):
        first = second = found = jnp.int32(0)
        for j in range(requests.shape[1]):
            local = requests[base + d, j] - owner * held
            mine = (local >= 0) & (local < held)
            first = jnp.where(mine & (found == 0), local, first)
            second = jnp.where(mine & (found > 0), local, second)
            found = jnp.where(mine, 1, found)
        return [
            pltpu.make_async_copy(source.at[block], out.at[2 * d + t], sem.at[2 * d + t])
            for t, block in enumerate((first, second))
        ]

    started = []
    for d in range(half):
        started += copies(d)
        started[-2].start()
        started[-1].start()
    for copy in started:
        copy.wait()


def pick_near(axis, half, requests, source):
    count = 2 * half
    return pl.pallas_call(
        functools.partial(pick_near_kernel, axis, half),
        out_shape=jax.ShapeDtypeStruct((count,) + source.shape[1:], source.dtype),
        in_specs=[pl.BlockSpec(memory_space=SMEM), pl.BlockSpec(memory_space=VMEM)],
        out_specs=pl.BlockSpec(memory_space=pl.ANY),
        scratch_shapes=[pltpu.SemaphoreType.DMA((count,))],
        compiler_params=pltpu.CompilerParams(vmem_limit_bytes=VMEM_LIMIT),
        name="pick_near_blocks",
    )(requests, source)


def lay_strip(slots, is_near, near, far, plane, out, sem):
    needed = slots.shape[0]
    width = near.shape[3]
    for j in range(needed):
        columns = pl.ds(j * width, width)

        @pl.when(is_near[j] == 1)
        def _():
            pltpu.make_async_copy(near.at[slots[j], plane], out.at[:, columns], sem.at[j]).start()

        @pl.when(is_near[j] == 0)
        def _():
            pltpu.make_async_copy(far.at[slots[j]], out.at[:, columns], sem.at[j]).start()

    for j in range(needed):
        columns = pl.ds(j * width, width)
        pltpu.make_async_copy(far.at[slots[j]], out.at[:, columns], sem.at[j]).wait()


def dot(a, b, contract=((1,), (0,))):
    return lax.dot_general(
        a, b, (contract, ((), ())), precision=HIGHEST, preferred_element_type=jnp.float32
    )


def dot16(a, b):
    return jnp.dot(a, b, preferred_element_type=jnp.float32)


def split(x):
    high = x.astype(jnp.bfloat16)
    return high, (x - high.astype(jnp.float32)).astype(jnp.bfloat16)


def dot_left(table, x):
    half = table.shape[0] // 2
    high, low = split(x)
    return dot16(table[:half, :], high) + (dot16(table[half:, :], high) + dot16(table[:half, :], low))


def dot_right(x, table):
    half = table.shape[0] // 2
    high, low = split(x)
    return dot16(high, table[:half, :]) + (dot16(low, table[:half, :]) + dot16(high, table[half:, :]))


def stamp_place(stamp_rows, stamp_cols, stamp, columns):
    row = stamp_rows[stamp] - (SS // 2 + MARGIN)
    col = stamp_cols[stamp] - (SS // 2 + MARGIN)
    base = pl.multiple_of(jnp.minimum(col // 128 * 128, columns - 256), 128)
    return row, col - base, pl.ds(base, 256)


def inner_stamp(x, row, off, k):
    moved = pltpu.roll(x, lax.rem(32 * k - off - MARGIN + 512, 256), 1)[:, :128]
    return pltpu.roll(moved, x.shape[0] - row - MARGIN, 0)[:SS]


def science_kernel(stamp_rows, stamp_cols, science, variance, science_stamps, variance_stamps, variance_sum):
    _, columns = science.shape
    narrow = lax.broadcasted_iota(jnp.int32, (1, 128), 1)
    for g in range(stamp_rows.shape[0] // 4):
        sci = var = None
        for k in range(4):
            row, off, cols = stamp_place(stamp_rows, stamp_cols, g * 4 + k, columns)
            s = inner_stamp(science[:, cols], row, off, k)
            v = inner_stamp(variance[:, cols], row, off, k)
            here = narrow // 32 == k
            sci, var = (s, v) if k == 0 else (jnp.where(here, s, sci), jnp.where(here, v, var))
        science_stamps[g * SS : (g + 1) * SS, :] = sci
        variance_stamps[g * SS : (g + 1) * SS, :] = var
    variance_sum[...] = jnp.broadcast_to(total_of(variance[...]), (8, 128))


def image_kernel(stamp_rows, stamp_cols, slots, is_near, near, far, science_stamps, *refs):
    tables_in, refs = refs[:TABLES], refs[TABLES:]
    template, top, bottom, flat_x, stamp_weights, images, sem, table_sem = refs[:8]
    tables = refs[8:]
    loads = [
        pltpu.make_async_copy(source, table, table_sem.at[i])
        for i, (source, table) in enumerate(zip(tables_in, tables))
    ]
    for load in loads:
        load.start()
    across_ref, down_ref, left_ref, right_ref, back_left_ref, back_right_ref, ones_ref = tables
    lay_strip(slots, is_near, near, far, 0, template, sem)
    height, columns = template.shape
    top[...] = template[:HALO, :]
    bottom[...] = template[height - HALO :, :]
    stamps = stamp_rows.shape[0]
    groups = stamps // 4
    lane = lax.broadcasted_iota(jnp.int32, (1, 256), 1)

    windows, sciences, templates = [], [], []
    for g in range(groups):
        window = tmp = None
        for k in range(4):
            row, off, cols = stamp_place(stamp_rows, stamp_cols, g * 4 + k, columns)
            t = template[:, cols]
            to64 = lax.rem(64 * k - off + 256, 256)
            tw = pltpu.roll(pltpu.roll(t, to64, 1), lax.rem(height - row, height), 0)[:WROWS]
            t = inner_stamp(t, row, off, k)
            if k == 0:
                window, tmp = tw, t
            else:
                window = jnp.where(lane // 64 == k, tw, window)
                tmp = jnp.where(lane[:, :128] // 32 == k, t, tmp)
        windows.append(window)
        templates.append(tmp)
        sciences.append(science_stamps[g * SS : (g + 1) * SS, :])
    for load in loads:
        load.wait()

    high, low = split(jnp.concatenate(windows, 0))
    table_high, table_low = across_ref[:, : NFUN * 128], across_ref[:, NFUN * 128 :]
    across = dot16(high, table_high) + (dot16(low, table_high) + dot16(high, table_low))
    row = 0
    for b, downs in GROUPS:
        piece = jnp.concatenate(
            [across[g * WROWS : (g + 1) * WROWS, b * 128 : (b + 1) * 128] for g in range(groups)], 1
        )
        count = len(downs) * SS
        high = piece.astype(jnp.bfloat16).astype(jnp.float32)
        stacked = jnp.concatenate([high, piece - high, high], 0).astype(jnp.bfloat16)
        made = dot16(down_ref[row : row + count, :], stacked)
        for g in range(groups):
            images[g, row : row + count, :] = made[:, g * 128 : (g + 1) * 128]
        row += count
    for g in range(groups):
        images[g, NB * SS : (NB + 1) * SS, :] = sciences[g] - templates[g]
        images[g, (NB + 1) * SS :, :] = jnp.zeros(((31 - NB) * SS, 128), jnp.float32)
    wide = groups * 128
    for r in range(SS):
        x = jnp.concatenate([images[g, pl.ds(r, 32, stride=SS), :] for g in range(groups)], 1)
        high = x.astype(jnp.bfloat16).astype(jnp.float32)
        pair = jnp.concatenate([high, x - high], 0).astype(jnp.bfloat16)
        flat_x[:, r * wide : (r + 1) * wide] = pair

    sci = jnp.concatenate(sciences, 0)
    tmp = jnp.concatenate(templates, 0)
    side = groups * SS
    first = dot_left(left_ref, jnp.concatenate([sci, tmp], 1))
    first = jnp.concatenate(
        [
            jnp.concatenate([first[:side, :128], first[side:, :128]], 1),
            jnp.concatenate([first[:side, 128:], first[side:, 128:]], 1),
        ],
        0,
    )
    second = dot_right(first, right_ref)
    sre, sim = second[:side, :128], second[:side, 128:]
    tre, tim = second[side:, :128], second[side:, 128:]
    cross_re = sre * tre + sim * tim
    cross_im = sim * tre - sre * tim
    magnitude = jnp.sqrt(cross_re * cross_re + cross_im * cross_im)
    mean = dot_right(dot_left(ones_ref, magnitude), ones_ref) * (1.0 / (SS * SS))
    scaling = 1.0 / jnp.maximum(magnitude, 0.25 * (mean + 1e-06))
    unit = jnp.concatenate([cross_re * scaling, cross_im * scaling], 0)
    back = dot_left(back_left_ref, unit)
    surface = dot_right(jnp.concatenate([back[:side], back[side:]], 1), back_right_ref)
    narrow = lane[:, :128]
    for g in range(groups):
        best = jnp.max(surface[g * SS : (g + 1) * SS], axis=0, keepdims=True)
        best = jnp.broadcast_to(best, (8, 128))
        for step in (1, 2, 4, 8, 16):
            partner = jnp.where(
                narrow // step % 2 == 0,
                pltpu.roll(best, 128 - step, 1),
                pltpu.roll(best, step, 1),
            )
            best = jnp.maximum(best, partner)
        stamp_weights[g * 8 : (g + 1) * 8, :] = jnp.maximum(best, 0.1)


def normal_kernel(stamp_rows, stamp_cols, slots, is_near, near, far, flat_x, variance_stamps,
                  stamp_weights, variance_sum, template_variance, out, images, flat_y, sem, images_sem):
    load = pltpu.make_async_copy(flat_x, images, images_sem)
    load.start()
    lay_strip(slots, is_near, near, far, 1, template_variance, sem)
    _, columns = template_variance.shape
    stamps = stamp_rows.shape[0]
    groups = stamps // 4
    narrow = lax.broadcasted_iota(jnp.int32, (1, 128), 1)
    pixel_weight = []
    for g in range(groups):
        weight = None
        for k in range(4):
            row, off, cols = stamp_place(stamp_rows, stamp_cols, g * 4 + k, columns)
            w = inner_stamp(template_variance[:, cols], row, off, k)
            weight = w if k == 0 else jnp.where(narrow // 32 == k, w, weight)
        weight = variance_stamps[g * SS : (g + 1) * SS, :] + weight
        pixel_weight.append(stamp_weights[g * 8 : g * 8 + 1, :] / weight)
    pixel_weight = jnp.concatenate(pixel_weight, 1)
    wide = groups * 128
    load.wait()
    for r in range(SS):
        at = slice(r * wide, (r + 1) * wide)
        pair = images[:, at].astype(jnp.float32)
        y = (pair[:32] + pair[32:]) * pixel_weight[r : r + 1, :]
        high = y.astype(jnp.bfloat16).astype(jnp.float32)
        flat_y[:, at] = jnp.concatenate([high, y - high], 0).astype(jnp.bfloat16)
    gram = lax.dot_general(
        flat_y[...], images[...], (((1,), (1,)), ((), ())), preferred_element_type=jnp.float32
    )
    gram = widen(gram[:32] + gram[32:])
    out[:32, :] = gram + pltpu.roll(gram, 96, 1)
    total_t = total_of(template_variance[...])
    out[32:, :] = jnp.where(narrow == 0, variance_sum[...], jnp.broadcast_to(total_t, (8, 128)))


def eliminate(a):
    row_index = lax.broadcasted_iota(jnp.int32, (32, 1), 0)
    for k in range(NB):
        pivot_row = a[k : k + 1, :]
        pivot_row = pivot_row / pivot_row[:, k : k + 1]
        column = a[:, k : k + 1] - (row_index == k).astype(jnp.float32)
        a = a - column * pivot_row
    return jnp.where(row_index < NB, a[:, NB : NB + 1], 0.0)


def widen(x):
    return jnp.concatenate([x, jnp.zeros((x.shape[0], 128 - x.shape[1]), jnp.float32)], 1)


def total_of(x):
    return jnp.sum(jnp.sum(x, axis=0, keepdims=True), axis=1, keepdims=True)


def correlate(kernel_t, before, own, after, stack, bands, products, out, science):
    height, columns = own.shape
    reach = height + 2 * MARGIN
    lead = HALO - MARGIN
    tiles = columns // 128 + 1
    high = kernel_t.astype(jnp.bfloat16).astype(jnp.float32)
    low = kernel_t - high
    blank = jnp.zeros_like(high)
    high, low = jnp.concatenate([high, blank], 1), jnp.concatenate([low, blank], 1)
    taps = high + pltpu.roll(high, reach, 1) + pltpu.roll(low, 2 * reach, 1)
    for v in range(KS):
        w, j = v // FINE, v % FINE
        band = jnp.broadcast_to(taps[v : v + 1, :], (height, 256))
        band = pltpu.roll(band, 0, 1, stride=1, stride_axis=0)
        bands[w * height : (w + 1) * height, j * 256 : (j + 1) * 256] = band.astype(jnp.bfloat16)

    lane = lax.broadcasted_iota(jnp.int32, (1, 128), 1)
    rest = jnp.zeros((256 - 3 * reach, 128), jnp.float32)
    empty = jnp.zeros((reach, 128), jnp.float32)

    def tile(t):
        if t % tiles == tiles - 1:
            return empty
        at = slice(t % tiles * 128, (t % tiles + 1) * 128)
        return jnp.concatenate([before[:, at], own[:, at], after[:, at]], 0)[lead : lead + reach]

    left, here = tile(-1), tile(0)
    left_last = pltpu.roll(left, 1, 1)
    here_last = pltpu.roll(here, 1, 1)
    here_next = pltpu.roll(here, 127, 1)
    for t in range(tiles):
        right = tile(t + 1)
        right_last, right_next = pltpu.roll(right, 1, 1), pltpu.roll(right, 127, 1)
        moved = (
            jnp.where(lane < 1, left_last, here_last),
            here,
            jnp.where(lane < 127, here_next, right_next),
        )
        for j, x in enumerate(moved):
            high = x.astype(jnp.bfloat16).astype(jnp.float32)
            stack[j * 256 : (j + 1) * 256, t * 128 : (t + 1) * 128] = jnp.concatenate(
                [high, x - high, high, rest], 0
            ).astype(jnp.bfloat16)
        left_last, here, here_last, here_next = here_last, right, right_last, right_next
    chunk = 1408 if tiles % 11 == 0 else 128
    for c in range(0, tiles * 128, chunk):
        at = slice(c, c + chunk)
        products[:, at] = jnp.dot(bands[...], stack[:, at], preferred_element_type=jnp.float32)

    def finish(g, carry):
        at = pl.multiple_of(g * 8, 8)

        def product(w):
            return products[pl.ds(w * height + at, 8), :]

        half = COARSE // 2
        total = product(half)
        for w in range(COARSE):
            if w != half:
                total = total + pltpu.roll(product(w), FINE * (half - w) % (tiles * 128), 1)
        total = total[:, :columns]
        rows = pl.ds(at, 8)
        out[rows, :] = total if science is None else science[rows, :] - total
        return carry

    lax.fori_loop(0, height // 8, finish, 0, unroll=True)


def first_kernel(pixels, p0, p1, p2, p3, science, before, own, after, lv, lu, left, right, back_left,
                 back_right, difference, top, bottom, filter_out, powers, stack, bands, products):
    sums = p0[...] + p1[...] + p2[...] + p3[...]
    coefficients = eliminate(sums[:32, :])
    mean_science = sums[32:33, 0:1] * (1.0 / pixels)
    mean_template = sums[32:33, 1:2] * (1.0 / pixels)
    kernel_t = dot_left(lv, coefficients * lu[...])
    v_index = lax.broadcasted_iota(jnp.int32, (32, 128), 0)
    u_index = lax.broadcasted_iota(jnp.int32, (32, 128), 1)
    kernel_t = kernel_t + ((v_index == MARGIN) & (u_index == MARGIN)).astype(jnp.float32)
    step = dot_left(left, kernel_t)
    both = dot_right(jnp.concatenate([step[:PD], step[PD:]], 1), right)
    re, im = both[:, :128], both[:, 128:]
    response = jnp.sqrt(
        (mean_science + mean_template) / (mean_science + mean_template * (re * re + im * im))
    )
    step = dot_left(back_left, response)
    filter_t = dot_right(jnp.concatenate([step[:32], step[32:]], 1), back_right)
    filter_out[...] = filter_t
    powers[0:1, :] = jnp.broadcast_to(total_of(kernel_t * kernel_t), (1, 128))
    powers[1:2, :] = jnp.broadcast_to(total_of(filter_t * filter_t), (1, 128))
    powers[2:, :] = jnp.zeros((6, 128), jnp.float32)
    correlate(kernel_t, before, own, after, stack, bands, products, difference, science)
    top[...] = difference[:HALO, :]
    bottom[...] = difference[difference.shape[0] - HALO :, :]


def second_kernel(filter_t, before, own, after, out, stack, bands, products):
    correlate(filter_t[...], before, own, after, stack, bands, products, out, None)


def correlation_scratch(height, columns):
    return [
        pltpu.VMEM((FINE * 256, columns + 128), jnp.bfloat16),
        pltpu.VMEM((COARSE * height, FINE * 256), jnp.bfloat16),
        pltpu.VMEM((COARSE * height, columns + 128), jnp.float32),
    ]


def edges(top, bottom, axis):
    devices = lax.axis_size(axis)
    up = [(i, i + 1) for i in range(devices - 1)]
    down = [(j, i) for i, j in up]
    before = lax.ppermute(bottom, axis, up)
    after = lax.ppermute(top, axis, down)
    return before, after


def per_device(science, variance, template_blocks, requests, stamp_rows, stamp_cols):
    height, columns = science.shape
    strips = lax.axis_size("det")
    device = lax.axis_index("det")
    held = template_blocks.shape[0]

    half = strips // 2
    here = device // half
    partner = lax.rem(device + half, strips)
    served = lax.dynamic_slice_in_dim(requests, here * half, half, 0)

    def picks_of(owner):
        local = served - owner * held
        mine = (local >= 0) & (local < held)
        again = mine & jnp.pad(mine[:, :-1], ((0, 0), (1, 0)))
        first = jnp.sum(jnp.where(mine & ~again, local, 0), axis=1)
        second = jnp.sum(jnp.where(again, local, 0), axis=1)
        return jnp.stack([first, second], axis=1).reshape(-1).astype(jnp.int32)

    wanted = lax.dynamic_index_in_dim(requests, device, 0, keepdims=False)
    owner = wanted // held
    repeat = owner == jnp.concatenate([owner[:1] - 1, owner[:-1]])
    slots = (owner % half * 2 + repeat).astype(jnp.int32)
    is_near = (owner // half == here).astype(jnp.int32)

    across_halves = [(i, (i + half) % strips) for i in range(strips)]
    halves = [list(range(half)), list(range(half, strips))]

    def serve(x):
        return lax.all_to_all(x, "det", 0, 0, axis_index_groups=halves, tiled=True)

    partner_blocks = lax.ppermute(template_blocks, "det", across_halves)
    near = serve(pick_near("det", half, requests, template_blocks))
    far_picks = picks_of(partner)
    vmem, smem, anywhere = (pl.BlockSpec(memory_space=m) for m in (VMEM, SMEM, pl.ANY))
    rows, cols = stamp_rows[0], stamp_cols[0]
    stamps = rows.shape[0]
    flat = SS * SS * stamps
    strip = jax.ShapeDtypeStruct((height, columns), jnp.float32)
    row = jax.ShapeDtypeStruct((8, 128), jnp.float32)
    edge = jax.ShapeDtypeStruct((HALO, columns), jnp.float32)
    tables = [jnp.asarray(t) for t in (across_table(), down_table(), *dft_blocks())]
    params = pltpu.CompilerParams(vmem_limit_bytes=VMEM_LIMIT)
    small = pltpu.CompilerParams(vmem_limit_bytes=VMEM_SMALL)
    stamp_rows_shape = jax.ShapeDtypeStruct((stamps // 4 * SS, 128), jnp.float32)
    science_stamps, variance_stamps, variance_sum = pl.pallas_call(
        science_kernel,
        out_shape=[stamp_rows_shape, stamp_rows_shape, row],
        in_specs=[smem] * 2 + [vmem] * 2,
        out_specs=[vmem] * 3,
        compiler_params=params,
        name="science_stamps",
    )(rows, cols, science, variance)
    partner_blocks, near, slots, is_near, science_stamps, variance_stamps, variance_sum = (
        lax.optimization_barrier(
            (partner_blocks, near, slots, is_near, science_stamps, variance_stamps, variance_sum)
        )
    )
    far_image = serve(pick(far_picks, partner_blocks, 0))
    picked_variance, far_image = lax.optimization_barrier(
        (pick(far_picks, partner_blocks, 1), far_image)
    )
    far_variance = serve(picked_variance)

    template_image, template_top, template_bottom, flat_x, stamp_weights = pl.pallas_call(
        image_kernel,
        out_shape=[
            strip,
            edge,
            edge,
            jax.ShapeDtypeStruct((64, flat), jnp.bfloat16),
            jax.ShapeDtypeStruct((stamps // 4 * 8, 128), jnp.float32),
        ],
        in_specs=[smem] * 4 + [anywhere] * 2 + [vmem] + [anywhere] * TABLES,
        out_specs=[vmem] * 5,
        scratch_shapes=[
            pltpu.VMEM((stamps // 4, 32 * SS, 128), jnp.float32),
            pltpu.SemaphoreType.DMA((wanted.shape[0],)),
            pltpu.SemaphoreType.DMA((TABLES,)),
            *[pltpu.VMEM(t.shape, t.dtype) for t in tables],
        ],
        compiler_params=params,
        name="stamp_images",
    )(rows, cols, slots, is_near, near, far_image, science_stamps, *tables)
    before, after = edges(template_top, template_bottom, "det")
    template_variance, partial = pl.pallas_call(
        normal_kernel,
        out_shape=[strip, jax.ShapeDtypeStruct((40, 128), jnp.float32)],
        in_specs=[smem] * 4 + [anywhere] * 3 + [vmem] * 3,
        out_specs=[vmem] * 2,
        scratch_shapes=[
            pltpu.VMEM((64, flat), jnp.bfloat16),
            pltpu.VMEM((64, flat), jnp.bfloat16),
            pltpu.SemaphoreType.DMA((wanted.shape[0],)),
            pltpu.SemaphoreType.DMA,
        ],
        compiler_params=params,
        name="normal_equations",
    )(rows, cols, slots, is_near, near, far_variance, flat_x, variance_stamps, stamp_weights, variance_sum)
    partials = [partial]
    for shift in range(1, CPER):
        partials.append(
            lax.ppermute(
                partial,
                "det",
                [(i, i // CPER * CPER + (i + shift) % CPER) for i in range(strips)],
            )
        )
    pixels = CPER * height * columns
    tables = [jnp.asarray(t) for t in (*basis_tables(), *filter_tables())]
    difference, top, bottom, filter_t, powers = pl.pallas_call(
        functools.partial(first_kernel, pixels),
        out_shape=[
            strip,
            edge,
            edge,
            jax.ShapeDtypeStruct((32, 128), jnp.float32),
            row,
        ],
        in_specs=[vmem] * 14,
        out_specs=[vmem] * 5,
        scratch_shapes=correlation_scratch(height, columns),
        compiler_params=small,
        name="solve_and_subtract",
    )(*partials, science, before, template_image, after, *tables)
    before, after = edges(top, bottom, "det")
    decorrelated_variance = powers[1:2, :1] * (variance + template_variance * powers[:1, :1])
    decorrelated = pl.pallas_call(
        second_kernel,
        out_shape=strip,
        in_specs=[vmem] * 4,
        out_specs=vmem,
        scratch_shapes=correlation_scratch(height, columns),
        compiler_params=small,
        name="decorrelate",
    )(filter_t, before, difference, after)
    return (decorrelated, decorrelated_variance)


def solution(mesh):
    placed = (
        P(("group", "det"), None),
        P(("group", "det"), None),
        P(("group", "det"), None, None, None),
        P("group", None),
        P(("group", "det"), None),
        P(("group", "det"), None),
    )
    return jax.shard_map(
        per_device,
        mesh=mesh,
        in_specs=placed,
        out_specs=(P(("group", "det"), None), P(("group", "det"), None)),
        check_vma=False,
    )
```
